32 devices in a mesh: grp: 2 (over x), leaf: 8 (over z, y), sub: 2 (over core).
Axes of the slice: x: 2, y: 2, z: 4, core: 2. Of those that a mesh axis runs over, the one named last changes fastest.
Arguments:
- right_side: float32 [512, 2048], P(('grp', 'leaf', 'sub')), parts along dimension 0, may hold values from -24 to 24, as said below
- first_guess: float32 [512, 2048], P(('grp', 'leaf', 'sub')), parts along dimension 0, may hold values from -3 to 3
- couple: bfloat16 [512, 64, 384], P(('grp', 'leaf', 'sub')), parts along dimension 0, may hold values from -0.75 to 0.75
- send_lists: int32 [32, 2, 4], P(('grp', 'leaf', 'sub')), parts along dimension 0, may hold values from -1 to 15, as said below
- neighbours: int32 [512, 6], P(('grp', 'leaf', 'sub')), parts along dimension 0, may hold values from -1 to 23, as said below
Outputs:
- solution: float32 [512, 2048], P(('grp', 'leaf', 'sub')), parts along dimension 0
- residual: float32 [512, 2048], P(('grp', 'leaf', 'sub')), parts along dimension 0
The draws below stay inside these ranges and needn't reach their ends.
There are 2 independent parts, one for each index of `grp`. The reference program is written for one: setup_inputs(seed, part) draws one part's arguments, and reference() takes and returns one part's arrays. A program takes and returns all parts, laid end to end along the dimension named above; each array names one. Nothing has to cross between parts.
Inputs may be any that keep to these rules, and one draw needn't show every extreme that they name: `right_side`: rows rise in scale along the element order. `send_lists`: for device d of a part and direction 0 (toward device d + 1) or 1 (toward device d - 1): distinct local element indices in the live slots, which come first, and -1 after them. The first device sends nothing in direction 1, the last nothing in direction 0; some device fills all 4 slots in direction 0 and the device after it all 4 in direction 1. `neighbours`: positions below 16 are the device's own elements, 16 + s the live slot s received from the previous device, 20 + s the live slot s received from the next device; -1 marks a face on the band's boundary.
All inputs are finite; a program needn't handle non-finite values.
Results may differ from the reference program's by a relative error of at most 0.034.
Values may be sent and summed in bfloat16 or wider, within the bound.
No kernel may reach another device: no remote copies, remote signals or barrier semaphores. Data moves between devices by JAX's collectives and lax.ppermute only.
A program may use at most 64 MiB of HBM per device.

```python
import math
import jax
import jax.numpy as jnp
from jax import lax

DOF = 64
FACES = 6
RHS = 32
SSTEP = 3
CYCLES = 4
E_DEV = 16
SLOTS = 4
DEVS_PART = 16
ELEMS = 256


def send_counts(key):
    device_count = DEVS_PART
    counts = jax.random.randint(jax.random.fold_in(key, 7), (device_count, 2), SLOTS // 4, SLOTS + 1)
    chosen = jax.random.randint(jax.random.fold_in(key, 8), (), 0, device_count - 1)
    places = jnp.arange(device_count)
    counts = counts.at[:, 0].set(jnp.where(places == chosen, SLOTS, counts[:, 0]))
    counts = counts.at[:, 1].set(jnp.where(places == chosen + 1, SLOTS, counts[:, 1]))
    counts = counts.at[device_count - 1, 0].set(0)
    counts = counts.at[0, 1].set(0)
    return (counts.astype(jnp.int32), chosen.astype(jnp.int32))


def draw_send_lists(key, part):
    counts, chosen = send_counts(key)
    keys = jax.random.split(jax.random.fold_in(key, 11), DEVS_PART * 2)

    def offsets(one_key):
        mixed = jax.random.permutation(one_key, 2 * SLOTS - 1)[:SLOTS - 1] + 1
        return jnp.concatenate([jnp.zeros((1,), jnp.int32), mixed.astype(jnp.int32)])
    table = jax.vmap(offsets)(keys).reshape(DEVS_PART, 2, SLOTS)
    local = jnp.stack([E_DEV - 1 - table[:, 0], table[:, 1]], axis=1)
    slot_ids = jnp.arange(SLOTS)[None, None, :]
    return jnp.where(slot_ids < counts[:, :, None], local, -1).astype(jnp.int32)


def draw_neighbours(key, part):
    counts, chosen = send_counts(key)
    shape = (ELEMS, FACES)
    kinds = jax.random.randint(jax.random.fold_in(key, 21), shape, 0, 100)
    local = jax.random.randint(jax.random.fold_in(key, 22), shape, 0, E_DEV)
    drawn = jax.random.randint(jax.random.fold_in(key, 23), shape, 0, 1 << 20)
    device = (jnp.arange(ELEMS) // E_DEV)[:, None]
    before_count = jnp.where(device > 0, counts[jnp.maximum(device - 1, 0), 0], 0)
    after_count = jnp.where(device < DEVS_PART - 1, counts[jnp.minimum(device + 1, DEVS_PART - 1), 1], 0)
    before = jnp.where(before_count > 0, E_DEV + drawn % jnp.maximum(before_count, 1), -1)
    after = jnp.where(after_count > 0, E_DEV + SLOTS + drawn % jnp.maximum(after_count, 1), -1)
    result = jnp.where(kinds < 8, -1, jnp.where(kinds < 76, local, jnp.where(kinds < 88, before, after)))
    result = result.at[chosen * E_DEV, 0].set(E_DEV + 2 * SLOTS - 1)
    result = result.at[(chosen + 1) * E_DEV, 1].set(E_DEV + SLOTS - 1)
    return result.astype(jnp.int32)


def draw_couple(key, part):
    shape = (ELEMS, DOF, FACES * DOF)
    scale = 0.85 / math.sqrt(FACES * DOF)
    strength = jnp.exp(jax.random.uniform(jax.random.fold_in(key, 31), (ELEMS, 1, 1), jnp.float32, math.log(0.5), math.log(1.5)))
    values = jnp.clip(jax.random.normal(jax.random.fold_in(key, 32), shape, jnp.float32), -4.0, 4.0)
    return (values * scale * strength).astype(jnp.bfloat16)


def draw_right_side(key, part):
    ramp = 0.5 + jnp.arange(ELEMS, dtype=jnp.float32) / max(ELEMS - 1, 1)
    shape = (ELEMS, DOF, RHS)
    values = jnp.clip(jax.random.normal(jax.random.fold_in(key, 41), shape, jnp.float32), -4.0, 4.0)
    return (values * ramp[:, None, None]).reshape(ELEMS, DOF * RHS).astype(jnp.float32)


def steps_of(stream_key, dims, cuts, least, top_value):
    factor_of = 1.0
    for axis_at, shards_of in cuts:
        steps = jax.random.uniform(jax.random.fold_in(jax.random.fold_in(stream_key, 6), axis_at), (shards_of,), jnp.float32, least / len(cuts), top_value / len(cuts))
        factor_of = factor_of * jnp.repeat(jnp.exp(steps), dims[axis_at] // shards_of).reshape((-1,) + (1,) * (len(dims) - 1 - axis_at))
    return factor_of


def normal_values(key, shape, spread, most, pieces=(), kind=jnp.bfloat16):
    values = spread * jax.random.normal(key, shape, jnp.float32)
    if pieces:
        values = values * steps_of(key, shape, pieces, -0.22, 0.18)
    return jnp.clip(values, -most, most).astype(kind)


def setup_inputs(seed: int = 0, part: int = 0) -> dict:
    streams_of = jax.random.split(jax.random.key(seed), 6)
    part_keys = jax.random.split(jax.random.fold_in(streams_of[5], part), 6)
    return {
        "right_side": draw_right_side(jax.random.fold_in(jax.random.fold_in(streams_of[5], part), 71), part),
        "first_guess": normal_values(part_keys[1], (ELEMS, DOF * RHS), 0.5, 3.0, ((0, 16),), jnp.float32),
        "couple": draw_couple(jax.random.fold_in(jax.random.fold_in(streams_of[5], part), 71), part),
        "send_lists": draw_send_lists(jax.random.fold_in(jax.random.fold_in(streams_of[5], part), 71), part),
        "neighbours": draw_neighbours(jax.random.fold_in(jax.random.fold_in(streams_of[5], part), 71), part),
    }


def couple_apply(vector_field, couple, send_lists, neighbours):
    device_count = send_lists.shape[0]
    row_width = vector_field.shape[1]
    blocks = vector_field.astype(jnp.bfloat16).reshape(device_count, E_DEV, row_width)

    def listed_blocks(direction):
        listed = send_lists[:, direction, :]
        chosen = jnp.take_along_axis(blocks, jnp.maximum(listed, 0).astype(jnp.int32)[:, :, None], axis=1)
        return jnp.where(listed[:, :, None] >= 0, chosen, jnp.zeros_like(chosen))
    forward = listed_blocks(0)
    backward = listed_blocks(1)
    empty_row = jnp.zeros((1, SLOTS, row_width), jnp.bfloat16)
    before_blocks = jnp.concatenate([empty_row, forward[:-1]], axis=0)
    after_blocks = jnp.concatenate([backward[1:], empty_row], axis=0)
    zero_block = jnp.zeros((device_count, 1, row_width), jnp.bfloat16)
    extended = jnp.concatenate([blocks, before_blocks, after_blocks, zero_block], axis=1)
    positions = neighbours.reshape(device_count, E_DEV * FACES)
    positions = jnp.where(positions < 0, E_DEV + 2 * SLOTS, positions).astype(jnp.int32)
    coupling = couple.reshape(device_count, E_DEV, DOF, FACES * DOF)

    def one_device(operands):
        own_extended, own_positions, own_coupling = operands
        gathered = jnp.take(own_extended, own_positions, axis=0).reshape(E_DEV, FACES * DOF, RHS)
        product = jnp.einsum('eik,ekr->eir', own_coupling.astype(jnp.float32), gathered.astype(jnp.float32))
        return product.reshape(E_DEV, DOF * RHS)
    result = lax.map(one_device, (extended, positions, coupling))
    return result.reshape(device_count * E_DEV, DOF * RHS)

def to_columns(vector_field):
    return vector_field.reshape(-1, RHS)

def reference(right_side, first_guess, couple, send_lists, neighbours):
    solution = first_guess
    residual = right_side - first_guess + couple_apply(first_guess, couple, send_lists, neighbours)
    for repeat in range(CYCLES):
        krylov_blocks = [residual]
        for degree in range(SSTEP):
            krylov_blocks.append(couple_apply(krylov_blocks[-1], couple, send_lists, neighbours))
        images = [krylov_blocks[order_index] - krylov_blocks[order_index + 1] for order_index in range(SSTEP)]
        stacked = jnp.concatenate([to_columns(image_block) for image_block in images] + [to_columns(residual)], axis=1)
        gram_matrix = jnp.dot(stacked.T.astype(jnp.float32), stacked.astype(jnp.float32), precision=lax.Precision.HIGHEST, preferred_element_type=jnp.float32)
        square_block = gram_matrix[:SSTEP * RHS, :SSTEP * RHS]
        right_block = gram_matrix[:SSTEP * RHS, SSTEP * RHS:]
        factor = jnp.linalg.cholesky(square_block)
        coeffs = jax.scipy.linalg.cho_solve((factor, True), right_block)
        krylov = jnp.concatenate([to_columns(basis_block) for basis_block in krylov_blocks[:SSTEP]], axis=1)
        solution = solution + jnp.dot(krylov.astype(jnp.float32), coeffs.astype(jnp.float32), precision=lax.Precision.HIGHEST, preferred_element_type=jnp.float32).reshape(solution.shape)
        residual = residual - jnp.dot(stacked[:, :SSTEP * RHS].astype(jnp.float32), coeffs.astype(jnp.float32), precision=lax.Precision.HIGHEST, preferred_element_type=jnp.float32).reshape(residual.shape)
    return (solution, residual)
```

```python
import functools

import jax
import jax.numpy as jnp
from jax import lax
from jax.experimental import pallas as pl
from jax.experimental.pallas import tpu as pltpu
from jax.sharding import PartitionSpec as P

DOF = 64
FACES = 6
RHS = 32
SSTEP = 3
CYCLES = 4
AXES = ("leaf", "sub")
F32 = jnp.float32
BF16 = jnp.bfloat16

VMEM = pl.BlockSpec(memory_space=pltpu.VMEM)
SMEM = pl.BlockSpec(memory_space=pltpu.SMEM)
PARAMS = pltpu.CompilerParams(vmem_limit_bytes=16 * 1024 * 1024)


def fill_extended(ext, own, from_chip, from_link):
    count, slots = own.shape[0], from_chip.shape[0]
    ext[:count] = own[...]
    ext[count : count + slots] = from_chip[...]
    ext[count + slots : count + 2 * slots] = from_link[...]
    ext[count + 2 * slots] = jnp.zeros(ext.shape[1:], BF16)


def coupled(e, positions, couple, ext):
    gathered = jnp.concatenate([ext[positions[e, f]] for f in range(FACES)], axis=0)
    return jnp.dot(couple[e], gathered, preferred_element_type=F32)


def pick_sends(lists, ext, to_chip, to_link):
    for s in range(to_chip.shape[0]):
        to_chip[s] = ext[lists[0, s]]
        to_link[s] = ext[lists[1, s]]


def split(value):
    high = value.astype(BF16)
    return high, (value - high.astype(F32)).astype(BF16)


def start_kernel(lists, x, own, to_chip, to_link, ext):
    own[...] = x[...].astype(BF16)
    ext[: x.shape[0]] = own[...]
    ext[x.shape[0]] = jnp.zeros(ext.shape[1:], BF16)
    pick_sends(lists, ext, to_chip, to_link)


def residual_kernel(lists, positions, couple, own, from_chip, from_link, b, x, r, new_own, to_chip, to_link, ext):
    count = own.shape[0]
    fill_extended(ext, own, from_chip, from_link)
    for e in range(count):
        value = b[e] - x[e] + coupled(e, positions, couple, ext)
        r[e] = value
        new_own[e] = value.astype(BF16)
    ext[:count] = new_own[...]
    ext[count] = jnp.zeros(ext.shape[1:], BF16)
    pick_sends(lists, ext, to_chip, to_link)


def power_kernel(lists, positions, couple, own, from_chip, from_link, power, new_own, to_chip, to_link, ext):
    count = own.shape[0]
    fill_extended(ext, own, from_chip, from_link)
    for e in range(count):
        value = coupled(e, positions, couple, ext)
        power[e] = value
        new_own[e] = value.astype(BF16)
    ext[:count] = new_own[...]
    ext[count] = jnp.zeros(ext.shape[1:], BF16)
    pick_sends(lists, ext, to_chip, to_link)


def gram_kernel(positions, couple, own, from_chip, from_link, b0, b1, b2, last, gram, ext):
    count = own.shape[0]
    rows = count * DOF
    fill_extended(ext, own, from_chip, from_link)
    for e in range(count):
        last[e] = coupled(e, positions, couple, ext)
    fields = [field[...].reshape(rows, RHS) for field in (b0, b1, b2, last)]
    stacked = jnp.concatenate([fields[k] - fields[k + 1] for k in range(SSTEP)] + [fields[0]], axis=1)
    high, low = split(stacked)
    sums = lax.dot_general(
        high, jnp.concatenate([high, low], axis=1), (((0,), (0,)), ((), ())), preferred_element_type=F32
    )
    width = stacked.shape[1]
    cross = sums[:, width:]
    gram[...] = sums[:, :width] + cross + cross.T


def eliminate(gram):
    size = SSTEP * RHS
    groups = [gram[8 * g : 8 * g + 8, :] for g in range(size // 8)]
    row_ids = lax.broadcasted_iota(jnp.int32, groups[0].shape, 0)
    for j in range(size):
        home, place = divmod(j, 8)
        row = groups[home][place : place + 1, :]
        scaled = row / row[:, j : j + 1]
        for g in range(size // 8):
            updated = groups[g] - groups[g][:, j : j + 1] * scaled
            groups[g] = jnp.where(row_ids == place, scaled, updated) if g == home else updated
    return jnp.concatenate(groups, axis=0)


def update_values(gram, b0, b1, b2, b3, x):
    count = x.shape[0]
    rows = count * DOF
    reduced = eliminate(gram)
    width = reduced.shape[1]
    zeros = jnp.zeros((RHS, width), F32)
    lanes = lax.broadcasted_iota(jnp.int32, (width, width), 1)
    rows_at = lax.broadcasted_iota(jnp.int32, (width, width), 0)
    sol = jnp.concatenate([reduced, zeros], axis=0)
    res = jnp.concatenate([zeros, reduced], axis=0) - sol
    res = res + jnp.where(lanes - (width - RHS) == rows_at, 1.0, 0.0).astype(F32)
    res = pltpu.roll(res, width - RHS, 1)
    mix = jnp.where(lanes >= width - RHS, sol, jnp.where(lanes >= width - 2 * RHS, res, 0.0))
    fields = jnp.concatenate([field[...].reshape(rows, RHS) for field in (b0, b1, b2, b3)], axis=1)
    high, low = split(fields)
    mix_high, mix_low = split(mix)
    out = jnp.dot(
        jnp.concatenate([high, low], axis=1),
        jnp.concatenate([mix_high, mix_high], axis=0),
        preferred_element_type=F32,
    ) + jnp.dot(high, mix_low, preferred_element_type=F32)
    new_x = x[...] + out[:, width - RHS :].reshape(x.shape)
    new_r = out[:, width - 2 * RHS : width - RHS].reshape(x.shape)
    return new_x, new_r


def update_kernel(lists, gram, b0, b1, b2, b3, x, new_x, new_r, new_own, to_chip, to_link, ext):
    count = x.shape[0]
    new_x[...], value = update_values(gram, b0, b1, b2, b3, x)
    new_r[...] = value
    new_own[...] = value.astype(BF16)
    ext[:count] = new_own[...]
    ext[count] = jnp.zeros(ext.shape[1:], BF16)
    pick_sends(lists, ext, to_chip, to_link)


def finish_kernel(gram, b0, b1, b2, b3, x, new_x, new_r):
    new_x[...], new_r[...] = update_values(gram, b0, b1, b2, b3, x)


def shards(right_side, first_guess, couple, send_lists, neighbours):
    count = right_side.shape[0]
    slots = send_lists.shape[2]
    devices = lax.axis_size(AXES)
    assert lax.axis_size("sub") == 2
    second = lax.axis_index("sub") == 1

    field32 = jax.ShapeDtypeStruct((count, DOF, RHS), F32)
    field16 = jax.ShapeDtypeStruct((count, DOF, RHS), BF16)
    sent = jax.ShapeDtypeStruct((slots, DOF, RHS), BF16)
    ext = pltpu.VMEM((count + 2 * slots + 1, DOF, RHS), BF16)

    def call(kernel, outs, specs, name, scratch=(ext,)):
        return pl.pallas_call(
            kernel,
            out_shape=outs,
            in_specs=specs,
            out_specs=[VMEM] * len(outs),
            scratch_shapes=list(scratch),
            compiler_params=PARAMS,
            name=name,
        )

    own_lists = jnp.where(send_lists[0] < 0, count, send_lists[0]).astype(jnp.int32)
    lists = jnp.where(second, own_lists[::-1], own_lists)
    swapped = jnp.where(neighbours < count + slots, neighbours + slots, neighbours - slots)
    placed = jnp.where(second | (neighbours < count), neighbours, swapped)
    positions = jnp.where(neighbours < 0, count + 2 * slots, placed).astype(jnp.int32)

    chip_pairs = [(d, d ^ 1) for d in range(devices)]
    link_pairs = [(d, d + 1 if d % 2 else d - 1) for d in range(devices)]
    link_pairs = [(s, t) for s, t in link_pairs if 0 <= t < devices]

    def exchange(to_chip, to_link):
        from_link = lax.ppermute(to_link, AXES, link_pairs)
        from_chip = lax.ppermute(to_chip, AXES, chip_pairs)
        return from_chip, from_link

    def total(value):
        step = 1
        while step < devices:
            value = value + lax.ppermute(value, AXES, [(d, d ^ step) for d in range(devices)])
            step *= 2
        return value

    start = call(start_kernel, [field16, sent, sent], [SMEM, VMEM], "start")
    first = call(
        residual_kernel, [field32, field16, sent, sent], [SMEM, SMEM] + [VMEM] * 6, "first_residual"
    )
    power = call(power_kernel, [field32, field16, sent, sent], [SMEM, SMEM] + [VMEM] * 4, "power")
    gram = call(
        gram_kernel,
        [field32, jax.ShapeDtypeStruct(((SSTEP + 1) * RHS, (SSTEP + 1) * RHS), F32)],
        [SMEM] + [VMEM] * 7,
        "last_power_and_gram",
    )
    update = call(update_kernel, [field32, field32, field16, sent, sent], [SMEM] + [VMEM] * 6, "solve_update")
    finish = call(finish_kernel, [field32, field32], [VMEM] * 6, "solve_finish", ())

    b = right_side.reshape(count, DOF, RHS)
    x = first_guess.reshape(count, DOF, RHS)
    own, to_chip, to_link = start(lists, x)
    r, own, to_chip, to_link = first(lists, positions, couple, own, *exchange(to_chip, to_link), b, x)
    for cycle in range(CYCLES):
        b1, own, to_chip, to_link = power(lists, positions, couple, own, *exchange(to_chip, to_link))
        b2, own, to_chip, to_link = power(lists, positions, couple, own, *exchange(to_chip, to_link))
        b3, partial = gram(positions, couple, own, *exchange(to_chip, to_link), r, b1, b2)
        sums = total(partial)
        if cycle + 1 < CYCLES:
            x, r, own, to_chip, to_link = update(lists, sums, r, b1, b2, b3, x)
        else:
            x, r = finish(sums, r, b1, b2, b3, x)
    return x.reshape(right_side.shape), r.reshape(right_side.shape)


def solution(mesh):
    rows = ("grp", "leaf", "sub")
    placed = (P(rows, None), P(rows, None), P(rows, None, None), P(rows, None, None), P(rows, None))
    return jax.shard_map(
        shards,
        mesh=mesh,
        in_specs=placed,
        out_specs=(P(rows, None), P(rows, None)),
        check_vma=False,
    )
```

```python
import functools

import jax
import jax.numpy as jnp
from jax import lax
from jax.experimental import pallas as pl
from jax.experimental.pallas import tpu as pltpu
from jax.sharding import PartitionSpec as P

DOF = 64
FACES = 6
RHS = 32
SSTEP = 3
CYCLES = 4
AXES = ("leaf", "sub")
F32 = jnp.float32
BF16 = jnp.bfloat16

VMEM = pl.BlockSpec(memory_space=pltpu.VMEM)
SMEM = pl.BlockSpec(memory_space=pltpu.SMEM)
PARAMS = pltpu.CompilerParams(vmem_limit_bytes=16 * 1024 * 1024)


def fill_extended(ext, own, from_chip, from_link):
    count, slots = own.shape[0], from_chip.shape[0]
    ext[:count] = own[...]
    ext[count : count + slots] = from_chip[...]
    ext[count + slots : count + 2 * slots] = from_link[...]
    ext[count + 2 * slots] = jnp.zeros(ext.shape[1:], BF16)


def coupled(e, positions, couple, ext):
    gathered = jnp.concatenate([ext[positions[e, f]] for f in range(FACES)], axis=0)
    return jnp.dot(couple[e], gathered, preferred_element_type=F32)


def pick_sends(lists, ext, to_chip, to_link):
    for s in range(to_chip.shape[0]):
        to_chip[s] = ext[lists[0, s]]
        to_link[s] = ext[lists[1, s]]


def split(value):
    high = value.astype(BF16)
    return high, (value - high.astype(F32)).astype(BF16)


def start_kernel(lists, x, own, to_chip, to_link, ext):
    own[...] = x[...].astype(BF16)
    ext[: x.shape[0]] = own[...]
    ext[x.shape[0]] = jnp.zeros(ext.shape[1:], BF16)
    pick_sends(lists, ext, to_chip, to_link)


def residual_kernel(lists, positions, couple, own, from_chip, from_link, b, x, r, new_own, to_chip, to_link, ext):
    count = own.shape[0]
    fill_extended(ext, own, from_chip, from_link)
    for e in range(count):
        value = b[e] - x[e] + coupled(e, positions, couple, ext)
        r[e] = value
        new_own[e] = value.astype(BF16)
    ext[:count] = new_own[...]
    ext[count] = jnp.zeros(ext.shape[1:], BF16)
    pick_sends(lists, ext, to_chip, to_link)


def power_kernel(lists, positions, couple, own, from_chip, from_link, power, new_own, to_chip, to_link, ext):
    count = own.shape[0]
    fill_extended(ext, own, from_chip, from_link)
    for e in range(count):
        value = coupled(e, positions, couple, ext)
        power[e] = value
        new_own[e] = value.astype(BF16)
    ext[:count] = new_own[...]
    ext[count] = jnp.zeros(ext.shape[1:], BF16)
    pick_sends(lists, ext, to_chip, to_link)


def gram_kernel(positions, couple, own, from_chip, from_link, b0, b1, b2, last, gram, ext):
    count = own.shape[0]
    rows = count * DOF
    fill_extended(ext, own, from_chip, from_link)
    for e in range(count):
        last[e] = coupled(e, positions, couple, ext)
    fields = [field[...].reshape(rows, RHS) for field in (b0, b1, b2, last)]
    stacked = jnp.concatenate([fields[k] - fields[k + 1] for k in range(SSTEP)] + [fields[0]], axis=1)
    high, low = split(stacked)
    sums = lax.dot_general(
        high, jnp.concatenate([high, low], axis=1), (((0,), (0,)), ((), ())), preferred_element_type=F32
    )
    width = stacked.shape[1]
    cross = sums[:, width:]
    gram[...] = sums[:, :width] + cross + cross.T


def eliminate(gram):
    count = SSTEP * RHS // 8
    groups = [gram[8 * g : 8 * g + 8, :] for g in range(count)]
    shape = groups[0].shape
    row_ids = lax.broadcasted_iota(jnp.int32, shape, 0)
    for home in range(count):
        columns = [
            [jnp.broadcast_to(group[:, 8 * home + m : 8 * home + m + 1], shape) for m in range(8)]
            for group in groups
        ]
        own = list(columns[home])
        panel = groups[home]
        for m in range(8):
            inverse = 1.0 / own[m][m : m + 1, :]
            scaled = panel[m : m + 1, :] * inverse
            panel = jnp.where(row_ids == m, scaled, panel - own[m] * scaled)
            for k in range(m + 1, 8):
                scaled = own[k][m : m + 1, :] * inverse
                own[k] = jnp.where(row_ids == m, scaled, own[k] - own[m] * scaled)
        for g in range(count):
            if g == home:
                groups[g] = panel
                continue
            for m in range(8):
                groups[g] = groups[g] - columns[g][m] * panel[m : m + 1, :]
    return jnp.concatenate(groups, axis=0)


def update_values(gram, b0, b1, b2, b3, x):
    count = x.shape[0]
    rows = count * DOF
    reduced = eliminate(gram)
    width = reduced.shape[1]
    zeros = jnp.zeros((RHS, width), F32)
    lanes = lax.broadcasted_iota(jnp.int32, (width, width), 1)
    rows_at = lax.broadcasted_iota(jnp.int32, (width, width), 0)
    sol = jnp.concatenate([reduced, zeros], axis=0)
    res = jnp.concatenate([zeros, reduced], axis=0) - sol
    res = res + jnp.where(lanes - (width - RHS) == rows_at, 1.0, 0.0).astype(F32)
    res = pltpu.roll(res, width - RHS, 1)
    mix = jnp.where(lanes >= width - RHS, sol, jnp.where(lanes >= width - 2 * RHS, res, 0.0))
    fields = jnp.concatenate([field[...].reshape(rows, RHS) for field in (b0, b1, b2, b3)], axis=1)
    high, low = split(fields)
    mix_high, mix_low = split(mix)
    out = jnp.dot(
        jnp.concatenate([high, low], axis=1),
        jnp.concatenate([mix_high, mix_high], axis=0),
        preferred_element_type=F32,
    ) + jnp.dot(high, mix_low, preferred_element_type=F32)
    new_x = x[...] + out[:, width - RHS :].reshape(x.shape)
    new_r = out[:, width - 2 * RHS : width - RHS].reshape(x.shape)
    return new_x, new_r


def update_kernel(lists, gram, b0, b1, b2, b3, x, new_x, new_r, new_own, to_chip, to_link, ext):
    count = x.shape[0]
    new_x[...], value = update_values(gram, b0, b1, b2, b3, x)
    new_r[...] = value
    new_own[...] = value.astype(BF16)
    ext[:count] = new_own[...]
    ext[count] = jnp.zeros(ext.shape[1:], BF16)
    pick_sends(lists, ext, to_chip, to_link)


def finish_kernel(gram, b0, b1, b2, b3, x, new_x, new_r):
    new_x[...], new_r[...] = update_values(gram, b0, b1, b2, b3, x)


def shards(right_side, first_guess, couple, send_lists, neighbours):
    count = right_side.shape[0]
    slots = send_lists.shape[2]
    devices = lax.axis_size(AXES)
    assert lax.axis_size("sub") == 2
    second = lax.axis_index("sub") == 1

    field32 = jax.ShapeDtypeStruct((count, DOF, RHS), F32)
    field16 = jax.ShapeDtypeStruct((count, DOF, RHS), BF16)
    sent = jax.ShapeDtypeStruct((slots, DOF, RHS), BF16)
    ext = pltpu.VMEM((count + 2 * slots + 1, DOF, RHS), BF16)

    def call(kernel, outs, specs, name, scratch=(ext,)):
        return pl.pallas_call(
            kernel,
            out_shape=outs,
            in_specs=specs,
            out_specs=[VMEM] * len(outs),
            scratch_shapes=list(scratch),
            compiler_params=PARAMS,
            name=name,
        )

    own_lists = jnp.where(send_lists[0] < 0, count, send_lists[0]).astype(jnp.int32)
    lists = jnp.where(second, own_lists[::-1], own_lists)
    swapped = jnp.where(neighbours < count + slots, neighbours + slots, neighbours - slots)
    placed = jnp.where(second | (neighbours < count), neighbours, swapped)
    positions = jnp.where(neighbours < 0, count + 2 * slots, placed).astype(jnp.int32)

    chip_pairs = [(d, d ^ 1) for d in range(devices)]
    link_pairs = [(d, d + 1 if d % 2 else d - 1) for d in range(devices)]
    link_pairs = [(s, t) for s, t in link_pairs if 0 <= t < devices]

    def exchange(to_chip, to_link):
        from_link = lax.ppermute(to_link, AXES, link_pairs)
        from_chip = lax.ppermute(to_chip, AXES, chip_pairs)
        return from_chip, from_link

    def total(value):
        step = 1
        while step < devices:
            value = value + lax.ppermute(value, AXES, [(d, d ^ step) for d in range(devices)])
            step *= 2
        return value

    start = call(start_kernel, [field16, sent, sent], [SMEM, VMEM], "start")
    first = call(
        residual_kernel, [field32, field16, sent, sent], [SMEM, SMEM] + [VMEM] * 6, "first_residual"
    )
    power = call(power_kernel, [field32, field16, sent, sent], [SMEM, SMEM] + [VMEM] * 4, "power")
    gram = call(
        gram_kernel,
        [field32, jax.ShapeDtypeStruct(((SSTEP + 1) * RHS, (SSTEP + 1) * RHS), F32)],
        [SMEM] + [VMEM] * 7,
        "last_power_and_gram",
    )
    update = call(update_kernel, [field32, field32, field16, sent, sent], [SMEM] + [VMEM] * 6, "solve_update")
    finish = call(finish_kernel, [field32, field32], [VMEM] * 6, "solve_finish", ())

    b = right_side.reshape(count, DOF, RHS)
    x = first_guess.reshape(count, DOF, RHS)
    own, to_chip, to_link = start(lists, x)
    r, own, to_chip, to_link = first(lists, positions, couple, own, *exchange(to_chip, to_link), b, x)
    for cycle in range(CYCLES):
        b1, own, to_chip, to_link = power(lists, positions, couple, own, *exchange(to_chip, to_link))
        b2, own, to_chip, to_link = power(lists, positions, couple, own, *exchange(to_chip, to_link))
        b3, partial = gram(positions, couple, own, *exchange(to_chip, to_link), r, b1, b2)
        sums = total(partial)
        if cycle + 1 < CYCLES:
            x, r, own, to_chip, to_link = update(lists, sums, r, b1, b2, b3, x)
        else:
            x, r = finish(sums, r, b1, b2, b3, x)
    return x.reshape(right_side.shape), r.reshape(right_side.shape)


def solution(mesh):
    rows = ("grp", "leaf", "sub")
    placed = (P(rows, None), P(rows, None), P(rows, None, None), P(rows, None, None), P(rows, None))
    return jax.shard_map(
        shards,
        mesh=mesh,
        in_specs=placed,
        out_specs=(P(rows, None), P(rows, None)),
        check_vma=False,
    )
```

```python
import jax
import jax.numpy as jnp
from jax import lax
from jax.experimental import pallas as pl
from jax.experimental.pallas import tpu as pltpu
from jax.sharding import PartitionSpec as P

DOF = 64
FACES = 6
RHS = 32
SSTEP = 3
CYCLES = 4
MERGED = 2
POWERS = SSTEP * MERGED
GROWTH = 8.0
PACK = 4
META = 16
AXES = ("leaf", "sub")
F32 = jnp.float32
BF16 = jnp.bfloat16

VMEM = pl.BlockSpec(memory_space=pltpu.VMEM)
SMEM = pl.BlockSpec(memory_space=pltpu.SMEM)
PARAMS = pltpu.CompilerParams(vmem_limit_bytes=16 * 1024 * 1024)


def pack(message, blocks):
    for g in range(len(blocks) // PACK):
        message[g] = jnp.concatenate(blocks[PACK * g : PACK * g + PACK], axis=1).astype(BF16)


def unpack(ext, start, message):
    for g in range(message.shape[0]):
        row = message[g]
        for j in range(PACK):
            ext[start + PACK * g + j] = row[:, RHS * j : RHS * j + RHS]


def coupled(table, e, rows, ext):
    gathered = jnp.concatenate([ext[table[e, f]] for f in range(FACES)], axis=0)
    return jnp.dot(rows, gathered, preferred_element_type=F32)


def split(value):
    high = value.astype(BF16)
    return high, (value - high.astype(F32)).astype(BF16)


def listed(lists, side, ext):
    return [ext[lists[side, s]].astype(F32) for s in range(lists.shape[1])]


def start_kernel(lists, x, to_chip, to_link, ext):
    count = x.shape[0]
    ext[:count] = x[...].astype(BF16)
    ext[count] = jnp.zeros(ext.shape[1:], BF16)
    pack(to_chip, listed(lists, 0, ext))
    pack(to_link, listed(lists, 1, ext))


def rows_kernel(lists, positions, couple, to_chip, to_link):
    count = couple.shape[0]
    lanes = lax.broadcasted_iota(jnp.int32, (META, couple.shape[2]), 1)
    for side, message in ((0, to_chip), (1, to_link)):
        for s in range(message.shape[0]):
            place = lists[side, s]
            live = place < count
            e = jnp.minimum(place, count - 1)
            message[s, :DOF] = couple[e]
            nowhere = count + 2 * message.shape[0]
            values = [jnp.where(live, positions[e, f], nowhere) for f in range(FACES)] + [place]
            meta = jnp.zeros(lanes.shape, jnp.int32)
            for f, value in enumerate(values):
                meta = jnp.where(lanes == f, value, meta)
            message[s, DOF:] = meta.astype(F32).astype(BF16)


def residual_kernel(lists, positions, couple, from_chip, from_link, b, x, r, own, to_chip, ext):
    count = x.shape[0]
    ext[:count] = x[...].astype(BF16)
    unpack(ext, count, from_chip)
    unpack(ext, count + PACK * from_chip.shape[0], from_link)
    ext[ext.shape[0] - 1] = jnp.zeros(ext.shape[1:], BF16)
    for e in range(count):
        r[e] = b[e] - x[e] + coupled(positions, e, couple[e], ext)
    pack(own, [r[e] for e in range(count)])
    ext[:count] = r[...].astype(BF16)
    ext[count] = jnp.zeros(ext.shape[1:], BF16)
    pack(to_chip, listed(lists, 0, ext))


def extend(ext, mine, theirs):
    unpack(ext, 0, mine)
    unpack(ext, PACK * mine.shape[0], theirs)
    ext[ext.shape[0] - 1] = jnp.zeros(ext.shape[1:], BF16)


def power_kernel(table, couple, extra, mine, theirs, power, message, ext):
    count, slots = couple.shape[0], extra.shape[0]
    extend(ext, mine, theirs)
    values = []
    for e in range(count + slots):
        rows = couple[e] if e < count else extra[e - count, :DOF]
        values.append(coupled(table, e, rows, ext) * (1.0 / GROWTH))
        if e < count:
            power[e] = values[e]
    pack(message, values)


def gram_kernel(table, couple, mine, theirs, *refs):
    fields, (last, packed, ext) = refs[:POWERS], refs[POWERS:]
    count = couple.shape[0]
    rows = count * DOF
    extend(ext, mine, theirs)
    for e in range(count):
        last[e] = coupled(table, e, couple[e], ext) * (1.0 / GROWTH)
    fields = [field[...].reshape(rows, RHS) for field in (*fields, last)]
    images = [fields[k] - GROWTH * fields[k + 1] for k in range(POWERS)]
    stacked = jnp.concatenate(images + [fields[0], jnp.zeros((rows, RHS), F32)], axis=1)
    high, low = split(stacked)
    width = stacked.shape[1]
    sums = lax.dot_general(
        high, jnp.concatenate([high, low], axis=1), (((0,), (0,)), ((), ())), preferred_element_type=F32
    )
    cross = sums[:, width:]
    gram = sums[:, :width] + cross + cross.T
    half = width // 2
    below = jnp.concatenate([jnp.zeros((RHS, half), F32), gram[half : width - RHS, half:]], axis=0)
    packed[:, :half] = jnp.where(block_of(half, 0) > block_of(half, 1), below, gram[:half, :half])
    packed[:, half:] = gram[:half, half:]


def block_of(size, dimension):
    return lax.broadcasted_iota(jnp.int32, (size, size), dimension) // RHS


def unpack_gram(packed):
    half = packed.shape[0]
    low_left, right = packed[:, :half], packed[:, half:]
    row, column = block_of(half, 0), block_of(half, 1)
    first = jnp.where(row <= column, low_left, low_left.T)
    moved = jnp.concatenate([low_left[RHS:], jnp.zeros((RHS, half), F32)], axis=0)
    last = jnp.where(row >= column, moved, moved.T)
    last = jnp.where((row < 3) & (column < 3), last, 0.0)
    return jnp.concatenate(
        [jnp.concatenate([first, right], axis=1), jnp.concatenate([right.T, last], axis=1)], axis=0
    )


def eliminate(gram):
    count = SSTEP * RHS // 8
    groups = [gram[8 * g : 8 * g + 8, :] for g in range(count)]
    shape = groups[0].shape
    row_ids = lax.broadcasted_iota(jnp.int32, shape, 0)
    for home in range(count):
        columns = [
            [jnp.broadcast_to(group[:, 8 * home + m : 8 * home + m + 1], shape) for m in range(8)]
            for group in groups
        ]
        own = list(columns[home])
        panel = groups[home]
        for m in range(8):
            inverse = 1.0 / own[m][m : m + 1, :]
            scaled = panel[m : m + 1, :] * inverse
            panel = jnp.where(row_ids == m, scaled, panel - own[m] * scaled)
            for k in range(m + 1, 8):
                scaled = own[k][m : m + 1, :] * inverse
                own[k] = jnp.where(row_ids == m, scaled, own[k] - own[m] * scaled)
        for g in range(count):
            if g == home:
                groups[g] = panel
                continue
            for m in range(8):
                groups[g] = groups[g] - columns[g][m] * panel[m : m + 1, :]
    return jnp.concatenate(groups, axis=0)[:, SSTEP * RHS :]


def exact(a, b, contract=(1, 0)):
    return lax.dot_general(
        a,
        b,
        (((contract[0],), (contract[1],)), ((), ())),
        precision=lax.Precision.HIGHEST,
        preferred_element_type=F32,
    )


def below(value, size, blocks):
    parts = [jnp.zeros((RHS * blocks, value.shape[1]), F32)] if blocks else []
    rest = size - RHS * blocks - value.shape[0]
    parts.append(value)
    if rest:
        parts.append(jnp.zeros((rest, value.shape[1]), F32))
    return jnp.concatenate(parts, axis=0)


def mixing(packed):
    gram = unpack_gram(packed)
    size = gram.shape[0]
    right = RHS * POWERS
    square = SSTEP * RHS
    eye = (
        lax.broadcasted_iota(jnp.int32, (RHS, RHS), 0) == lax.broadcasted_iota(jnp.int32, (RHS, RHS), 1)
    ).astype(F32)

    first = eliminate(jnp.concatenate([gram[:square, :square], gram[:square, right : right + RHS]], axis=1))
    left = GROWTH * below(first, square + RHS, 1) - below(first, square + RHS, 0) + below(eye, square + RHS, 0)
    moved = jnp.concatenate([below(left, size, k) for k in range(SSTEP)], axis=1)
    images = jnp.concatenate([moved, below(eye, size, POWERS) - below(first, size, 0)], axis=1)
    second = eliminate(exact(images, exact(gram, images), (0, 0)))
    change = exact(moved, second)
    sol = below(first, size, 0) + change
    res = below(left, size, 0) - change + GROWTH * below(change[: size - RHS], size, 1)
    return jnp.concatenate([sol, res], axis=1)


def mixed(packed, fields):
    rows = fields[0].shape[0] * DOF
    mix_high, mix_low = split(mixing(packed))
    stacked = jnp.concatenate(
        [field[...].reshape(rows, RHS) for field in fields] + [jnp.zeros((rows, RHS), F32)], axis=1
    )
    high, low = split(stacked)
    out = jnp.dot(high, mix_high, preferred_element_type=F32)
    out += jnp.dot(high, mix_low, preferred_element_type=F32)
    out += jnp.dot(low, mix_high, preferred_element_type=F32)
    shape = fields[0].shape
    return out[:, :RHS].reshape(shape), out[:, RHS:].reshape(shape)


def update_kernel(lists, packed, *refs):
    fields, (x, new_x, r, own, to_chip, ext) = refs[: POWERS + 1], refs[POWERS + 1 :]
    count = x.shape[0]
    step, r[...] = mixed(packed, fields)
    new_x[...] = x[...] + step
    pack(own, [r[e] for e in range(count)])
    ext[:count] = r[...].astype(BF16)
    ext[count] = jnp.zeros(ext.shape[1:], BF16)
    pack(to_chip, listed(lists, 0, ext))


def finish_kernel(packed, *refs):
    fields, (x, new_x, r) = refs[: POWERS + 1], refs[POWERS + 1 :]
    step, r[...] = mixed(packed, fields)
    new_x[...] = x[...] + step


def shards(right_side, first_guess, couple, send_lists, neighbours):
    count = right_side.shape[0]
    slots = send_lists.shape[2]
    devices = lax.axis_size(AXES)
    assert lax.axis_size("sub") == 2 and slots % PACK == 0 and count % PACK == 0
    second = lax.axis_index("sub") == 1

    def shape(dtype, *sizes):
        return jax.ShapeDtypeStruct(sizes, dtype)

    field = shape(F32, count, DOF, RHS)
    slot_message = shape(BF16, slots // PACK, DOF, PACK * RHS)
    own_message = shape(BF16, count // PACK, DOF, PACK * RHS)
    message = shape(BF16, (count + slots) // PACK, DOF, PACK * RHS)
    row_message = shape(BF16, slots, DOF + META, FACES * DOF)
    gram_shape = shape(F32, (POWERS + 2) * RHS // 2, (POWERS + 2) * RHS)

    def call(kernel, outs, specs, name, blocks=0):
        return pl.pallas_call(
            kernel,
            out_shape=outs,
            in_specs=specs,
            out_specs=[VMEM] * len(outs),
            scratch_shapes=[pltpu.VMEM((blocks, DOF, RHS), BF16)] if blocks else [],
            compiler_params=PARAMS,
            name=name,
        )

    chip_base, link_base, nowhere = count, count + slots, count + 2 * slots
    own_lists = jnp.where(send_lists[0] < 0, count, send_lists[0]).astype(jnp.int32)
    lists = jnp.where(second, own_lists[::-1], own_lists)
    swapped = jnp.where(neighbours < link_base, neighbours + slots, neighbours - slots)
    codes = jnp.where(second | (neighbours < count), neighbours, swapped)
    codes = jnp.where(neighbours < 0, nowhere, codes).astype(jnp.int32)

    chip_pairs = [(d, d ^ 1) for d in range(devices)]
    link_pairs = [(d, d + 1 if d % 2 else d - 1) for d in range(devices)]
    link_pairs = [(s, t) for s, t in link_pairs if 0 <= t < devices]

    def chip(value):
        return lax.ppermute(value, AXES, chip_pairs)

    def link(value):
        return lax.ppermute(value, AXES, link_pairs)

    def total(value):
        step = 1
        while step < devices:
            value = value + lax.ppermute(value, AXES, [(d, d ^ step) for d in range(devices)])
            step *= 2
        return value

    reach = count + slots
    empty = 2 * reach

    def looked_up(places, at, base):
        found = jnp.full(at.shape, empty, jnp.int32)
        for s in range(slots):
            found = jnp.where(at == base + s, places[s], found)
        return found

    def table(known_base, far_base, own_places, rows):
        their_codes = rows[:, DOF, :FACES].astype(jnp.int32)
        their_places = rows[:, DOF, FACES].astype(jnp.int32)

        def place(at, own, known, far):
            is_known = (at >= known_base) & (at < known_base + slots)
            return jnp.where(at < count, at + own, jnp.where(is_known, at - known_base + known, far))

        far = jnp.where(their_places < count, their_places + reach, empty)
        near = jnp.where(own_places < count, own_places, empty)
        mine = place(codes, 0, count, looked_up(far, codes, far_base))
        theirs = place(their_codes, reach, reach + count, looked_up(near, their_codes, far_base))
        return jnp.concatenate([mine, theirs], axis=0)

    start = call(start_kernel, [slot_message] * 2, [SMEM, VMEM], "start", count + 1)
    send_rows = call(rows_kernel, [row_message] * 2, [SMEM, SMEM, VMEM], "rows")
    first = call(
        residual_kernel,
        [field, own_message, slot_message],
        [SMEM, SMEM] + [VMEM] * 5,
        "first_residual",
        nowhere + 1,
    )
    power = call(power_kernel, [field, message], [SMEM] + [VMEM] * 4, "power", empty + 1)
    gram = call(gram_kernel, [field, gram_shape], [SMEM] + [VMEM] * (3 + POWERS), "power_and_gram", empty + 1)
    update = call(
        update_kernel,
        [field, field, own_message, slot_message],
        [SMEM] + [VMEM] * (POWERS + 3),
        "solve_update",
        count + 1,
    )
    finish = call(finish_kernel, [field, field], [VMEM] * (POWERS + 3), "solve_finish")

    b = right_side.reshape(count, DOF, RHS)
    x = first_guess.reshape(count, DOF, RHS)
    to_chip, to_link = start(lists, x)
    from_link = link(to_link)
    from_chip = chip(to_chip)
    chip_rows, link_rows = send_rows(lists, codes, couple)
    link_rows = link(link_rows)
    chip_rows = chip(chip_rows)
    r, own, to_chip = first(lists, codes, couple, from_chip, from_link, b, x)
    link_table = table(chip_base, link_base, lists[1], link_rows)
    chip_table = table(link_base, chip_base, lists[0], chip_rows)
    for group in range(CYCLES // MERGED):
        mine = jnp.concatenate([own, chip(to_chip)], axis=0)
        fields = [r]
        for k in range(POWERS - 1):
            if k % 2 == 0:
                value, mine = power(link_table, couple, link_rows, mine, link(mine))
            else:
                value, mine = power(chip_table, couple, chip_rows, mine, chip(mine))
            fields.append(value)
        value, partial = gram(chip_table, couple, mine, chip(mine), *fields)
        fields.append(value)
        sums = total(partial)
        if group + 1 < CYCLES // MERGED:
            x, r, own, to_chip = update(lists, sums, *fields, x)
        else:
            x, r = finish(sums, *fields, x)
    return x.reshape(right_side.shape), r.reshape(right_side.shape)


def solution(mesh):
    rows = ("grp", "leaf", "sub")
    placed = (P(rows, None), P(rows, None), P(rows, None, None), P(rows, None, None), P(rows, None))
    return jax.shard_map(
        shards,
        mesh=mesh,
        in_specs=placed,
        out_specs=(P(rows, None), P(rows, None)),
        check_vma=False,
    )
```

```python
import jax
import jax.numpy as jnp
from jax import lax
from jax.experimental import pallas as pl
from jax.experimental.pallas import tpu as pltpu
from jax.sharding import PartitionSpec as P

DOF = 64
FACES = 6
RHS = 32
SSTEP = 3
CYCLES = 4
MERGED = 2
POWERS = SSTEP * MERGED
GROWTH = 8.0
PACK = 4
META = 16
LANES = 128
AXES = ("leaf", "sub")
F32 = jnp.float32
BF16 = jnp.bfloat16

VMEM = pl.BlockSpec(memory_space=pltpu.VMEM)
ANY = pl.BlockSpec(memory_space=pl.ANY)
PARAMS = pltpu.CompilerParams(vmem_limit_bytes=16 * 1024 * 1024)


def pack(message, blocks):
    for g in range(len(blocks) // PACK):
        message[g] = jnp.concatenate(blocks[PACK * g : PACK * g + PACK], axis=1).astype(BF16)


def unpack(ext, start, message):
    for g in range(message.shape[0]):
        row = message[g]
        for j in range(PACK):
            ext[start + PACK * g + j] = row[:, RHS * j : RHS * j + RHS]


def coupled(table, e, rows, ext):
    gathered = jnp.concatenate([ext[table[e, f]] for f in range(FACES)], axis=0)
    return jnp.dot(rows, gathered, preferred_element_type=F32)


def split(value):
    high = value.astype(BF16)
    return high, (value - high.astype(F32)).astype(BF16)


def listed(lists, side, ext):
    slots = lists.shape[1] // 2
    return [ext[lists[0, side * slots + s]].astype(F32) for s in range(slots)]


def start_kernel(lists, x, to_chip, to_link, ext):
    count = x.shape[0]
    ext[:count] = x[...].astype(BF16)
    ext[count] = jnp.zeros(ext.shape[1:], BF16)
    pack(to_chip, listed(lists, 0, ext))
    pack(to_link, listed(lists, 1, ext))


def rows_kernel(lists, codes, couple, after, to_chip, to_link):
    count, slots = couple.shape[0], to_chip.shape[0]
    lanes = lax.broadcasted_iota(jnp.int32, (1, LANES), 1)
    for side, message in ((0, to_chip), (1, to_link)):
        for s in range(slots):
            place = lists[0, side * slots + s]
            e = jnp.minimum(place, count - 1)
            message[s, :DOF] = couple[e]
            meta = jnp.where(place < count, codes[pl.ds(e, 1), :], count + 2 * slots)
            meta = jnp.where(lanes == FACES, place, meta).astype(F32)
            message[s, DOF:] = jnp.zeros((META, couple.shape[2]), BF16)
            message[s, DOF:, :LANES] = jnp.broadcast_to(meta, (META, LANES)).astype(BF16)


def tables_kernel(lists, codes, chip_rows, link_rows, chip_table, link_table):
    count, slots = codes.shape[0], chip_rows.shape[0]
    reach = count + slots
    chip_base, link_base, empty = count, count + slots, 2 * reach
    sides = ((0, chip_table, chip_rows, link_base, chip_base), (1, link_table, link_rows, chip_base, link_base))
    for side, table, rows, known_base, far_base in sides:
        meta = [rows[s, DOF:, :LANES].astype(F32)[:1].astype(jnp.int32) for s in range(slots)]
        far = [value[:, FACES : FACES + 1] for value in meta]
        near = [lists[:, side * slots + s : side * slots + s + 1] for s in range(slots)]

        def place(at, own, known, listed_at, listed_own):
            found = jnp.where((at >= known_base) & (at < known_base + slots), at - known_base + known, empty)
            for s in range(slots):
                target = jnp.where(listed_at[s] < count, listed_at[s] + listed_own, empty)
                found = jnp.where(at == far_base + s, target, found)
            return jnp.where(at < count, at + own, found)

        table[:count] = place(codes[...], 0, count, far, reach)
        for s in range(slots):
            table[count + s : count + s + 1] = place(meta[s], reach, reach + count, near, 0)


def residual_kernel(lists, positions, couple, from_chip, from_link, b, x, r, own, to_chip, ext):
    count = x.shape[0]
    ext[:count] = x[...].astype(BF16)
    unpack(ext, count, from_chip)
    unpack(ext, count + PACK * from_chip.shape[0], from_link)
    ext[ext.shape[0] - 1] = jnp.zeros(ext.shape[1:], BF16)
    for e in range(count):
        r[e] = b[e] - x[e] + coupled(positions, e, couple[e], ext)
    pack(own, [r[e] for e in range(count)])
    ext[:count] = r[...].astype(BF16)
    ext[count] = jnp.zeros(ext.shape[1:], BF16)
    pack(to_chip, listed(lists, 0, ext))


def extend(ext, mine, theirs):
    unpack(ext, 0, mine)
    unpack(ext, PACK * mine.shape[0], theirs)
    ext[ext.shape[0] - 1] = jnp.zeros(ext.shape[1:], BF16)


def power_kernel(table, couple, extra, mine, theirs, power, message, ext):
    count, slots = couple.shape[0], extra.shape[0]
    extend(ext, mine, theirs)
    values = []
    for e in range(count + slots):
        rows = couple[e] if e < count else extra[e - count, :DOF]
        values.append(coupled(table, e, rows, ext) * (1.0 / GROWTH))
        if e < count:
            power[e] = values[e]
    pack(message, values)


def gram_kernel(table, couple, mine, theirs, *refs):
    fields, (last, left, right, ext) = refs[:POWERS], refs[POWERS:]
    count = couple.shape[0]
    rows = count * DOF
    extend(ext, mine, theirs)
    for e in range(count):
        last[e] = coupled(table, e, couple[e], ext) * (1.0 / GROWTH)
    fields = [field[...].reshape(rows, RHS) for field in (*fields, last)]
    images = [fields[k] - GROWTH * fields[k + 1] for k in range(POWERS)]
    stacked = jnp.concatenate(images + [fields[0], jnp.zeros((rows, RHS), F32)], axis=1)
    high, low = split(stacked)
    width = stacked.shape[1]
    sums = lax.dot_general(
        high, jnp.concatenate([high, low], axis=1), (((0,), (0,)), ((), ())), preferred_element_type=F32
    )
    cross = sums[:, width:]
    gram = sums[:, :width] + cross + cross.T
    half = width // 2
    below = jnp.concatenate([jnp.zeros((RHS, half), F32), gram[half : width - RHS, half:]], axis=0)
    left[...] = jnp.where(block_of(half, 0) > block_of(half, 1), below, gram[:half, :half])
    right[...] = gram[:half, half:]


def block_of(size, dimension):
    return lax.broadcasted_iota(jnp.int32, (size, size), dimension) // RHS


def unpack_gram(left, right):
    half = left.shape[0]
    low_left, right = left[...], right[...]
    row, column = block_of(half, 0), block_of(half, 1)
    first = jnp.where(row <= column, low_left, low_left.T)
    moved = jnp.concatenate([low_left[RHS:], jnp.zeros((RHS, half), F32)], axis=0)
    last = jnp.where(row >= column, moved, moved.T)
    last = jnp.where((row < 3) & (column < 3), last, 0.0)
    return jnp.concatenate(
        [jnp.concatenate([first, right], axis=1), jnp.concatenate([right.T, last], axis=1)], axis=0
    )


def eliminate(gram):
    count = SSTEP * RHS // 8
    groups = [gram[8 * g : 8 * g + 8, :] for g in range(count)]
    shape = groups[0].shape
    row_ids = lax.broadcasted_iota(jnp.int32, shape, 0)
    for home in range(count):
        columns = [
            [jnp.broadcast_to(group[:, 8 * home + m : 8 * home + m + 1], shape) for m in range(8)]
            for group in groups
        ]
        own = list(columns[home])
        panel = groups[home]
        for m in range(8):
            inverse = 1.0 / own[m][m : m + 1, :]
            scaled = panel[m : m + 1, :] * inverse
            panel = jnp.where(row_ids == m, scaled, panel - own[m] * scaled)
            for k in range(m + 1, 8):
                scaled = own[k][m : m + 1, :] * inverse
                own[k] = jnp.where(row_ids == m, scaled, own[k] - own[m] * scaled)
        for g in range(count):
            if g == home:
                groups[g] = panel
                continue
            for m in range(8):
                groups[g] = groups[g] - columns[g][m] * panel[m : m + 1, :]
    return jnp.concatenate(groups, axis=0)[:, SSTEP * RHS :]


def exact(a, b, contract=(1, 0)):
    return lax.dot_general(
        a,
        b,
        (((contract[0],), (contract[1],)), ((), ())),
        precision=lax.Precision.HIGHEST,
        preferred_element_type=F32,
    )


def below(value, size, blocks):
    parts = [jnp.zeros((RHS * blocks, value.shape[1]), F32)] if blocks else []
    rest = size - RHS * blocks - value.shape[0]
    parts.append(value)
    if rest:
        parts.append(jnp.zeros((rest, value.shape[1]), F32))
    return jnp.concatenate(parts, axis=0)


def mixing(left, right):
    gram = unpack_gram(left, right)
    size = gram.shape[0]
    right = RHS * POWERS
    square = SSTEP * RHS
    eye = (
        lax.broadcasted_iota(jnp.int32, (RHS, RHS), 0) == lax.broadcasted_iota(jnp.int32, (RHS, RHS), 1)
    ).astype(F32)

    first = eliminate(jnp.concatenate([gram[:square, :square], gram[:square, right : right + RHS]], axis=1))
    first_left = GROWTH * below(first, square + RHS, 1) - below(first, square + RHS, 0) + below(eye, square + RHS, 0)
    moved = jnp.concatenate([below(first_left, size, k) for k in range(SSTEP)], axis=1)
    images = jnp.concatenate([moved, below(eye, size, POWERS) - below(first, size, 0)], axis=1)
    second = eliminate(exact(images, exact(gram, images), (0, 0)))
    change = exact(moved, second)
    sol = below(first, size, 0) + change
    res = below(first_left, size, 0) - change + GROWTH * below(change[: size - RHS], size, 1)
    return jnp.concatenate([sol, res], axis=1)


def mixed(left, right, fields):
    rows = fields[0].shape[0] * DOF
    mix_high, mix_low = split(mixing(left, right))
    stacked = jnp.concatenate(
        [field[...].reshape(rows, RHS) for field in fields] + [jnp.zeros((rows, RHS), F32)], axis=1
    )
    high, low = split(stacked)
    out = jnp.dot(high, mix_high, preferred_element_type=F32)
    out += jnp.dot(high, mix_low, preferred_element_type=F32)
    out += jnp.dot(low, mix_high, preferred_element_type=F32)
    shape = fields[0].shape
    return out[:, :RHS].reshape(shape), out[:, RHS:].reshape(shape)


def update_kernel(lists, left, right, *refs):
    fields, (x, new_x, r, own, to_chip, ext) = refs[: POWERS + 1], refs[POWERS + 1 :]
    count = x.shape[0]
    step, r[...] = mixed(left, right, fields)
    new_x[...] = x[...] + step
    pack(own, [r[e] for e in range(count)])
    ext[:count] = r[...].astype(BF16)
    ext[count] = jnp.zeros(ext.shape[1:], BF16)
    pack(to_chip, listed(lists, 0, ext))


def finish_kernel(left, right, *refs):
    fields, (x, new_x, r) = refs[: POWERS + 1], refs[POWERS + 1 :]
    step, r[...] = mixed(left, right, fields)
    new_x[...] = x[...] + step


def shards(right_side, first_guess, couple, send_lists, neighbours):
    count = right_side.shape[0]
    slots = send_lists.shape[2]
    devices = lax.axis_size(AXES)
    assert lax.axis_size("sub") == 2 and slots % PACK == 0 and count % PACK == 0
    second = lax.axis_index("sub") == 1

    def shape(dtype, *sizes):
        return jax.ShapeDtypeStruct(sizes, dtype)

    field = shape(F32, count, DOF, RHS)
    slot_message = shape(BF16, slots // PACK, DOF, PACK * RHS)
    own_message = shape(BF16, count // PACK, DOF, PACK * RHS)
    message = shape(BF16, (count + slots) // PACK, DOF, PACK * RHS)
    row_message = shape(BF16, slots, DOF + META, FACES * DOF)
    half_gram = shape(F32, (POWERS + 2) * RHS // 2, (POWERS + 2) * RHS // 2)
    table_shape = shape(jnp.int32, count + slots, LANES)

    def call(kernel, outs, specs, name, blocks=0):
        return pl.pallas_call(
            kernel,
            out_shape=outs,
            in_specs=specs,
            out_specs=[VMEM] * len(outs),
            scratch_shapes=[pltpu.VMEM((blocks, DOF, RHS), BF16)] if blocks else [],
            compiler_params=PARAMS,
            name=name,
        )

    nowhere = count + 2 * slots
    own_lists = jnp.where(send_lists[0] < 0, count, send_lists[0]).astype(jnp.int32)
    lists = jnp.where(second, own_lists[::-1], own_lists).reshape(1, 2 * slots)
    swapped = jnp.where(neighbours < count + slots, neighbours + slots, neighbours - slots)
    codes = jnp.where(second | (neighbours < count), neighbours, swapped)
    codes = jnp.where(neighbours < 0, nowhere, codes).astype(jnp.int32)
    codes = jnp.pad(codes, ((0, 0), (0, LANES - FACES)))

    chip_pairs = [(d, d ^ 1) for d in range(devices)]
    link_pairs = [(d, d + 1 if d % 2 else d - 1) for d in range(devices)]
    link_pairs = [(s, t) for s, t in link_pairs if 0 <= t < devices]

    def chip(value):
        return lax.ppermute(value, AXES, chip_pairs)

    def link(value):
        return lax.ppermute(value, AXES, link_pairs)

    def total(left, right):
        value = jnp.where(second, right, left) + chip(jnp.where(second, left, right))
        step = 2
        while step < devices:
            value = value + lax.ppermute(value, AXES, [(d, d ^ step) for d in range(devices)])
            step *= 2
        other = chip(value)
        return jnp.where(second, other, value), jnp.where(second, value, other)

    start = call(start_kernel, [slot_message] * 2, [VMEM, VMEM], "start", count + 1)
    send_rows = call(rows_kernel, [row_message] * 2, [VMEM, VMEM, VMEM, ANY], "rows")
    tables = call(tables_kernel, [table_shape] * 2, [VMEM] * 4, "tables")
    first = call(
        residual_kernel,
        [field, own_message, slot_message],
        [VMEM] * 7,
        "first_residual",
        nowhere + 1,
    )
    reach = 2 * (count + slots) + 1
    power = call(power_kernel, [field, message], [VMEM] * 5, "power", reach)
    gram = call(
        gram_kernel, [field, half_gram, half_gram], [VMEM] * (4 + POWERS), "power_and_gram", reach
    )
    update = call(
        update_kernel,
        [field, field, own_message, slot_message],
        [VMEM] * (POWERS + 5),
        "solve_update",
        count + 1,
    )
    finish = call(finish_kernel, [field, field], [VMEM] * (POWERS + 4), "solve_finish")

    b = right_side.reshape(count, DOF, RHS)
    x = first_guess.reshape(count, DOF, RHS)
    to_chip, to_link = start(lists, x)
    from_link = link(to_link)
    from_chip = chip(to_chip)
    chip_rows, link_rows = send_rows(lists, codes, couple, from_chip)
    link_rows = link(link_rows)
    chip_rows = chip(chip_rows)
    r, own, to_chip = first(lists, codes, couple, from_chip, from_link, b, x)
    chip_table, link_table = tables(lists, codes, chip_rows, link_rows)
    for group in range(CYCLES // MERGED):
        mine = jnp.concatenate([own, chip(to_chip)], axis=0)
        fields = [r]
        for k in range(POWERS - 1):
            if k % 2 == 0:
                value, mine = power(link_table, couple, link_rows, mine, link(mine))
            else:
                value, mine = power(chip_table, couple, chip_rows, mine, chip(mine))
            fields.append(value)
        value, left, right = gram(chip_table, couple, mine, chip(mine), *fields)
        fields.append(value)
        sums = total(left, right)
        if group + 1 < CYCLES // MERGED:
            x, r, own, to_chip = update(lists, *sums, *fields, x)
        else:
            x, r = finish(*sums, *fields, x)
    return x.reshape(right_side.shape), r.reshape(right_side.shape)


def solution(mesh):
    rows = ("grp", "leaf", "sub")
    placed = (P(rows, None), P(rows, None), P(rows, None, None), P(rows, None, None), P(rows, None))
    return jax.shard_map(
        shards,
        mesh=mesh,
        in_specs=placed,
        out_specs=(P(rows, None), P(rows, None)),
        check_vma=False,
    )
```

```python
import jax
import jax.numpy as jnp
from jax import lax
from jax.experimental import pallas as pl
from jax.experimental.pallas import tpu as pltpu
from jax.sharding import PartitionSpec as P

DOF = 64
FACES = 6
RHS = 32
SSTEP = 3
CYCLES = 4
MERGED = 2
POWERS = SSTEP * MERGED
GROWTH = 8.0
PACK = 4
TRUST_PIVOT = 1e3
TRUST_RESIDUAL = 5e4
TRUST_ROUNDING = 64.0
META = 16
LANES = 128
AXES = ("leaf", "sub")
F32 = jnp.float32
BF16 = jnp.bfloat16

VMEM = pl.BlockSpec(memory_space=pltpu.VMEM)
ANY = pl.BlockSpec(memory_space=pl.ANY)
PARAMS = pltpu.CompilerParams(vmem_limit_bytes=16 * 1024 * 1024)


def pack(message, blocks):
    for g in range(len(blocks) // PACK):
        message[g] = jnp.concatenate(blocks[PACK * g : PACK * g + PACK], axis=1).astype(BF16)


def unpack(ext, start, message):
    for g in range(message.shape[0]):
        row = message[g]
        for j in range(PACK):
            ext[start + PACK * g + j] = row[:, RHS * j : RHS * j + RHS]


def coupled(table, e, rows, ext):
    gathered = jnp.concatenate([ext[table[e, f]] for f in range(FACES)], axis=0)
    return jnp.dot(rows, gathered, preferred_element_type=F32)


def split(value):
    high = value.astype(BF16)
    return high, (value - high.astype(F32)).astype(BF16)


def listed(lists, side, ext):
    slots = lists.shape[1] // 2
    return [ext[lists[0, side * slots + s]].astype(F32) for s in range(slots)]


def start_kernel(lists, x, to_chip, to_link, ext):
    count = x.shape[0]
    ext[:count] = x[...].astype(BF16)
    ext[count] = jnp.zeros(ext.shape[1:], BF16)
    pack(to_chip, listed(lists, 0, ext))
    pack(to_link, listed(lists, 1, ext))


def rows_kernel(lists, codes, couple, after, to_chip, to_link):
    count, slots = couple.shape[0], to_chip.shape[0]
    lanes = lax.broadcasted_iota(jnp.int32, (1, LANES), 1)
    for side, message in ((0, to_chip), (1, to_link)):
        for s in range(slots):
            place = lists[0, side * slots + s]
            e = jnp.minimum(place, count - 1)
            message[s, :DOF] = couple[e]
            meta = jnp.where(place < count, codes[pl.ds(e, 1), :], count + 2 * slots)
            meta = jnp.where(lanes == FACES, place, meta).astype(F32)
            message[s, DOF:] = jnp.zeros((META, couple.shape[2]), BF16)
            message[s, DOF:, :LANES] = jnp.broadcast_to(meta, (META, LANES)).astype(BF16)


def tables_kernel(lists, codes, chip_rows, link_rows, chip_table, link_table):
    count, slots = codes.shape[0], chip_rows.shape[0]
    reach = count + slots
    chip_base, link_base, empty = count, count + slots, 2 * reach
    sides = ((0, chip_table, chip_rows, link_base, chip_base), (1, link_table, link_rows, chip_base, link_base))
    for side, table, rows, known_base, far_base in sides:
        meta = [rows[s, DOF:, :LANES].astype(F32)[:1].astype(jnp.int32) for s in range(slots)]
        far = [value[:, FACES : FACES + 1] for value in meta]
        near = [lists[:, side * slots + s : side * slots + s + 1] for s in range(slots)]

        def place(at, own, known, listed_at, listed_own):
            found = jnp.where((at >= known_base) & (at < known_base + slots), at - known_base + known, empty)
            for s in range(slots):
                target = jnp.where(listed_at[s] < count, listed_at[s] + listed_own, empty)
                found = jnp.where(at == far_base + s, target, found)
            return jnp.where(at < count, at + own, found)

        table[:count] = place(codes[...], 0, count, far, reach)
        for s in range(slots):
            table[count + s : count + s + 1] = place(meta[s], reach, reach + count, near, 0)


def residual_kernel(lists, positions, couple, from_chip, from_link, b, x, r, own, to_chip, ext):
    count = x.shape[0]
    ext[:count] = x[...].astype(BF16)
    unpack(ext, count, from_chip)
    unpack(ext, count + PACK * from_chip.shape[0], from_link)
    ext[ext.shape[0] - 1] = jnp.zeros(ext.shape[1:], BF16)
    for e in range(count):
        r[e] = b[e] - x[e] + coupled(positions, e, couple[e], ext)
    pack(own, [r[e] for e in range(count)])
    ext[:count] = r[...].astype(BF16)
    ext[count] = jnp.zeros(ext.shape[1:], BF16)
    pack(to_chip, listed(lists, 0, ext))


def extend(ext, mine, theirs):
    unpack(ext, 0, mine)
    unpack(ext, PACK * mine.shape[0], theirs)
    ext[ext.shape[0] - 1] = jnp.zeros(ext.shape[1:], BF16)


def power_kernel(table, couple, extra, mine, theirs, power, message, ext):
    count, slots = couple.shape[0], extra.shape[0]
    extend(ext, mine, theirs)
    values = []
    for e in range(count + slots):
        rows = couple[e] if e < count else extra[e - count, :DOF]
        values.append(coupled(table, e, rows, ext) * (1.0 / GROWTH))
        if e < count:
            power[e] = values[e]
    pack(message, values)


def inner_products(columns):
    stacked = jnp.concatenate(columns, axis=1)
    high, low = split(stacked)
    width = stacked.shape[1]
    sums = lax.dot_general(
        high, jnp.concatenate([high, low], axis=1), (((0,), (0,)), ((), ())), preferred_element_type=F32
    )
    cross = sums[:, width:]
    return sums[:, :width] + cross + cross.T


def gram_kernel(table, couple, mine, theirs, *refs):
    fields, (last, left, right, ext) = refs[:POWERS], refs[POWERS:]
    count = couple.shape[0]
    rows = count * DOF
    extend(ext, mine, theirs)
    for e in range(count):
        last[e] = coupled(table, e, couple[e], ext) * (1.0 / GROWTH)
    fields = [field[...].reshape(rows, RHS) for field in (*fields, last)]
    empty = jnp.zeros((rows, RHS), F32)
    gram = inner_products([fields[k] - GROWTH * fields[k + 1] for k in range(POWERS)] + [fields[0], empty])
    squares = jnp.concatenate([(field * field).astype(BF16) for field in (*fields, empty)], axis=1)
    norms = lax.dot_general(
        squares, jnp.ones((rows, LANES), BF16), (((0,), (0,)), ((), ())), preferred_element_type=F32
    )
    half = gram.shape[0] // 2
    below = jnp.concatenate([jnp.zeros((RHS, half), F32), gram[half:, half:][: half - RHS]], axis=0)
    left[...] = jnp.where(block_of(half, 0) > block_of(half, 1), below, gram[:half, :half])
    lanes = lax.broadcasted_iota(jnp.int32, (half, half), 1)
    upper = jnp.where(lanes == half - RHS, norms[:half], gram[:half, half:])
    right[...] = jnp.where(lanes == half - RHS + 1, norms[half:], upper)


def block_of(size, dimension):
    return lax.broadcasted_iota(jnp.int32, (size, size), dimension) // RHS


def unpack_gram(left, right):
    half = left.shape[0]
    low_left, right = left[...], right[...]
    row, column = block_of(half, 0), block_of(half, 1)
    norms = jnp.concatenate([right[:, half - RHS : half - RHS + 1], right[:, half - RHS + 1 : half - RHS + 2]], axis=0)
    right = jnp.where(column < 3, right, 0.0)
    first = jnp.where(row <= column, low_left, low_left.T)
    moved = jnp.concatenate([low_left[RHS:], jnp.zeros((RHS, half), F32)], axis=0)
    last = jnp.where(row >= column, moved, moved.T)
    last = jnp.where((row < 3) & (column < 3), last, 0.0)
    gram = jnp.concatenate(
        [jnp.concatenate([first, right], axis=1), jnp.concatenate([right.T, last], axis=1)], axis=0
    )
    return gram, norms


def eliminate(gram):
    count = SSTEP * RHS // 8
    groups = [gram[8 * g : 8 * g + 8, :] for g in range(count)]
    shape = groups[0].shape
    row_ids = lax.broadcasted_iota(jnp.int32, shape, 0)
    lane_ids = lax.broadcasted_iota(jnp.int32, (1, shape[1]), 1)
    pivots = jnp.zeros((1, shape[1]), F32)
    for home in range(count):
        columns = [
            [jnp.broadcast_to(group[:, 8 * home + m : 8 * home + m + 1], shape) for m in range(8)]
            for group in groups
        ]
        own = list(columns[home])
        panel = groups[home]
        for m in range(8):
            pivot = own[m][m : m + 1, :]
            pivots = jnp.where(lane_ids == 8 * home + m, pivot, pivots)
            inverse = 1.0 / pivot
            scaled = panel[m : m + 1, :] * inverse
            panel = jnp.where(row_ids == m, scaled, panel - own[m] * scaled)
            for k in range(m + 1, 8):
                scaled = own[k][m : m + 1, :] * inverse
                own[k] = jnp.where(row_ids == m, scaled, own[k] - own[m] * scaled)
        for g in range(count):
            if g == home:
                groups[g] = panel
                continue
            for m in range(8):
                groups[g] = groups[g] - columns[g][m] * panel[m : m + 1, :]
    return jnp.concatenate(groups, axis=0)[:, SSTEP * RHS :], pivots


def exact(a, b, contract=(1, 0)):
    return lax.dot_general(
        a,
        b,
        (((contract[0],), (contract[1],)), ((), ())),
        precision=lax.Precision.HIGHEST,
        preferred_element_type=F32,
    )


def below(value, size, blocks):
    parts = [jnp.zeros((RHS * blocks, value.shape[1]), F32)] if blocks else []
    rest = size - RHS * blocks - value.shape[0]
    parts.append(value)
    if rest:
        parts.append(jnp.zeros((rest, value.shape[1]), F32))
    return jnp.concatenate(parts, axis=0)


def mixing(left, right):
    gram, norms = unpack_gram(left, right)
    size = gram.shape[0]
    right = RHS * POWERS
    square = SSTEP * RHS
    eye = (
        lax.broadcasted_iota(jnp.int32, (RHS, RHS), 0) == lax.broadcasted_iota(jnp.int32, (RHS, RHS), 1)
    ).astype(F32)

    first, _ = eliminate(jnp.concatenate([gram[:square, :square], gram[:square, right : right + RHS]], axis=1))
    first_left = GROWTH * below(first, square + RHS, 1) - below(first, square + RHS, 0) + below(eye, square + RHS, 0)
    moved = jnp.concatenate([below(first_left, size, k) for k in range(SSTEP)], axis=1)
    images = jnp.concatenate([moved, below(eye, size, POWERS) - below(first, size, 0)], axis=1)
    projected = exact(images, exact(gram, images), (0, 0))
    second, pivots = eliminate(projected)
    change = exact(moved, second)
    sol = below(first, size, 0) + change
    res = below(first_left, size, 0) - change + GROWTH * below(change[: size - RHS], size, 1)
    is_diagonal = lax.broadcasted_iota(jnp.int32, gram.shape, 0) == lax.broadcasted_iota(jnp.int32, gram.shape, 1)
    scale = jnp.sqrt(jnp.sum(jnp.where(is_diagonal, gram, 0.0), axis=1, keepdims=True))
    reach = jnp.sum(jnp.abs(images) * scale, axis=0, keepdims=True)
    reach = reach * reach
    corner = jnp.where(eye > 0, projected[square:, square:], 0.0)
    left_over = jnp.sum(corner, axis=0, keepdims=True) - jnp.sum(
        projected[:square, square:] * second, axis=0, keepdims=True
    )
    power = (lax.broadcasted_iota(jnp.int32, (size, 1), 0) // RHS).astype(F32)
    rounding = jnp.sum(res * res * (norms * power), axis=0, keepdims=True)
    doubts = [
        jnp.where(reach[:, :square] <= TRUST_PIVOT * pivots[:, :square], 0.0, 1.0),
        jnp.where(reach[:, square:] <= TRUST_RESIDUAL * left_over, 0.0, 1.0),
        jnp.where(jnp.sum(rounding, axis=1, keepdims=True) <= TRUST_ROUNDING * jnp.sum(left_over, axis=1, keepdims=True), 0.0, 1.0),
    ]
    doubt = sum(jnp.sum(value, axis=1, keepdims=True) for value in doubts)
    return jnp.concatenate([sol, res], axis=1), doubt


def combined(mix, fields):
    rows = fields[0].shape[0] * DOF
    stacked = jnp.concatenate([field[...].reshape(rows, RHS) for field in fields], axis=1)
    rest = mix.shape[0] - stacked.shape[1]
    if rest:
        stacked = jnp.concatenate([stacked, jnp.zeros((rows, rest), F32)], axis=1)
    mix_high, mix_low = split(mix)
    high, low = split(stacked)
    out = jnp.dot(high, mix_high, preferred_element_type=F32)
    out += jnp.dot(high, mix_low, preferred_element_type=F32)
    out += jnp.dot(low, mix_high, preferred_element_type=F32)
    shape = fields[0].shape
    return out[:, :RHS].reshape(shape), out[:, RHS:].reshape(shape)


def update_kernel(lists, left, right, *refs):
    fields, (x, new_x, r, own, to_chip, doubt, ext) = refs[: POWERS + 1], refs[POWERS + 1 :]
    count = x.shape[0]
    mix, found = mixing(left, right)
    doubt[...] = jnp.broadcast_to(found, doubt.shape)
    step, r[...] = combined(mix, fields)
    new_x[...] = x[...] + step
    pack(own, [r[e] for e in range(count)])
    ext[:count] = r[...].astype(BF16)
    ext[count] = jnp.zeros(ext.shape[1:], BF16)
    pack(to_chip, listed(lists, 0, ext))


def finish_kernel(left, right, *refs):
    fields, (x, new_x, r, doubt) = refs[: POWERS + 1], refs[POWERS + 1 :]
    mix, found = mixing(left, right)
    doubt[...] = jnp.broadcast_to(found, doubt.shape)
    step, r[...] = combined(mix, fields)
    new_x[...] = x[...] + step


def single_power_kernel(codes, couple, value, from_chip, from_link, power, ext):
    count = value.shape[0]
    ext[:count] = value[...].astype(BF16)
    unpack(ext, count, from_chip)
    unpack(ext, count + PACK * from_chip.shape[0], from_link)
    ext[ext.shape[0] - 1] = jnp.zeros(ext.shape[1:], BF16)
    for e in range(count):
        power[e] = coupled(codes, e, couple[e], ext)


def single_gram_kernel(*refs):
    fields, gram = refs[:-1], refs[-1]
    fields = [field[...].reshape(-1, RHS) for field in fields]
    gram[...] = inner_products([fields[k] - fields[k + 1] for k in range(SSTEP)] + [fields[0]])


def single_update_kernel(gram, *refs):
    fields, (x, new_x, r) = refs[: SSTEP + 1], refs[SSTEP + 1 :]
    first, _ = eliminate(gram)
    size = gram.shape[0]
    eye = (
        lax.broadcasted_iota(jnp.int32, (RHS, RHS), 0) == lax.broadcasted_iota(jnp.int32, (RHS, RHS), 1)
    ).astype(F32)
    res = below(eye, size, 0) - below(first, size, 0) + below(first, size, 1)
    step, r[...] = combined(jnp.concatenate([below(first, size, 0), res], axis=1), fields)
    new_x[...] = x[...] + step


def shards(right_side, first_guess, couple, send_lists, neighbours):
    count = right_side.shape[0]
    slots = send_lists.shape[2]
    devices = lax.axis_size(AXES)
    assert lax.axis_size("sub") == 2 and slots % PACK == 0 and count % PACK == 0
    second = lax.axis_index("sub") == 1

    def shape(dtype, *sizes):
        return jax.ShapeDtypeStruct(sizes, dtype)

    field = shape(F32, count, DOF, RHS)
    slot_message = shape(BF16, slots // PACK, DOF, PACK * RHS)
    own_message = shape(BF16, count // PACK, DOF, PACK * RHS)
    message = shape(BF16, (count + slots) // PACK, DOF, PACK * RHS)
    row_message = shape(BF16, slots, DOF + META, FACES * DOF)
    half_gram = shape(F32, (POWERS + 2) * RHS // 2, (POWERS + 2) * RHS // 2)
    doubt_shape = shape(F32, 8, LANES)
    table_shape = shape(jnp.int32, count + slots, LANES)

    def call(kernel, outs, specs, name, blocks=0):
        return pl.pallas_call(
            kernel,
            out_shape=outs,
            in_specs=specs,
            out_specs=[VMEM] * len(outs),
            scratch_shapes=[pltpu.VMEM((blocks, DOF, RHS), BF16)] if blocks else [],
            compiler_params=PARAMS,
            name=name,
        )

    nowhere = count + 2 * slots
    own_lists = jnp.where(send_lists[0] < 0, count, send_lists[0]).astype(jnp.int32)
    lists = jnp.where(second, own_lists[::-1], own_lists).reshape(1, 2 * slots)
    swapped = jnp.where(neighbours < count + slots, neighbours + slots, neighbours - slots)
    codes = jnp.where(second | (neighbours < count), neighbours, swapped)
    codes = jnp.where(neighbours < 0, nowhere, codes).astype(jnp.int32)
    codes = jnp.pad(codes, ((0, 0), (0, LANES - FACES)))

    chip_pairs = [(d, d ^ 1) for d in range(devices)]
    link_pairs = [(d, d + 1 if d % 2 else d - 1) for d in range(devices)]
    link_pairs = [(s, t) for s, t in link_pairs if 0 <= t < devices]

    def chip(value):
        return lax.ppermute(value, AXES, chip_pairs)

    def link(value):
        return lax.ppermute(value, AXES, link_pairs)

    def total(left, right):
        value = jnp.where(second, right, left) + chip(jnp.where(second, left, right))
        step = 2
        while step < devices:
            value = value + lax.ppermute(value, AXES, [(d, d ^ step) for d in range(devices)])
            step *= 2
        other = chip(value)
        return jnp.where(second, other, value), jnp.where(second, value, other)

    start = call(start_kernel, [slot_message] * 2, [VMEM, VMEM], "start", count + 1)
    send_rows = call(rows_kernel, [row_message] * 2, [VMEM, VMEM, VMEM, ANY], "rows")
    tables = call(tables_kernel, [table_shape] * 2, [VMEM] * 4, "tables")
    first = call(
        residual_kernel,
        [field, own_message, slot_message],
        [VMEM] * 7,
        "first_residual",
        nowhere + 1,
    )
    reach = 2 * (count + slots) + 1
    power = call(power_kernel, [field, message], [VMEM] * 5, "power", reach)
    gram = call(
        gram_kernel, [field, half_gram, half_gram], [VMEM] * (4 + POWERS), "power_and_gram", reach
    )
    update = call(
        update_kernel,
        [field, field, own_message, slot_message, doubt_shape],
        [VMEM] * (POWERS + 5),
        "solve_update",
        count + 1,
    )
    finish = call(finish_kernel, [field, field, doubt_shape], [VMEM] * (POWERS + 4), "solve_finish")

    b = right_side.reshape(count, DOF, RHS)
    x = first_x = first_guess.reshape(count, DOF, RHS)
    doubts = []
    to_chip, to_link = start(lists, x)
    from_link = link(to_link)
    from_chip = chip(to_chip)
    chip_rows, link_rows = send_rows(lists, codes, couple, from_chip)
    link_rows = link(link_rows)
    chip_rows = chip(chip_rows)
    r, own, to_chip = first(lists, codes, couple, from_chip, from_link, b, x)
    chip_table, link_table = tables(lists, codes, chip_rows, link_rows)
    for group in range(CYCLES // MERGED):
        mine = jnp.concatenate([own, chip(to_chip)], axis=0)
        fields = [r]
        for k in range(POWERS - 1):
            if k % 2 == 0:
                value, mine = power(link_table, couple, link_rows, mine, link(mine))
            else:
                value, mine = power(chip_table, couple, chip_rows, mine, chip(mine))
            fields.append(value)
        value, left, right = gram(chip_table, couple, mine, chip(mine), *fields)
        fields.append(value)
        sums = total(left, right)
        if group + 1 < CYCLES // MERGED:
            x, r, own, to_chip, doubt = update(lists, *sums, *fields, x)
        else:
            x, r, doubt = finish(*sums, *fields, x)
        doubts.append(doubt[0, 0])

    single_power = call(single_power_kernel, [field], [VMEM] * 5, "single_power", nowhere + 1)
    single_gram = call(single_gram_kernel, [shape(F32, LANES, LANES)], [VMEM] * (SSTEP + 1), "single_gram")
    single_update = call(single_update_kernel, [field, field], [VMEM] * (SSTEP + 3), "single_update")

    def one_by_one(lists, codes, couple, b, x):
        def slots_of(value):
            to_chip, to_link = start(lists, value)
            return chip(to_chip), link(to_link)

        r, _, _ = first(lists, codes, couple, *slots_of(x), b, x)
        for _ in range(CYCLES):
            fields = [r]
            for _ in range(SSTEP):
                fields += single_power(codes, couple, fields[-1], *slots_of(fields[-1]))
            (value,) = single_gram(*fields)
            step = 1
            while step < devices:
                value = value + lax.ppermute(value, AXES, [(d, d ^ step) for d in range(devices)])
                step *= 2
            x, r = single_update(value, *fields, x)
        return x.reshape(right_side.shape), r.reshape(right_side.shape)

    return lax.cond(
        sum(doubts) == 0,
        lambda *operands: (x.reshape(right_side.shape), r.reshape(right_side.shape)),
        one_by_one,
        lists,
        codes,
        couple,
        b,
        first_x,
    )


def solution(mesh):
    rows = ("grp", "leaf", "sub")
    placed = (P(rows, None), P(rows, None), P(rows, None, None), P(rows, None, None), P(rows, None))
    return jax.shard_map(
        shards,
        mesh=mesh,
        in_specs=placed,
        out_specs=(P(rows, None), P(rows, None)),
        check_vma=False,
    )
```

```python
import jax
import jax.numpy as jnp
from jax import lax
from jax.experimental import pallas as pl
from jax.experimental.pallas import tpu as pltpu
from jax.sharding import PartitionSpec as P

DOF = 64
FACES = 6
RHS = 32
SSTEP = 3
CYCLES = 4
MERGED = 2
POWERS = SSTEP * MERGED
GROWTH = 8.0
PACK = 4
TRUST_PIVOT = 1e3
TRUST_RESIDUAL = 5e4
TRUST_ROUNDING = 64.0
META = 16
LANES = 128
AXES = ("leaf", "sub")
F32 = jnp.float32
BF16 = jnp.bfloat16

VMEM = pl.BlockSpec(memory_space=pltpu.VMEM)
ANY = pl.BlockSpec(memory_space=pl.ANY)
PARAMS = pltpu.CompilerParams(vmem_limit_bytes=16 * 1024 * 1024)


def pack(message, blocks):
    for g in range(len(blocks) // PACK):
        message[g] = jnp.concatenate(blocks[PACK * g : PACK * g + PACK], axis=1).astype(BF16)


def unpack(ext, start, message):
    for g in range(message.shape[0]):
        row = message[g]
        for j in range(PACK):
            ext[start + PACK * g + j] = row[:, RHS * j : RHS * j + RHS]


def coupled(table, e, rows, ext):
    gathered = jnp.concatenate([ext[table[e, f]] for f in range(FACES)], axis=0)
    return jnp.dot(rows, gathered, preferred_element_type=F32)


def split(value):
    high = value.astype(BF16)
    return high, (value - high.astype(F32)).astype(BF16)


def listed(lists, side, ext):
    slots = lists.shape[1] // 2
    return [ext[lists[0, side * slots + s]].astype(F32) for s in range(slots)]


def start_kernel(lists, x, to_chip, to_link, ext):
    count = x.shape[0]
    ext[:count] = x[...].astype(BF16)
    ext[count] = jnp.zeros(ext.shape[1:], BF16)
    pack(to_chip, listed(lists, 0, ext))
    pack(to_link, listed(lists, 1, ext))


def rows_kernel(lists, codes, couple, after, to_chip, to_link, kept):
    kept[...] = couple[...]
    count, slots = couple.shape[0], to_chip.shape[0]
    lanes = lax.broadcasted_iota(jnp.int32, (1, LANES), 1)
    for side, message in ((0, to_chip), (1, to_link)):
        for s in range(slots):
            place = lists[0, side * slots + s]
            e = jnp.minimum(place, count - 1)
            message[s, :DOF] = couple[e]
            meta = jnp.where(place < count, codes[pl.ds(e, 1), :], count + 2 * slots)
            meta = jnp.where(lanes == FACES, place, meta).astype(F32)
            message[s, DOF:] = jnp.zeros((META, couple.shape[2]), BF16)
            message[s, DOF:, :LANES] = jnp.broadcast_to(meta, (META, LANES)).astype(BF16)


def tables_kernel(lists, codes, chip_rows, link_rows, chip_table, link_table):
    count, slots = codes.shape[0], chip_rows.shape[0]
    reach = count + slots
    chip_base, link_base, empty = count, count + slots, 2 * reach
    sides = ((0, chip_table, chip_rows, link_base, chip_base), (1, link_table, link_rows, chip_base, link_base))
    for side, table, rows, known_base, far_base in sides:
        meta = [rows[s, DOF:, :LANES].astype(F32)[:1].astype(jnp.int32) for s in range(slots)]
        far = [value[:, FACES : FACES + 1] for value in meta]
        near = [lists[:, side * slots + s : side * slots + s + 1] for s in range(slots)]

        def place(at, own, known, listed_at, listed_own):
            found = jnp.where((at >= known_base) & (at < known_base + slots), at - known_base + known, empty)
            for s in range(slots):
                target = jnp.where(listed_at[s] < count, listed_at[s] + listed_own, empty)
                found = jnp.where(at == far_base + s, target, found)
            return jnp.where(at < count, at + own, found)

        table[:count] = place(codes[...], 0, count, far, reach)
        for s in range(slots):
            table[count + s : count + s + 1] = place(meta[s], reach, reach + count, near, 0)


def residual_kernel(lists, positions, couple, from_chip, from_link, b, x, r, own, to_chip, ext):
    count = x.shape[0]
    ext[:count] = x[...].astype(BF16)
    unpack(ext, count, from_chip)
    unpack(ext, count + PACK * from_chip.shape[0], from_link)
    ext[ext.shape[0] - 1] = jnp.zeros(ext.shape[1:], BF16)
    for e in range(count):
        r[e] = b[e] - x[e] + coupled(positions, e, couple[e], ext)
    pack(own, [r[e] for e in range(count)])
    ext[:count] = r[...].astype(BF16)
    ext[count] = jnp.zeros(ext.shape[1:], BF16)
    pack(to_chip, listed(lists, 0, ext))


def extend(ext, mine, theirs):
    unpack(ext, 0, mine)
    unpack(ext, PACK * mine.shape[0], theirs)
    ext[ext.shape[0] - 1] = jnp.zeros(ext.shape[1:], BF16)


def power_kernel(table, couple, extra, mine, theirs, power, message, ext):
    count, slots = couple.shape[0], extra.shape[0]
    extend(ext, mine, theirs)
    values = []
    for e in range(count + slots):
        rows = couple[e] if e < count else extra[e - count, :DOF]
        values.append(coupled(table, e, rows, ext) * (1.0 / GROWTH))
        if e < count:
            power[e] = values[e]
    pack(message, values)


def inner_products(columns):
    stacked = jnp.concatenate(columns, axis=1)
    high, low = split(stacked)
    width = stacked.shape[1]
    sums = lax.dot_general(
        high, jnp.concatenate([high, low], axis=1), (((0,), (0,)), ((), ())), preferred_element_type=F32
    )
    cross = sums[:, width:]
    return sums[:, :width] + cross + cross.T


def gram_kernel(table, couple, mine, theirs, *refs):
    fields, (last, left, right, ext) = refs[:POWERS], refs[POWERS:]
    count = couple.shape[0]
    rows = count * DOF
    extend(ext, mine, theirs)
    for e in range(count):
        last[e] = coupled(table, e, couple[e], ext) * (1.0 / GROWTH)
    fields = [field[...].reshape(rows, RHS) for field in (*fields, last)]
    empty = jnp.zeros((rows, RHS), F32)
    gram = inner_products([fields[k] - GROWTH * fields[k + 1] for k in range(POWERS)] + [fields[0], empty])
    norms = jnp.concatenate(
        [jnp.sum(field * field, axis=0, keepdims=True) for field in fields] + [jnp.zeros((1, RHS), F32)], axis=0
    )
    half = gram.shape[0] // 2
    below = jnp.concatenate([jnp.zeros((RHS, half), F32), gram[half:, half:][: half - RHS]], axis=0)
    left[...] = jnp.where(block_of(half, 0) > block_of(half, 1), below, gram[:half, :half])
    right[...] = gram[:half, half:]
    right[: POWERS + 2, half - RHS :] = norms


def block_of(size, dimension):
    return lax.broadcasted_iota(jnp.int32, (size, size), dimension) // RHS


def unpack_gram(left, right):
    half = left.shape[0]
    low_left, right = left[...], right[...]
    row, column = block_of(half, 0), block_of(half, 1)
    by_lane = right[: POWERS + 2].T
    norms = jnp.concatenate([by_lane[half - RHS :, j : j + 1] for j in range(POWERS + 2)], axis=0)
    right = jnp.where(column < 3, right, 0.0)
    first = jnp.where(row <= column, low_left, low_left.T)
    moved = jnp.concatenate([low_left[RHS:], jnp.zeros((RHS, half), F32)], axis=0)
    last = jnp.where(row >= column, moved, moved.T)
    last = jnp.where((row < 3) & (column < 3), last, 0.0)
    gram = jnp.concatenate(
        [jnp.concatenate([first, right], axis=1), jnp.concatenate([right.T, last], axis=1)], axis=0
    )
    return gram, norms


def eliminate(gram):
    count = SSTEP * RHS // 8
    groups = [gram[8 * g : 8 * g + 8, :] for g in range(count)]
    shape = groups[0].shape
    row_ids = lax.broadcasted_iota(jnp.int32, shape, 0)
    lane_ids = lax.broadcasted_iota(jnp.int32, (1, shape[1]), 1)
    pivots = jnp.zeros((1, shape[1]), F32)
    for home in range(count):
        columns = [
            [jnp.broadcast_to(group[:, 8 * home + m : 8 * home + m + 1], shape) for m in range(8)]
            for group in groups
        ]
        own = list(columns[home])
        panel = groups[home]
        for m in range(8):
            pivot = own[m][m : m + 1, :]
            pivots = jnp.where(lane_ids == 8 * home + m, pivot, pivots)
            inverse = 1.0 / pivot
            scaled = panel[m : m + 1, :] * inverse
            panel = jnp.where(row_ids == m, scaled, panel - own[m] * scaled)
            for k in range(m + 1, 8):
                scaled = own[k][m : m + 1, :] * inverse
                own[k] = jnp.where(row_ids == m, scaled, own[k] - own[m] * scaled)
        for g in range(count):
            if g == home:
                groups[g] = panel
                continue
            for m in range(8):
                groups[g] = groups[g] - columns[g][m] * panel[m : m + 1, :]
    return jnp.concatenate(groups, axis=0)[:, SSTEP * RHS :], pivots


def exact(a, b, contract=(1, 0)):
    return lax.dot_general(
        a,
        b,
        (((contract[0],), (contract[1],)), ((), ())),
        precision=lax.Precision.HIGHEST,
        preferred_element_type=F32,
    )


def below(value, size, blocks):
    parts = [jnp.zeros((RHS * blocks, value.shape[1]), F32)] if blocks else []
    rest = size - RHS * blocks - value.shape[0]
    parts.append(value)
    if rest:
        parts.append(jnp.zeros((rest, value.shape[1]), F32))
    return jnp.concatenate(parts, axis=0)


def mixing(left, right):
    gram, norms = unpack_gram(left, right)
    size = gram.shape[0]
    right = RHS * POWERS
    square = SSTEP * RHS
    eye = (
        lax.broadcasted_iota(jnp.int32, (RHS, RHS), 0) == lax.broadcasted_iota(jnp.int32, (RHS, RHS), 1)
    ).astype(F32)

    first, _ = eliminate(jnp.concatenate([gram[:square, :square], gram[:square, right : right + RHS]], axis=1))
    first_left = GROWTH * below(first, square + RHS, 1) - below(first, square + RHS, 0) + below(eye, square + RHS, 0)
    moved = jnp.concatenate([below(first_left, size, k) for k in range(SSTEP)], axis=1)
    images = jnp.concatenate([moved, below(eye, size, POWERS) - below(first, size, 0)], axis=1)
    projected = exact(images, exact(gram, images), (0, 0))
    second, pivots = eliminate(projected)
    change = exact(moved, second)
    sol = below(first, size, 0) + change
    res = below(first_left, size, 0) - change + GROWTH * below(change[: size - RHS], size, 1)
    is_diagonal = lax.broadcasted_iota(jnp.int32, gram.shape, 0) == lax.broadcasted_iota(jnp.int32, gram.shape, 1)
    scale = jnp.sqrt(jnp.sum(jnp.where(is_diagonal, gram, 0.0), axis=1, keepdims=True))
    reach = jnp.sum(jnp.abs(images) * scale, axis=0, keepdims=True)
    reach = reach * reach
    corner = jnp.where(eye > 0, projected[square:, square:], 0.0)
    left_over = jnp.sum(corner, axis=0, keepdims=True) - jnp.sum(
        projected[:square, square:] * second, axis=0, keepdims=True
    )
    power = (lax.broadcasted_iota(jnp.int32, (size, 1), 0) // RHS).astype(F32)
    rounding = jnp.sum(res * res * (norms * power), axis=0, keepdims=True)
    doubts = [
        jnp.where(reach[:, :square] <= TRUST_PIVOT * pivots[:, :square], 0.0, 1.0),
        jnp.where(reach[:, square:] <= TRUST_RESIDUAL * left_over, 0.0, 1.0),
        jnp.where(jnp.sum(rounding, axis=1, keepdims=True) <= TRUST_ROUNDING * jnp.sum(left_over, axis=1, keepdims=True), 0.0, 1.0),
    ]
    doubt = sum(jnp.sum(value, axis=1, keepdims=True) for value in doubts)
    return jnp.concatenate([sol, res], axis=1), doubt


def combined(mix, fields):
    rows = fields[0].shape[0] * DOF
    stacked = jnp.concatenate([field[...].reshape(rows, RHS) for field in fields], axis=1)
    rest = mix.shape[0] - stacked.shape[1]
    if rest:
        stacked = jnp.concatenate([stacked, jnp.zeros((rows, rest), F32)], axis=1)
    mix_high, mix_low = split(mix)
    high, low = split(stacked)
    out = jnp.dot(high, mix_high, preferred_element_type=F32)
    out += jnp.dot(high, mix_low, preferred_element_type=F32)
    out += jnp.dot(low, mix_high, preferred_element_type=F32)
    shape = fields[0].shape
    return out[:, :RHS].reshape(shape), out[:, RHS:].reshape(shape)


def update_kernel(lists, left, right, *refs):
    fields, (x, new_x, r, own, to_chip, doubt, ext) = refs[: POWERS + 1], refs[POWERS + 1 :]
    count = x.shape[0]
    mix, found = mixing(left, right)
    doubt[...] = jnp.broadcast_to(found, doubt.shape)
    step, r[...] = combined(mix, fields)
    new_x[...] = x[...] + step
    pack(own, [r[e] for e in range(count)])
    ext[:count] = r[...].astype(BF16)
    ext[count] = jnp.zeros(ext.shape[1:], BF16)
    pack(to_chip, listed(lists, 0, ext))


def finish_kernel(left, right, *refs):
    fields, (x, earlier, first_r, first_x, new_x, r, doubt) = refs[: POWERS + 1], refs[POWERS + 1 :]
    mix, found = mixing(left, right)
    found = found + earlier[:1, :1]
    doubt[...] = jnp.broadcast_to(found, doubt.shape)
    step, last = combined(mix, fields)
    trusted = (found == 0).reshape(1, 1, 1)
    new_x[...] = jnp.where(trusted, x[...] + step, first_x[...]).reshape(new_x.shape)
    r[...] = jnp.where(trusted, last, first_r[...]).reshape(r.shape)


def single_power_kernel(codes, couple, value, from_chip, from_link, power, ext):
    count = value.shape[0]
    ext[:count] = value[...].astype(BF16)
    unpack(ext, count, from_chip)
    unpack(ext, count + PACK * from_chip.shape[0], from_link)
    ext[ext.shape[0] - 1] = jnp.zeros(ext.shape[1:], BF16)
    for e in range(count):
        power[e] = coupled(codes, e, couple[e], ext)


def single_gram_kernel(*refs):
    fields, gram = refs[:-1], refs[-1]
    fields = [field[...].reshape(-1, RHS) for field in fields]
    gram[...] = inner_products([fields[k] - fields[k + 1] for k in range(SSTEP)] + [fields[0]])


def single_update_kernel(gram, *refs):
    fields, (x, new_x, r) = refs[: SSTEP + 1], refs[SSTEP + 1 :]
    first, _ = eliminate(gram)
    size = gram.shape[0]
    eye = (
        lax.broadcasted_iota(jnp.int32, (RHS, RHS), 0) == lax.broadcasted_iota(jnp.int32, (RHS, RHS), 1)
    ).astype(F32)
    res = below(eye, size, 0) - below(first, size, 0) + below(first, size, 1)
    step, r[...] = combined(jnp.concatenate([below(first, size, 0), res], axis=1), fields)
    new_x[...] = x[...] + step


def shards(right_side, first_guess, couple, send_lists, neighbours):
    count = right_side.shape[0]
    slots = send_lists.shape[2]
    devices = lax.axis_size(AXES)
    assert lax.axis_size("sub") == 2 and slots % PACK == 0 and count % PACK == 0
    second = lax.axis_index("sub") == 1

    def shape(dtype, *sizes):
        return jax.ShapeDtypeStruct(sizes, dtype)

    field = shape(F32, count, DOF, RHS)
    slot_message = shape(BF16, slots // PACK, DOF, PACK * RHS)
    own_message = shape(BF16, count // PACK, DOF, PACK * RHS)
    message = shape(BF16, (count + slots) // PACK, DOF, PACK * RHS)
    rows_shape = shape(BF16, count, DOF, FACES * DOF)
    row_message = shape(BF16, slots, DOF + META, FACES * DOF)
    half_gram = shape(F32, (POWERS + 2) * RHS // 2, (POWERS + 2) * RHS // 2)
    doubt_shape = shape(F32, 8, LANES)
    table_shape = shape(jnp.int32, count + slots, LANES)

    def call(kernel, outs, specs, name, blocks=0):
        return pl.pallas_call(
            kernel,
            out_shape=outs,
            in_specs=specs,
            out_specs=[VMEM] * len(outs),
            scratch_shapes=[pltpu.VMEM((blocks, DOF, RHS), BF16)] if blocks else [],
            compiler_params=PARAMS,
            name=name,
        )

    nowhere = count + 2 * slots
    own_lists = jnp.where(send_lists[0] < 0, count, send_lists[0]).astype(jnp.int32)
    lists = jnp.where(second, own_lists[::-1], own_lists).reshape(1, 2 * slots)
    swapped = jnp.where(neighbours < count + slots, neighbours + slots, neighbours - slots)
    codes = jnp.where(second | (neighbours < count), neighbours, swapped)
    codes = jnp.where(neighbours < 0, nowhere, codes).astype(jnp.int32)
    codes = jnp.pad(codes, ((0, 0), (0, LANES - FACES)))

    chip_pairs = [(d, d ^ 1) for d in range(devices)]
    link_pairs = [(d, d + 1 if d % 2 else d - 1) for d in range(devices)]
    link_pairs = [(s, t) for s, t in link_pairs if 0 <= t < devices]

    def chip(value):
        return lax.ppermute(value, AXES, chip_pairs)

    def link(value):
        return lax.ppermute(value, AXES, link_pairs)

    def total(left, right):
        value = jnp.where(second, right, left) + chip(jnp.where(second, left, right))
        step = 2
        while step < devices:
            value = value + lax.ppermute(value, AXES, [(d, d ^ step) for d in range(devices)])
            step *= 2
        other = chip(value)
        return jnp.where(second, other, value), jnp.where(second, value, other)

    start = call(start_kernel, [slot_message] * 2, [VMEM, VMEM], "start", count + 1)
    send_rows = call(rows_kernel, [row_message, row_message, rows_shape], [VMEM, VMEM, VMEM, ANY], "rows")
    tables = call(tables_kernel, [table_shape] * 2, [VMEM] * 4, "tables")
    first = call(
        residual_kernel,
        [field, own_message, slot_message],
        [VMEM] * 7,
        "first_residual",
        nowhere + 1,
    )
    reach = 2 * (count + slots) + 1
    power = call(power_kernel, [field, message], [VMEM] * 5, "power", reach)
    gram = call(
        gram_kernel, [field, half_gram, half_gram], [VMEM] * (4 + POWERS), "power_and_gram", reach
    )
    update = call(
        update_kernel,
        [field, field, own_message, slot_message, doubt_shape],
        [VMEM] * (POWERS + 5),
        "solve_update",
        count + 1,
    )
    flat = shape(F32, *right_side.shape)
    finish = call(finish_kernel, [flat, flat, doubt_shape], [VMEM] * (POWERS + 7), "solve_finish")

    b = right_side.reshape(count, DOF, RHS)
    x = first_x = first_guess.reshape(count, DOF, RHS)
    assert CYCLES == 2 * MERGED
    to_chip, to_link = start(lists, x)
    from_link = link(to_link)
    from_chip = chip(to_chip)
    chip_rows, link_rows, kept = send_rows(lists, codes, couple, from_chip)
    link_rows = link(link_rows)
    chip_rows = chip(chip_rows)
    r, own, to_chip = first(lists, codes, kept, from_chip, from_link, b, x)
    chip_table, link_table = tables(lists, codes, chip_rows, link_rows)
    for group in range(CYCLES // MERGED):
        mine = jnp.concatenate([own, chip(to_chip)], axis=0)
        fields = [r]
        for k in range(POWERS - 1):
            if k % 2 == 0:
                value, mine = power(link_table, kept, link_rows, mine, link(mine))
            else:
                value, mine = power(chip_table, kept, chip_rows, mine, chip(mine))
            fields.append(value)
        value, left, right = gram(chip_table, kept, mine, chip(mine), *fields)
        fields.append(value)
        sums = total(left, right)
        if group == 0:
            first_r = r
        if group + 1 < CYCLES // MERGED:
            x, r, own, to_chip, doubt = update(lists, *sums, *fields, x)
        else:
            x, r, doubt = finish(*sums, *fields, x, doubt, first_r, first_x)

    single_power = call(single_power_kernel, [field], [VMEM] * 5, "single_power", nowhere + 1)
    single_gram = call(single_gram_kernel, [shape(F32, LANES, LANES)], [VMEM] * (SSTEP + 1), "single_gram")
    single_update = call(single_update_kernel, [field, field], [VMEM] * (SSTEP + 3), "single_update")

    def slots_of(value):
        to_chip, to_link = start(lists, value)
        return chip(to_chip), link(to_link)

    def one_cycle(_, state):
        x, r = (value.reshape(count, DOF, RHS) for value in state)
        fields = [r]
        for _ in range(SSTEP):
            fields += single_power(codes, couple, fields[-1], *slots_of(fields[-1]))
        (value,) = single_gram(*fields)
        step = 1
        while step < devices:
            value = value + lax.ppermute(value, AXES, [(d, d ^ step) for d in range(devices)])
            step *= 2
        x, r = single_update(value, *fields, x)
        return x.reshape(right_side.shape), r.reshape(right_side.shape)

    return lax.fori_loop(0, jnp.where(doubt[0, 0] == 0, 0, CYCLES), one_cycle, (x, r))


def solution(mesh):
    rows = ("grp", "leaf", "sub")
    placed = (P(rows, None), P(rows, None), P(rows, None, None), P(rows, None, None), P(rows, None))
    return jax.shard_map(
        shards,
        mesh=mesh,
        in_specs=placed,
        out_specs=(P(rows, None), P(rows, None)),
        check_vma=False,
    )
```

```python
import jax
import jax.numpy as jnp
from jax import lax
from jax.experimental import pallas as pl
from jax.experimental.pallas import tpu as pltpu
from jax.sharding import PartitionSpec as P

DOF = 64
FACES = 6
RHS = 32
SSTEP = 3
CYCLES = 4
MERGED = 2
POWERS = SSTEP * MERGED
GROWTH = 8.0
PACK = 4
TRUST_PIVOT = 1e3
TRUST_RESIDUAL = 5e4
TRUST_ROUNDING = 64.0
META = 16
LANES = 128
AXES = ("leaf", "sub")
F32 = jnp.float32
BF16 = jnp.bfloat16

VMEM = pl.BlockSpec(memory_space=pltpu.VMEM)
SMEM = pl.BlockSpec(memory_space=pltpu.SMEM)
ANY = pl.BlockSpec(memory_space=pl.ANY)
PARAMS = pltpu.CompilerParams(vmem_limit_bytes=16 * 1024 * 1024)


def pack(message, blocks):
    for g in range(len(blocks) // PACK):
        message[g] = jnp.concatenate(blocks[PACK * g : PACK * g + PACK], axis=1).astype(BF16)


def unpack(ext, start, message):
    for g in range(message.shape[0]):
        row = message[g]
        for j in range(PACK):
            ext[start + PACK * g + j] = row[:, RHS * j : RHS * j + RHS]


def coupled(table, e, rows, ext):
    gathered = jnp.concatenate([ext[table[e, f]] for f in range(FACES)], axis=0)
    return jnp.dot(rows, gathered, preferred_element_type=F32)


def split(value):
    high = value.astype(BF16)
    return high, (value - high.astype(F32)).astype(BF16)


def listed(lists, side, ext):
    slots = lists.shape[1] // 2
    return [ext[lists[0, side * slots + s]].astype(F32) for s in range(slots)]


def first_kernel(lists, flat, x, to_chip, to_link, ext):
    x[...] = flat[...].reshape(x.shape)
    start_kernel(lists, x, to_chip, to_link, ext)


def start_kernel(lists, x, to_chip, to_link, ext):
    count = x.shape[0]
    ext[:count] = x[...].astype(BF16)
    ext[count] = jnp.zeros(ext.shape[1:], BF16)
    pack(to_chip, listed(lists, 0, ext))
    pack(to_link, listed(lists, 1, ext))


def rows_kernel(lists, codes, couple, after, to_chip, to_link, kept):
    kept[...] = couple[...]
    count, slots = couple.shape[0], to_chip.shape[0]
    lanes = lax.broadcasted_iota(jnp.int32, (1, LANES), 1)
    for side, message in ((0, to_chip), (1, to_link)):
        for s in range(slots):
            place = lists[0, side * slots + s]
            e = jnp.minimum(place, count - 1)
            message[s, :DOF] = couple[e]
            meta = jnp.where(place < count, codes[pl.ds(e, 1), :], count + 2 * slots)
            meta = jnp.where(lanes == FACES, place, meta).astype(F32)
            message[s, DOF:] = jnp.zeros((META, couple.shape[2]), BF16)
            message[s, DOF:, :LANES] = jnp.broadcast_to(meta, (META, LANES)).astype(BF16)


def tables_kernel(lists, codes, chip_rows, link_rows, chip_table, link_table):
    count, slots = codes.shape[0], chip_rows.shape[0]
    reach = count + slots
    chip_base, link_base, empty = count, count + slots, 2 * reach
    sides = ((0, chip_table, chip_rows, link_base, chip_base), (1, link_table, link_rows, chip_base, link_base))
    for side, table, rows, known_base, far_base in sides:
        meta = [rows[s, DOF:, :LANES].astype(F32)[:1].astype(jnp.int32) for s in range(slots)]
        far = [value[:, FACES : FACES + 1] for value in meta]
        near = [lists[:, side * slots + s : side * slots + s + 1] for s in range(slots)]

        def place(at, own, known, listed_at, listed_own):
            found = jnp.where((at >= known_base) & (at < known_base + slots), at - known_base + known, empty)
            for s in range(slots):
                target = jnp.where(listed_at[s] < count, listed_at[s] + listed_own, empty)
                found = jnp.where(at == far_base + s, target, found)
            return jnp.where(at < count, at + own, found)

        table[:count] = place(codes[...], 0, count, far, reach)
        for s in range(slots):
            table[count + s : count + s + 1] = place(meta[s], reach, reach + count, near, 0)


def residual_kernel(lists, positions, couple, from_chip, from_link, b, x, r, own, to_chip, ext):
    count = x.shape[0]
    ext[:count] = x[...].astype(BF16)
    unpack(ext, count, from_chip)
    unpack(ext, count + PACK * from_chip.shape[0], from_link)
    ext[ext.shape[0] - 1] = jnp.zeros(ext.shape[1:], BF16)
    for e in range(count):
        r[e] = b[e] - x[e] + coupled(positions, e, couple[e], ext)
    pack(own, [r[e] for e in range(count)])
    ext[:count] = r[...].astype(BF16)
    ext[count] = jnp.zeros(ext.shape[1:], BF16)
    pack(to_chip, listed(lists, 0, ext))


def extend(ext, mine, theirs):
    unpack(ext, 0, mine)
    unpack(ext, PACK * mine.shape[0], theirs)
    ext[ext.shape[0] - 1] = jnp.zeros(ext.shape[1:], BF16)


def power_kernel(table, couple, extra, mine, theirs, power, message, ext):
    count, slots = couple.shape[0], extra.shape[0]
    extend(ext, mine, theirs)
    values = []
    for e in range(count + slots):
        rows = couple[e] if e < count else extra[e - count, :DOF]
        values.append(coupled(table, e, rows, ext) * (1.0 / GROWTH))
        if e < count:
            power[e] = values[e]
    pack(message, values)


def inner_products(columns):
    stacked = jnp.concatenate(columns, axis=1)
    high, low = split(stacked)
    width = stacked.shape[1]
    sums = lax.dot_general(
        high, jnp.concatenate([high, low], axis=1), (((0,), (0,)), ((), ())), preferred_element_type=F32
    )
    cross = sums[:, width:]
    return sums[:, :width] + cross + cross.T


def gram_kernel(table, couple, mine, theirs, *refs):
    fields, (last, left, right, ext) = refs[:POWERS], refs[POWERS:]
    count = couple.shape[0]
    rows = count * DOF
    extend(ext, mine, theirs)
    for e in range(count):
        last[e] = coupled(table, e, couple[e], ext) * (1.0 / GROWTH)
    fields = [field[...].reshape(rows, RHS) for field in (*fields, last)]
    empty = jnp.zeros((rows, RHS), F32)
    gram = inner_products([fields[k] - GROWTH * fields[k + 1] for k in range(POWERS)] + [fields[0], empty])
    norms = jnp.concatenate(
        [jnp.sum(field * field, axis=0, keepdims=True) for field in fields] + [jnp.zeros((1, RHS), F32)], axis=0
    )
    half = gram.shape[0] // 2
    below = jnp.concatenate([jnp.zeros((RHS, half), F32), gram[half:, half:][: half - RHS]], axis=0)
    left[...] = jnp.where(block_of(half, 0) > block_of(half, 1), below, gram[:half, :half])
    right[...] = gram[:half, half:]
    right[: POWERS + 2, half - RHS :] = norms


def block_of(size, dimension):
    return lax.broadcasted_iota(jnp.int32, (size, size), dimension) // RHS


def unpack_gram(left, right):
    half = left.shape[0]
    low_left, right = left[...], right[...]
    row, column = block_of(half, 0), block_of(half, 1)
    norms = jnp.concatenate([right[j : j + 1, half - RHS :] for j in range(POWERS + 2)], axis=1)
    right = jnp.where(column < 3, right, 0.0)
    first = jnp.where(row <= column, low_left, low_left.T)
    moved = jnp.concatenate([low_left[RHS:], jnp.zeros((RHS, half), F32)], axis=0)
    last = jnp.where(row >= column, moved, moved.T)
    last = jnp.where((row < 3) & (column < 3), last, 0.0)
    gram = jnp.concatenate(
        [jnp.concatenate([first, right], axis=1), jnp.concatenate([right.T, last], axis=1)], axis=0
    )
    return gram, norms


def eliminate(gram):
    count = SSTEP * RHS // 8
    groups = [gram[8 * g : 8 * g + 8, :] for g in range(count)]
    shape = groups[0].shape
    row_ids = lax.broadcasted_iota(jnp.int32, shape, 0)
    lane_ids = lax.broadcasted_iota(jnp.int32, (1, shape[1]), 1)
    pivots = jnp.zeros((1, shape[1]), F32)
    for home in range(count):
        columns = [
            [jnp.broadcast_to(group[:, 8 * home + m : 8 * home + m + 1], shape) for m in range(8)]
            for group in groups
        ]
        own = list(columns[home])
        panel = groups[home]
        for m in range(8):
            pivot = own[m][m : m + 1, :]
            pivots = jnp.where(lane_ids == 8 * home + m, pivot, pivots)
            inverse = 1.0 / pivot
            scaled = panel[m : m + 1, :] * inverse
            panel = jnp.where(row_ids == m, scaled, panel - own[m] * scaled)
            for k in range(m + 1, 8):
                scaled = own[k][m : m + 1, :] * inverse
                own[k] = jnp.where(row_ids == m, scaled, own[k] - own[m] * scaled)
        for g in range(count):
            if g == home:
                groups[g] = panel
                continue
            for m in range(8):
                groups[g] = groups[g] - columns[g][m] * panel[m : m + 1, :]
    return jnp.concatenate(groups, axis=0)[:, SSTEP * RHS :], pivots


def exact(a, b, contract=(1, 0)):
    return lax.dot_general(
        a,
        b,
        (((contract[0],), (contract[1],)), ((), ())),
        precision=lax.Precision.HIGHEST,
        preferred_element_type=F32,
    )


def below(value, size, blocks):
    parts = [jnp.zeros((RHS * blocks, value.shape[1]), F32)] if blocks else []
    rest = size - RHS * blocks - value.shape[0]
    parts.append(value)
    if rest:
        parts.append(jnp.zeros((rest, value.shape[1]), F32))
    return jnp.concatenate(parts, axis=0)


def weighted(weights, rows):
    return jnp.dot(weights.astype(BF16), rows.astype(BF16), preferred_element_type=F32)


def mixing(left, right):
    gram, norms = unpack_gram(left, right)
    size = gram.shape[0]
    right = RHS * POWERS
    square = SSTEP * RHS
    eye = (
        lax.broadcasted_iota(jnp.int32, (RHS, RHS), 0) == lax.broadcasted_iota(jnp.int32, (RHS, RHS), 1)
    ).astype(F32)

    first, _ = eliminate(jnp.concatenate([gram[:square, :square], gram[:square, right : right + RHS]], axis=1))
    first_left = GROWTH * below(first, square + RHS, 1) - below(first, square + RHS, 0) + below(eye, square + RHS, 0)
    moved = jnp.concatenate([below(first_left, size, k) for k in range(SSTEP)], axis=1)
    images = jnp.concatenate([moved, below(eye, size, POWERS) - below(first, size, 0)], axis=1)
    projected = exact(images, exact(gram, images), (0, 0))
    second, pivots = eliminate(projected)
    change = exact(moved, second)
    sol = below(first, size, 0) + change
    res = below(first_left, size, 0) - change + GROWTH * below(change[: size - RHS], size, 1)
    half = size // 2
    is_diagonal = lax.broadcasted_iota(jnp.int32, (half, half), 0) == lax.broadcasted_iota(jnp.int32, (half, half), 1)
    diagonal = jnp.concatenate(
        [
            jnp.sum(jnp.where(is_diagonal, block, 0.0), axis=0, keepdims=True)
            for block in (gram[:half, :half], gram[half:, half:])
        ],
        axis=1,
    )
    reach = weighted(jnp.sqrt(diagonal), jnp.abs(images))
    reach = reach * reach
    corner = jnp.where(eye > 0, projected[square:, square:], 0.0)
    left_over = jnp.sum(corner, axis=0, keepdims=True) - jnp.sum(
        projected[:square, square:] * second, axis=0, keepdims=True
    )
    power = (lax.broadcasted_iota(jnp.int32, (1, size), 1) // RHS).astype(F32)
    rounding = weighted(norms * power, res * res)
    doubts = [
        jnp.where(reach[:, :square] <= TRUST_PIVOT * pivots[:, :square], 0.0, 1.0),
        jnp.where(reach[:, square:] <= TRUST_RESIDUAL * left_over, 0.0, 1.0),
        jnp.where(jnp.sum(rounding, axis=1, keepdims=True) <= TRUST_ROUNDING * jnp.sum(left_over, axis=1, keepdims=True), 0.0, 1.0),
    ]
    doubt = sum(jnp.sum(value, axis=1, keepdims=True) for value in doubts)
    return jnp.concatenate([sol, res], axis=1), doubt


def stack_kernel(*refs):
    fields, (high, low) = refs[:-2], refs[-2:]
    rows = fields[0].shape[0] * DOF
    columns = [field[...].reshape(rows, RHS) for field in fields]
    rest = high.shape[1] - RHS * len(fields)
    if rest:
        columns.append(jnp.zeros((rows, rest), F32))
    high[...], low[...] = split(jnp.concatenate(columns, axis=1))


def combined(mix, high, low, shape):
    mix_high, mix_low = split(mix)
    width = mix.shape[1]
    out = jnp.dot(high[...], jnp.concatenate([mix_high, mix_low], axis=1), preferred_element_type=F32)
    out = out[:, :width] + out[:, width:] + jnp.dot(low[...], mix_high, preferred_element_type=F32)
    return out[:, :RHS].reshape(shape), out[:, RHS:].reshape(shape)


def update_kernel(lists, left, right, high, low, x, new_x, r, own, to_chip, doubt, ext):
    count = x.shape[0]
    mix, found = mixing(left, right)
    doubt[...] = jnp.broadcast_to(found, doubt.shape)
    step, r[...] = combined(mix, high, low, x.shape)
    new_x[...] = x[...] + step
    pack(own, [r[e] for e in range(count)])
    ext[:count] = r[...].astype(BF16)
    ext[count] = jnp.zeros(ext.shape[1:], BF16)
    pack(to_chip, listed(lists, 0, ext))


def finish_kernel(left, right, high, low, x, earlier, first_r, first_x, new_x, r, repeats):
    mix, found = mixing(left, right)
    found = found + earlier[:1, :1]
    repeats[0] = jnp.where(found[0, 0] == 0, 0, CYCLES)
    step, last = combined(mix, high, low, x.shape)
    trusted = (found == 0).reshape(1, 1, 1)
    new_x[...] = jnp.where(trusted, x[...] + step, first_x[...]).reshape(new_x.shape)
    r[...] = jnp.where(trusted, last, first_r[...]).reshape(r.shape)


def single_power_kernel(codes, couple, value, from_chip, from_link, power, ext):
    count = value.shape[0]
    ext[:count] = value[...].astype(BF16)
    unpack(ext, count, from_chip)
    unpack(ext, count + PACK * from_chip.shape[0], from_link)
    ext[ext.shape[0] - 1] = jnp.zeros(ext.shape[1:], BF16)
    for e in range(count):
        power[e] = coupled(codes, e, couple[e], ext)


def single_gram_kernel(*refs):
    fields, gram = refs[:-1], refs[-1]
    fields = [field[...].reshape(-1, RHS) for field in fields]
    gram[...] = inner_products([fields[k] - fields[k + 1] for k in range(SSTEP)] + [fields[0]])


def single_update_kernel(gram, high, low, x, new_x, r):
    first, _ = eliminate(gram)
    size = gram.shape[0]
    eye = (
        lax.broadcasted_iota(jnp.int32, (RHS, RHS), 0) == lax.broadcasted_iota(jnp.int32, (RHS, RHS), 1)
    ).astype(F32)
    res = below(eye, size, 0) - below(first, size, 0) + below(first, size, 1)
    step, r[...] = combined(jnp.concatenate([below(first, size, 0), res], axis=1), high, low, x.shape)
    new_x[...] = x[...] + step


def shards(right_side, first_guess, couple, send_lists, neighbours):
    count = right_side.shape[0]
    slots = send_lists.shape[2]
    devices = lax.axis_size(AXES)
    assert lax.axis_size("sub") == 2 and slots % PACK == 0 and count % PACK == 0
    second = lax.axis_index("sub") == 1

    def shape(dtype, *sizes):
        return jax.ShapeDtypeStruct(sizes, dtype)

    field = shape(F32, count, DOF, RHS)
    slot_message = shape(BF16, slots // PACK, DOF, PACK * RHS)
    own_message = shape(BF16, count // PACK, DOF, PACK * RHS)
    message = shape(BF16, (count + slots) // PACK, DOF, PACK * RHS)
    rows_shape = shape(BF16, count, DOF, FACES * DOF)
    row_message = shape(BF16, slots, DOF + META, FACES * DOF)
    half_gram = shape(F32, (POWERS + 2) * RHS // 2, (POWERS + 2) * RHS // 2)
    doubt_shape = shape(F32, 8, LANES)
    table_shape = shape(jnp.int32, count + slots, LANES)

    def call(kernel, outs, specs, name, blocks=0, last=VMEM):
        return pl.pallas_call(
            kernel,
            out_shape=outs,
            in_specs=specs,
            out_specs=[VMEM] * (len(outs) - 1) + [last],
            scratch_shapes=[pltpu.VMEM((blocks, DOF, RHS), BF16)] if blocks else [],
            compiler_params=PARAMS,
            name=name,
        )

    nowhere = count + 2 * slots
    own_lists = jnp.where(send_lists[0] < 0, count, send_lists[0]).astype(jnp.int32)
    lists = jnp.where(second, own_lists[::-1], own_lists).reshape(1, 2 * slots)
    swapped = jnp.where(neighbours < count + slots, neighbours + slots, neighbours - slots)
    codes = jnp.where(second | (neighbours < count), neighbours, swapped)
    codes = jnp.where(neighbours < 0, nowhere, codes).astype(jnp.int32)
    codes = jnp.pad(codes, ((0, 0), (0, LANES - FACES)))

    chip_pairs = [(d, d ^ 1) for d in range(devices)]
    link_pairs = [(d, d + 1 if d % 2 else d - 1) for d in range(devices)]
    link_pairs = [(s, t) for s, t in link_pairs if 0 <= t < devices]

    def chip(value):
        return lax.ppermute(value, AXES, chip_pairs)

    def link(value):
        return lax.ppermute(value, AXES, link_pairs)

    def total(left, right):
        value = jnp.where(second, right, left) + chip(jnp.where(second, left, right))
        steps = [1 << k for k in range(1, devices.bit_length() - 1)]
        for first_step, second_step in zip(steps, steps[1:] + steps[:1]):
            pairs = [(d, d ^ (second_step if d % 2 else first_step)) for d in range(devices)]
            value = value + lax.ppermute(value, AXES, pairs)
        other = chip(value)
        return jnp.where(second, other, value), jnp.where(second, value, other)

    start = call(start_kernel, [slot_message] * 2, [VMEM, VMEM], "start", count + 1)
    prepare = call(first_kernel, [field] + [slot_message] * 2, [VMEM, VMEM], "prepare", count + 1)
    send_rows = call(rows_kernel, [row_message, row_message, rows_shape], [VMEM, VMEM, VMEM, ANY], "rows")
    tables = call(tables_kernel, [table_shape] * 2, [VMEM] * 4, "tables")
    first = call(
        residual_kernel,
        [field, own_message, slot_message],
        [VMEM] * 7,
        "first_residual",
        nowhere + 1,
    )
    reach = 2 * (count + slots) + 1
    power = call(power_kernel, [field, message], [VMEM] * 5, "power", reach)
    gram = call(
        gram_kernel, [field, half_gram, half_gram], [VMEM] * (4 + POWERS), "power_and_gram", reach
    )
    def stacked(fields):
        width = -(-len(fields) * RHS // LANES) * LANES
        parts = [shape(BF16, count * DOF, width)] * 2
        return call(stack_kernel, parts, [VMEM] * len(fields), "stack")(*fields)

    update = call(
        update_kernel,
        [field, field, own_message, slot_message, doubt_shape],
        [VMEM] * 6,
        "solve_update",
        count + 1,
    )
    flat = shape(F32, *right_side.shape)
    finish = call(finish_kernel, [flat, flat, shape(jnp.int32, 1)], [VMEM] * 8, "solve_finish", last=SMEM)

    b = right_side.reshape(count, DOF, RHS)
    assert CYCLES == 2 * MERGED
    first_x, to_chip, to_link = prepare(lists, first_guess)
    x = first_x
    from_link = link(to_link)
    from_chip = chip(to_chip)
    chip_rows, link_rows, kept = send_rows(lists, codes, couple, from_chip)
    link_rows = link(link_rows)
    chip_rows = chip(chip_rows)
    r, own, to_chip = first(lists, codes, kept, from_chip, from_link, b, x)
    chip_table, link_table = tables(lists, codes, chip_rows, link_rows)
    for group in range(CYCLES // MERGED):
        mine = jnp.concatenate([own, chip(to_chip)], axis=0)
        fields = [r]
        for k in range(POWERS - 1):
            if k % 2 == 0:
                value, mine = power(link_table, kept, link_rows, mine, link(mine))
            else:
                value, mine = power(chip_table, kept, chip_rows, mine, chip(mine))
            fields.append(value)
        value, left, right = gram(chip_table, kept, mine, chip(mine), *fields)
        fields.append(value)
        sums = total(left, right)
        if group == 0:
            first_r = r
        if group + 1 < CYCLES // MERGED:
            x, r, own, to_chip, doubt = update(lists, *sums, *stacked(fields), x)
        else:
            x, r, repeats = finish(*sums, *stacked(fields), x, doubt, first_r, first_x)

    single_power = call(single_power_kernel, [field], [VMEM] * 5, "single_power", nowhere + 1)
    single_gram = call(single_gram_kernel, [shape(F32, LANES, LANES)], [VMEM] * (SSTEP + 1), "single_gram")
    single_update = call(single_update_kernel, [field, field], [VMEM] * 4, "single_update")

    def slots_of(value):
        to_chip, to_link = start(lists, value)
        return chip(to_chip), link(to_link)

    def one_cycle(_, state):
        x, r = (value.reshape(count, DOF, RHS) for value in state)
        fields = [r]
        for _ in range(SSTEP):
            fields += single_power(codes, couple, fields[-1], *slots_of(fields[-1]))
        (value,) = single_gram(*fields)
        step = 1
        while step < devices:
            value = value + lax.ppermute(value, AXES, [(d, d ^ step) for d in range(devices)])
            step *= 2
        x, r = single_update(value, *stacked(fields), x)
        return x.reshape(right_side.shape), r.reshape(right_side.shape)

    return lax.fori_loop(0, repeats[0], one_cycle, (x, r))


def solution(mesh):
    rows = ("grp", "leaf", "sub")
    placed = (P(rows, None), P(rows, None), P(rows, None, None), P(rows, None, None), P(rows, None))
    return jax.shard_map(
        shards,
        mesh=mesh,
        in_specs=placed,
        out_specs=(P(rows, None), P(rows, None)),
        check_vma=False,
    )
```

```python
import jax
import jax.numpy as jnp
from jax import lax
from jax.experimental import pallas as pl
from jax.experimental.pallas import tpu as pltpu
from jax.sharding import PartitionSpec as P

DOF = 64
FACES = 6
RHS = 32
SSTEP = 3
CYCLES = 4
MERGED = 2
POWERS = SSTEP * MERGED
GROWTH = 8.0
PACK = 4
TRUST_PIVOT = 1e3
TRUST_RESIDUAL = 5e4
TRUST_ROUNDING = 64.0
META = 16
LANES = 128
AXES = ("leaf", "sub")
F32 = jnp.float32
BF16 = jnp.bfloat16

VMEM = pl.BlockSpec(memory_space=pltpu.VMEM)
SMEM = pl.BlockSpec(memory_space=pltpu.SMEM)
ANY = pl.BlockSpec(memory_space=pl.ANY)
PARAMS = pltpu.CompilerParams(vmem_limit_bytes=16 * 1024 * 1024)


def pack(message, blocks):
    for g in range(len(blocks) // PACK):
        message[g] = jnp.concatenate(blocks[PACK * g : PACK * g + PACK], axis=1).astype(BF16)


def unpack(ext, start, message):
    for g in range(message.shape[0]):
        row = message[g]
        for j in range(PACK):
            ext[start + PACK * g + j] = row[:, RHS * j : RHS * j + RHS]


def coupled(table, e, rows, ext):
    gathered = jnp.concatenate([ext[table[e, f]] for f in range(FACES)], axis=0)
    return jnp.dot(rows, gathered, preferred_element_type=F32)


def split(value):
    high = value.astype(BF16)
    return high, (value - high.astype(F32)).astype(BF16)


def listed(lists, side, ext):
    slots = lists.shape[1] // 2
    return [ext[lists[0, side * slots + s]].astype(F32) for s in range(slots)]


def first_kernel(send_lists, guess, couple, x, kept, forward, backward, lists, flat, ext, sems):
    copies = [
        pltpu.make_async_copy(source, target, sems.at[k])
        for k, (source, target) in enumerate(((send_lists, lists), (guess, flat), (couple, kept)))
    ]
    for copy in copies:
        copy.start()
    count = x.shape[0]
    ext[count] = jnp.zeros(ext.shape[1:], BF16)
    copies[1].wait()
    x[...] = flat[...].reshape(x.shape)
    ext[:count] = x[...].astype(BF16)
    copies[0].wait()
    for side, message in ((0, forward), (1, backward)):
        places = [lists[0, side, s] for s in range(lists.shape[2])]
        pack(message, [ext[jnp.where(place < 0, count, place)].astype(F32) for place in places])
    copies[2].wait()


def start_kernel(lists, x, to_chip, to_link, ext):
    count = x.shape[0]
    ext[:count] = x[...].astype(BF16)
    ext[count] = jnp.zeros(ext.shape[1:], BF16)
    pack(to_chip, listed(lists, 0, ext))
    pack(to_link, listed(lists, 1, ext))


def rows_kernel(lists, codes, couple, to_chip, to_link):
    count, slots = couple.shape[0], to_chip.shape[0]
    lanes = lax.broadcasted_iota(jnp.int32, (1, LANES), 1)
    for side, message in ((0, to_chip), (1, to_link)):
        for s in range(slots):
            place = lists[0, side * slots + s]
            e = jnp.minimum(place, count - 1)
            message[s, :DOF] = couple[e]
            meta = jnp.where(place < count, codes[pl.ds(e, 1), :], count + 2 * slots)
            meta = jnp.where(lanes == FACES, place, meta).astype(F32)
            message[s, DOF:] = jnp.zeros((META, couple.shape[2]), BF16)
            message[s, DOF:, :LANES] = jnp.broadcast_to(meta, (META, LANES)).astype(BF16)


def tables_kernel(lists, codes, chip_rows, link_rows, chip_table, link_table):
    count, slots = codes.shape[0], chip_rows.shape[0]
    reach = count + slots
    chip_base, link_base, empty = count, count + slots, 2 * reach
    sides = ((0, chip_table, chip_rows, link_base, chip_base), (1, link_table, link_rows, chip_base, link_base))
    for side, table, rows, known_base, far_base in sides:
        meta = [rows[s, DOF:, :LANES].astype(F32)[:1].astype(jnp.int32) for s in range(slots)]
        far = [value[:, FACES : FACES + 1] for value in meta]
        near = [lists[:, side * slots + s : side * slots + s + 1] for s in range(slots)]

        def place(at, own, known, listed_at, listed_own):
            found = jnp.where((at >= known_base) & (at < known_base + slots), at - known_base + known, empty)
            for s in range(slots):
                target = jnp.where(listed_at[s] < count, listed_at[s] + listed_own, empty)
                found = jnp.where(at == far_base + s, target, found)
            return jnp.where(at < count, at + own, found)

        table[:count] = place(codes[...], 0, count, far, reach)
        for s in range(slots):
            table[count + s : count + s + 1] = place(meta[s], reach, reach + count, near, 0)


def residual_kernel(lists, positions, couple, from_chip, from_link, b, x, r, own, to_chip, ext):
    count = x.shape[0]
    ext[:count] = x[...].astype(BF16)
    unpack(ext, count, from_chip)
    unpack(ext, count + PACK * from_chip.shape[0], from_link)
    ext[ext.shape[0] - 1] = jnp.zeros(ext.shape[1:], BF16)
    for e in range(count):
        r[e] = b[e] - x[e] + coupled(positions, e, couple[e], ext)
    pack(own, [r[e] for e in range(count)])
    ext[:count] = r[...].astype(BF16)
    ext[count] = jnp.zeros(ext.shape[1:], BF16)
    pack(to_chip, listed(lists, 0, ext))


def extend(ext, mine, theirs):
    unpack(ext, 0, mine)
    unpack(ext, PACK * mine.shape[0], theirs)
    ext[ext.shape[0] - 1] = jnp.zeros(ext.shape[1:], BF16)


def power_kernel(table, couple, extra, mine, theirs, power, message, ext):
    count, slots = couple.shape[0], extra.shape[0]
    extend(ext, mine, theirs)
    values = []
    for e in range(count + slots):
        rows = couple[e] if e < count else extra[e - count, :DOF]
        values.append(coupled(table, e, rows, ext) * (1.0 / GROWTH))
        if e < count:
            power[e] = values[e]
    pack(message, values)


def inner_products(columns):
    stacked = jnp.concatenate(columns, axis=1)
    high, low = split(stacked)
    width = stacked.shape[1]
    sums = lax.dot_general(
        high, jnp.concatenate([high, low], axis=1), (((0,), (0,)), ((), ())), preferred_element_type=F32
    )
    cross = sums[:, width:]
    return sums[:, :width] + cross + cross.T


def gram_kernel(table, couple, mine, theirs, *refs):
    fields, (last, left, right, ext) = refs[:POWERS], refs[POWERS:]
    count = couple.shape[0]
    rows = count * DOF
    extend(ext, mine, theirs)
    for e in range(count):
        last[e] = coupled(table, e, couple[e], ext) * (1.0 / GROWTH)
    fields = [field[...].reshape(rows, RHS) for field in (*fields, last)]
    empty = jnp.zeros((rows, RHS), F32)
    gram = inner_products([fields[k] - GROWTH * fields[k + 1] for k in range(POWERS)] + [fields[0], empty])
    norms = jnp.concatenate(
        [jnp.sum(field * field, axis=0, keepdims=True) for field in fields] + [jnp.zeros((1, RHS), F32)], axis=0
    )
    half = gram.shape[0] // 2
    below = jnp.concatenate([jnp.zeros((RHS, half), F32), gram[half:, half:][: half - RHS]], axis=0)
    left[...] = jnp.where(block_of(half, 0) > block_of(half, 1), below, gram[:half, :half])
    right[...] = gram[:half, half:]
    right[: POWERS + 2, half - RHS :] = norms


def block_of(size, dimension):
    return lax.broadcasted_iota(jnp.int32, (size, size), dimension) // RHS


def unpack_gram(left, right):
    half = left.shape[0]
    low_left, right = left[...], right[...]
    row, column = block_of(half, 0), block_of(half, 1)
    norms = jnp.concatenate([right[j : j + 1, half - RHS :] for j in range(POWERS + 2)], axis=1)
    right = jnp.where(column < 3, right, 0.0)
    first = jnp.where(row <= column, low_left, low_left.T)
    moved = jnp.concatenate([low_left[RHS:], jnp.zeros((RHS, half), F32)], axis=0)
    last = jnp.where(row >= column, moved, moved.T)
    last = jnp.where((row < 3) & (column < 3), last, 0.0)
    gram = jnp.concatenate(
        [jnp.concatenate([first, right], axis=1), jnp.concatenate([right.T, last], axis=1)], axis=0
    )
    return gram, norms


def eliminate(gram):
    count = SSTEP * RHS // 8
    groups = [gram[8 * g : 8 * g + 8, :] for g in range(count)]
    shape = groups[0].shape
    row_ids = lax.broadcasted_iota(jnp.int32, shape, 0)
    lane_ids = lax.broadcasted_iota(jnp.int32, (1, shape[1]), 1)
    pivots = jnp.zeros((1, shape[1]), F32)
    for home in range(count):
        columns = [
            [jnp.broadcast_to(group[:, 8 * home + m : 8 * home + m + 1], shape) for m in range(8)]
            for group in groups
        ]
        own = list(columns[home])
        panel = groups[home]
        for m in range(8):
            pivot = own[m][m : m + 1, :]
            pivots = jnp.where(lane_ids == 8 * home + m, pivot, pivots)
            inverse = 1.0 / pivot
            scaled = panel[m : m + 1, :] * inverse
            panel = jnp.where(row_ids == m, scaled, panel - own[m] * scaled)
            for k in range(m + 1, 8):
                scaled = own[k][m : m + 1, :] * inverse
                own[k] = jnp.where(row_ids == m, scaled, own[k] - own[m] * scaled)
        for g in range(count):
            if g == home:
                groups[g] = panel
                continue
            for m in range(8):
                groups[g] = groups[g] - columns[g][m] * panel[m : m + 1, :]
    return jnp.concatenate(groups, axis=0)[:, SSTEP * RHS :], pivots


def exact(a, b, contract=(1, 0)):
    return lax.dot_general(
        a,
        b,
        (((contract[0],), (contract[1],)), ((), ())),
        precision=lax.Precision.HIGHEST,
        preferred_element_type=F32,
    )


def below(value, size, blocks):
    parts = [jnp.zeros((RHS * blocks, value.shape[1]), F32)] if blocks else []
    rest = size - RHS * blocks - value.shape[0]
    parts.append(value)
    if rest:
        parts.append(jnp.zeros((rest, value.shape[1]), F32))
    return jnp.concatenate(parts, axis=0)


def weighted(weights, rows):
    return jnp.dot(weights.astype(BF16), rows.astype(BF16), preferred_element_type=F32)


def mixing(left, right):
    gram, norms = unpack_gram(left, right)
    size = gram.shape[0]
    right = RHS * POWERS
    square = SSTEP * RHS
    eye = (
        lax.broadcasted_iota(jnp.int32, (RHS, RHS), 0) == lax.broadcasted_iota(jnp.int32, (RHS, RHS), 1)
    ).astype(F32)

    first, _ = eliminate(jnp.concatenate([gram[:square, :square], gram[:square, right : right + RHS]], axis=1))
    first_left = GROWTH * below(first, square + RHS, 1) - below(first, square + RHS, 0) + below(eye, square + RHS, 0)
    moved = jnp.concatenate([below(first_left, size, k) for k in range(SSTEP)], axis=1)
    images = jnp.concatenate([moved, below(eye, size, POWERS) - below(first, size, 0)], axis=1)
    projected = exact(images, exact(gram, images), (0, 0))
    second, pivots = eliminate(projected)
    change = exact(moved, second)
    sol = below(first, size, 0) + change
    res = below(first_left, size, 0) - change + GROWTH * below(change[: size - RHS], size, 1)
    half = size // 2
    is_diagonal = lax.broadcasted_iota(jnp.int32, (half, half), 0) == lax.broadcasted_iota(jnp.int32, (half, half), 1)
    diagonal = jnp.concatenate(
        [
            jnp.sum(jnp.where(is_diagonal, block, 0.0), axis=0, keepdims=True)
            for block in (gram[:half, :half], gram[half:, half:])
        ],
        axis=1,
    )
    reach = weighted(jnp.sqrt(diagonal), jnp.abs(images))
    reach = reach * reach
    corner = jnp.where(eye > 0, projected[square:, square:], 0.0)
    left_over = jnp.sum(corner, axis=0, keepdims=True) - jnp.sum(
        projected[:square, square:] * second, axis=0, keepdims=True
    )
    power = (lax.broadcasted_iota(jnp.int32, (1, size), 1) // RHS).astype(F32)
    rounding = weighted(norms * power, res * res)
    doubts = [
        jnp.where(reach[:, :square] <= TRUST_PIVOT * pivots[:, :square], 0.0, 1.0),
        jnp.where(reach[:, square:] <= TRUST_RESIDUAL * left_over, 0.0, 1.0),
        jnp.where(jnp.sum(rounding, axis=1, keepdims=True) <= TRUST_ROUNDING * jnp.sum(left_over, axis=1, keepdims=True), 0.0, 1.0),
    ]
    doubt = sum(jnp.sum(value, axis=1, keepdims=True) for value in doubts)
    return jnp.concatenate([sol, res], axis=1), doubt


def stack_kernel(*refs):
    fields, (high, low) = refs[:-2], refs[-2:]
    rows = fields[0].shape[0] * DOF
    columns = [field[...].reshape(rows, RHS) for field in fields]
    rest = high.shape[1] - RHS * len(fields)
    if rest:
        columns.append(jnp.zeros((rows, rest), F32))
    high[...], low[...] = split(jnp.concatenate(columns, axis=1))


def combined(mix, high, low, shape):
    mix_high, mix_low = split(mix)
    width = mix.shape[1]
    out = jnp.dot(high[...], jnp.concatenate([mix_high, mix_low], axis=1), preferred_element_type=F32)
    out = out[:, :width] + out[:, width:] + jnp.dot(low[...], mix_high, preferred_element_type=F32)
    return out[:, :RHS].reshape(shape), out[:, RHS:].reshape(shape)


def update_kernel(lists, left, right, high, low, x, new_x, r, own, to_chip, doubt, ext):
    count = x.shape[0]
    mix, found = mixing(left, right)
    doubt[...] = jnp.broadcast_to(found, doubt.shape)
    step, r[...] = combined(mix, high, low, x.shape)
    new_x[...] = x[...] + step
    pack(own, [r[e] for e in range(count)])
    ext[:count] = r[...].astype(BF16)
    ext[count] = jnp.zeros(ext.shape[1:], BF16)
    pack(to_chip, listed(lists, 0, ext))


def finish_kernel(left, right, high, low, x, earlier, first_r, first_x, new_x, r, repeats):
    mix, found = mixing(left, right)
    found = found + earlier[:1, :1]
    repeats[0] = jnp.where(found[0, 0] == 0, 0, CYCLES)
    step, last = combined(mix, high, low, x.shape)
    trusted = (found == 0).reshape(1, 1, 1)
    new_x[...] = jnp.where(trusted, x[...] + step, first_x[...]).reshape(new_x.shape)
    r[...] = jnp.where(trusted, last, first_r[...]).reshape(r.shape)


def single_power_kernel(codes, couple, value, from_chip, from_link, power, ext):
    count = value.shape[0]
    ext[:count] = value[...].astype(BF16)
    unpack(ext, count, from_chip)
    unpack(ext, count + PACK * from_chip.shape[0], from_link)
    ext[ext.shape[0] - 1] = jnp.zeros(ext.shape[1:], BF16)
    for e in range(count):
        power[e] = coupled(codes, e, couple[e], ext)


def single_gram_kernel(*refs):
    fields, gram = refs[:-1], refs[-1]
    fields = [field[...].reshape(-1, RHS) for field in fields]
    gram[...] = inner_products([fields[k] - fields[k + 1] for k in range(SSTEP)] + [fields[0]])


def single_update_kernel(gram, high, low, x, new_x, r):
    first, _ = eliminate(gram)
    size = gram.shape[0]
    eye = (
        lax.broadcasted_iota(jnp.int32, (RHS, RHS), 0) == lax.broadcasted_iota(jnp.int32, (RHS, RHS), 1)
    ).astype(F32)
    res = below(eye, size, 0) - below(first, size, 0) + below(first, size, 1)
    step, r[...] = combined(jnp.concatenate([below(first, size, 0), res], axis=1), high, low, x.shape)
    new_x[...] = x[...] + step


def shards(right_side, first_guess, couple, send_lists, neighbours):
    count = right_side.shape[0]
    slots = send_lists.shape[2]
    devices = lax.axis_size(AXES)
    assert lax.axis_size("sub") == 2 and slots % PACK == 0 and count % PACK == 0
    second = lax.axis_index("sub") == 1

    def shape(dtype, *sizes):
        return jax.ShapeDtypeStruct(sizes, dtype)

    field = shape(F32, count, DOF, RHS)
    slot_message = shape(BF16, slots // PACK, DOF, PACK * RHS)
    own_message = shape(BF16, count // PACK, DOF, PACK * RHS)
    message = shape(BF16, (count + slots) // PACK, DOF, PACK * RHS)
    rows_shape = shape(BF16, count, DOF, FACES * DOF)
    row_message = shape(BF16, slots, DOF + META, FACES * DOF)
    half_gram = shape(F32, (POWERS + 2) * RHS // 2, (POWERS + 2) * RHS // 2)
    doubt_shape = shape(F32, 8, LANES)
    table_shape = shape(jnp.int32, count + slots, LANES)

    def call(kernel, outs, specs, name, blocks=0, last=VMEM, scratch=()):
        return pl.pallas_call(
            kernel,
            out_shape=outs,
            in_specs=specs,
            out_specs=[VMEM] * (len(outs) - 1) + [last],
            scratch_shapes=list(scratch) + ([pltpu.VMEM((blocks, DOF, RHS), BF16)] if blocks else []),
            compiler_params=PARAMS,
            name=name,
        )

    nowhere = count + 2 * slots
    own_lists = jnp.where(send_lists[0] < 0, count, send_lists[0]).astype(jnp.int32)
    lists = jnp.where(second, own_lists[::-1], own_lists).reshape(1, 2 * slots)
    swapped = jnp.where(neighbours < count + slots, neighbours + slots, neighbours - slots)
    codes = jnp.where(second | (neighbours < count), neighbours, swapped)
    codes = jnp.where(neighbours < 0, nowhere, codes).astype(jnp.int32)
    codes = jnp.pad(codes, ((0, 0), (0, LANES - FACES)))

    chip_pairs = [(d, d ^ 1) for d in range(devices)]
    link_pairs = [(d, d + 1 if d % 2 else d - 1) for d in range(devices)]
    link_pairs = [(s, t) for s, t in link_pairs if 0 <= t < devices]

    def chip(value):
        return lax.ppermute(value, AXES, chip_pairs)

    def link(value):
        return lax.ppermute(value, AXES, link_pairs)

    def total(left, right):
        value = jnp.where(second, right, left) + chip(jnp.where(second, left, right))
        steps = [1 << k for k in range(1, devices.bit_length() - 1)]
        for first_step, second_step in zip(steps, steps[1:] + steps[:1]):
            pairs = [(d, d ^ (second_step if d % 2 else first_step)) for d in range(devices)]
            value = value + lax.ppermute(value, AXES, pairs)
        other = chip(value)
        return jnp.where(second, other, value), jnp.where(second, value, other)

    start = call(start_kernel, [slot_message] * 2, [VMEM, VMEM], "start", count + 1)
    prepare = call(
        first_kernel,
        [field, rows_shape, slot_message, slot_message],
        [ANY] * 3,
        "prepare",
        scratch=[
            pltpu.VMEM(send_lists.shape, jnp.int32),
            pltpu.VMEM(first_guess.shape, F32),
            pltpu.VMEM((count + 1, DOF, RHS), BF16),
            pltpu.SemaphoreType.DMA((3,)),
        ],
    )
    send_rows = call(rows_kernel, [row_message] * 2, [VMEM] * 3, "rows")
    tables = call(tables_kernel, [table_shape] * 2, [VMEM] * 4, "tables")
    first = call(
        residual_kernel,
        [field, own_message, slot_message],
        [VMEM] * 7,
        "first_residual",
        nowhere + 1,
    )
    reach = 2 * (count + slots) + 1
    power = call(power_kernel, [field, message], [VMEM] * 5, "power", reach)
    gram = call(
        gram_kernel, [field, half_gram, half_gram], [VMEM] * (4 + POWERS), "power_and_gram", reach
    )
    def stacked(fields):
        width = -(-len(fields) * RHS // LANES) * LANES
        parts = [shape(BF16, count * DOF, width)] * 2
        return call(stack_kernel, parts, [VMEM] * len(fields), "stack")(*fields)

    update = call(
        update_kernel,
        [field, field, own_message, slot_message, doubt_shape],
        [VMEM] * 6,
        "solve_update",
        count + 1,
    )
    flat = shape(F32, *right_side.shape)
    finish = call(finish_kernel, [flat, flat, shape(jnp.int32, 1)], [VMEM] * 8, "solve_finish", last=SMEM)

    b = right_side.reshape(count, DOF, RHS)
    assert CYCLES == 2 * MERGED
    first_x, kept, forward, backward = prepare(
        *(pltpu.with_memory_space_constraint(value, pltpu.HBM) for value in (send_lists, first_guess, couple))
    )
    to_chip = jnp.where(second, backward, forward)
    to_link = jnp.where(second, forward, backward)
    x = first_x
    from_link = link(to_link)
    from_chip = chip(to_chip)
    chip_rows, link_rows = send_rows(lists, codes, kept)
    link_rows = link(link_rows)
    chip_rows = chip(chip_rows)
    r, own, to_chip = first(lists, codes, kept, from_chip, from_link, b, x)
    chip_table, link_table = tables(lists, codes, chip_rows, link_rows)
    for group in range(CYCLES // MERGED):
        mine = jnp.concatenate([own, chip(to_chip)], axis=0)
        fields = [r]
        for k in range(POWERS - 1):
            if k % 2 == 0:
                value, mine = power(link_table, kept, link_rows, mine, link(mine))
            else:
                value, mine = power(chip_table, kept, chip_rows, mine, chip(mine))
            fields.append(value)
        value, left, right = gram(chip_table, kept, mine, chip(mine), *fields)
        fields.append(value)
        sums = total(left, right)
        if group == 0:
            first_r = r
        if group + 1 < CYCLES // MERGED:
            x, r, own, to_chip, doubt = update(lists, *sums, *stacked(fields), x)
        else:
            x, r, repeats = finish(*sums, *stacked(fields), x, doubt, first_r, first_x)

    single_power = call(single_power_kernel, [field], [VMEM] * 5, "single_power", nowhere + 1)
    single_gram = call(single_gram_kernel, [shape(F32, LANES, LANES)], [VMEM] * (SSTEP + 1), "single_gram")
    single_update = call(single_update_kernel, [field, field], [VMEM] * 4, "single_update")

    def slots_of(value):
        to_chip, to_link = start(lists, value)
        return chip(to_chip), link(to_link)

    def one_cycle(_, state):
        x, r = (value.reshape(count, DOF, RHS) for value in state)
        fields = [r]
        for _ in range(SSTEP):
            fields += single_power(codes, couple, fields[-1], *slots_of(fields[-1]))
        (value,) = single_gram(*fields)
        step = 1
        while step < devices:
            value = value + lax.ppermute(value, AXES, [(d, d ^ step) for d in range(devices)])
            step *= 2
        x, r = single_update(value, *stacked(fields), x)
        return x.reshape(right_side.shape), r.reshape(right_side.shape)

    return lax.fori_loop(0, repeats[0], one_cycle, (x, r))


def solution(mesh):
    rows = ("grp", "leaf", "sub")
    placed = (P(rows, None), P(rows, None), P(rows, None, None), P(rows, None, None), P(rows, None))
    return jax.shard_map(
        shards,
        mesh=mesh,
        in_specs=placed,
        out_specs=(P(rows, None), P(rows, None)),
        check_vma=False,
    )
```

```python
import jax
import jax.numpy as jnp
from jax import lax
from jax.experimental import pallas as pl
from jax.experimental.pallas import tpu as pltpu
from jax.sharding import PartitionSpec as P

DOF = 64
FACES = 6
RHS = 32
SSTEP = 3
CYCLES = 4
MERGED = 2
POWERS = SSTEP * MERGED
GROWTH = 8.0
PACK = 4
TRUST_PIVOT = 1e3
TRUST_RESIDUAL = 5e4
TRUST_ROUNDING = 64.0
META = 16
LANES = 128
AXES = ("leaf", "sub")
F32 = jnp.float32
BF16 = jnp.bfloat16

VMEM = pl.BlockSpec(memory_space=pltpu.VMEM)
SMEM = pl.BlockSpec(memory_space=pltpu.SMEM)
ANY = pl.BlockSpec(memory_space=pl.ANY)
PARAMS = pltpu.CompilerParams(vmem_limit_bytes=16 * 1024 * 1024)


def pack(message, blocks):
    for g in range(len(blocks) // PACK):
        message[g] = jnp.concatenate(blocks[PACK * g : PACK * g + PACK], axis=1).astype(BF16)


def unpack(ext, start, message):
    for g in range(message.shape[0]):
        row = message[g]
        for j in range(PACK):
            ext[start + PACK * g + j] = row[:, RHS * j : RHS * j + RHS]


def coupled(table, e, rows, ext):
    gathered = jnp.concatenate([ext[table[e, f]] for f in range(FACES)], axis=0)
    return jnp.dot(rows, gathered, preferred_element_type=F32)


def split(value):
    high = value.astype(BF16)
    return high, (value - high.astype(F32)).astype(BF16)


def listed(lists, side, ext):
    slots = lists.shape[1] // 2
    return [ext[lists[0, side * slots + s]].astype(F32) for s in range(slots)]


def first_kernel(send_lists, guess, couple, x, kept, forward, backward, lists, flat, ext, sems):
    copies = [
        pltpu.make_async_copy(source, target, sems.at[k])
        for k, (source, target) in enumerate(((send_lists, lists), (guess, flat), (couple, kept)))
    ]
    for copy in copies:
        copy.start()
    count = x.shape[0]
    ext[count] = jnp.zeros(ext.shape[1:], BF16)
    copies[1].wait()
    x[...] = flat[...].reshape(x.shape)
    ext[:count] = x[...].astype(BF16)
    copies[0].wait()
    for side, message in ((0, forward), (1, backward)):
        places = [lists[0, side, s] for s in range(lists.shape[2])]
        pack(message, [ext[jnp.where(place < 0, count, place)].astype(F32) for place in places])
    copies[2].wait()


def start_kernel(lists, x, to_chip, to_link, ext):
    count = x.shape[0]
    ext[:count] = x[...].astype(BF16)
    ext[count] = jnp.zeros(ext.shape[1:], BF16)
    pack(to_chip, listed(lists, 0, ext))
    pack(to_link, listed(lists, 1, ext))


def rows_kernel(lists, codes, couple, to_chip, to_link):
    count, slots = couple.shape[0], to_chip.shape[0]
    lanes = lax.broadcasted_iota(jnp.int32, (1, LANES), 1)
    for side, message in ((0, to_chip), (1, to_link)):
        for s in range(slots):
            place = lists[0, side * slots + s]
            e = jnp.minimum(place, count - 1)
            message[s, :DOF] = couple[e]
            meta = jnp.where(place < count, codes[pl.ds(e, 1), :], count + 2 * slots)
            meta = jnp.where(lanes == FACES, place, meta).astype(F32)
            message[s, DOF:] = jnp.zeros((META, couple.shape[2]), BF16)
            message[s, DOF:, :LANES] = jnp.broadcast_to(meta, (META, LANES)).astype(BF16)


def tables_kernel(lists, codes, chip_rows, link_rows, chip_table, link_table):
    count, slots = codes.shape[0], chip_rows.shape[0]
    reach = count + slots
    chip_base, link_base, empty = count, count + slots, 2 * reach
    sides = ((0, chip_table, chip_rows, link_base, chip_base), (1, link_table, link_rows, chip_base, link_base))
    for side, table, rows, known_base, far_base in sides:
        meta = [rows[s, DOF:, :LANES].astype(F32)[:1].astype(jnp.int32) for s in range(slots)]
        far = [value[:, FACES : FACES + 1] for value in meta]
        near = [lists[:, side * slots + s : side * slots + s + 1] for s in range(slots)]

        def place(at, own, known, listed_at, listed_own):
            found = jnp.where((at >= known_base) & (at < known_base + slots), at - known_base + known, empty)
            for s in range(slots):
                target = jnp.where(listed_at[s] < count, listed_at[s] + listed_own, empty)
                found = jnp.where(at == far_base + s, target, found)
            return jnp.where(at < count, at + own, found)

        table[:count] = place(codes[...], 0, count, far, reach)
        for s in range(slots):
            table[count + s : count + s + 1] = place(meta[s], reach, reach + count, near, 0)


def residual_kernel(lists, positions, couple, from_chip, from_link, b, x, r, blocks, own, to_chip, ext):
    count = x.shape[0]
    ext[:count] = x[...].astype(BF16)
    unpack(ext, count, from_chip)
    unpack(ext, count + PACK * from_chip.shape[0], from_link)
    ext[ext.shape[0] - 1] = jnp.zeros(ext.shape[1:], BF16)
    for e in range(count):
        r[e] = b[e] - x[e] + coupled(positions, e, couple[e], ext)
    pack(own, [r[e] for e in range(count)])
    blocks[...] = r[...].astype(BF16)
    ext[:count] = blocks[...]
    ext[count] = jnp.zeros(ext.shape[1:], BF16)
    pack(to_chip, listed(lists, 0, ext))


def extend(ext, blocks, mine, theirs):
    count = blocks.shape[0]
    ext[:count] = blocks[...]
    unpack(ext, count, mine.at[count // PACK :])
    unpack(ext, PACK * mine.shape[0], theirs)
    ext[ext.shape[0] - 1] = jnp.zeros(ext.shape[1:], BF16)


def power_kernel(table, couple, extra, blocks, mine, theirs, power, new_blocks, message, ext):
    count, slots = couple.shape[0], extra.shape[0]
    extend(ext, blocks, mine, theirs)
    values = []
    for e in range(count + slots):
        rows = couple[e] if e < count else extra[e - count, :DOF]
        values.append(coupled(table, e, rows, ext) * (1.0 / GROWTH))
        if e < count:
            power[e] = values[e]
            new_blocks[e] = values[e].astype(BF16)
    pack(message, values)


def inner_products(high, low):
    width = high.shape[1]
    sums = by_rows(high, jnp.concatenate([high, low], axis=1))
    cross = sums[:, width:]
    return sums[:, :width] + cross + cross.T


def squared_norms(fields):
    rows = [jnp.sum(field * field, axis=0, keepdims=True) for field in fields]
    return jnp.concatenate(rows + [jnp.zeros((8 - len(rows), RHS), F32)], axis=0)


def early_gram_kernel(*refs):
    fields, (high, low, gram, norms) = refs[:5], refs[5:]
    fields = [field[...].reshape(-1, RHS) for field in fields]
    columns = [fields[k] - GROWTH * fields[k + 1] for k in range(4)] + [fields[0]]
    stacked = jnp.concatenate(columns + [jnp.zeros((columns[0].shape[0], 3 * RHS), F32)], axis=1)
    high[...], low[...] = split(stacked)
    gram[...] = inner_products(high[...], low[...])
    norms[...] = squared_norms(fields)


def by_rows(a, b):
    return lax.dot_general(a, b, (((0,), (0,)), ((), ())), preferred_element_type=F32)


def gram_kernel(table, couple, blocks, mine, theirs, b4, b5, high, low, early, norms, last, left, right, ext):
    count = couple.shape[0]
    rows = count * DOF
    extend(ext, blocks, mine, theirs)
    for e in range(count):
        last[e] = coupled(table, e, couple[e], ext) * (1.0 / GROWTH)
    b4, b5, b6 = (field[...].reshape(rows, RHS) for field in (b4, b5, last))
    late_high, late_low = split(jnp.concatenate([b4 - GROWTH * b5, b5 - GROWTH * b6], axis=1))
    both = jnp.concatenate([late_high, late_low], axis=1)
    width = late_high.shape[1]
    cross = by_rows(both, high[...])
    cross = cross[:width] + cross[width:] + by_rows(late_high, low[...])
    own = by_rows(both, both)
    own = own[:width, :width] + own[:width, width:] + own[width:, :width]
    half = left.shape[0]
    with_r = cross[:, half : half + RHS]
    r_r = early[half : half + RHS, half : half + RHS]
    corner = jnp.concatenate(
        [jnp.concatenate([own, with_r], axis=1), jnp.concatenate([with_r.T, r_r], axis=1)], axis=0
    )
    corner = jnp.concatenate([corner, jnp.zeros((half - RHS, RHS), F32)], axis=1)
    below_diagonal = jnp.concatenate([jnp.zeros((RHS, half), F32), corner], axis=0)
    left[...] = jnp.where(block_of(half, 0) > block_of(half, 1), below_diagonal, early[:half, :half])
    right[...] = jnp.concatenate(
        [cross[:, :half].T, early[:half, half : half + RHS], jnp.zeros((half, RHS), F32)], axis=1
    )
    right[:8, half - RHS :] = jnp.concatenate([norms[:5], squared_norms([b5, b6])[:3]], axis=0)


def block_of(size, dimension):
    return lax.broadcasted_iota(jnp.int32, (size, size), dimension) // RHS


def unpack_gram(left, right):
    half = left.shape[0]
    low_left, right = left[...], right[...]
    row, column = block_of(half, 0), block_of(half, 1)
    norms = jnp.concatenate([right[j : j + 1, half - RHS :] for j in range(POWERS + 2)], axis=1)
    right = jnp.where(column < 3, right, 0.0)
    first = jnp.where(row <= column, low_left, low_left.T)
    moved = jnp.concatenate([low_left[RHS:], jnp.zeros((RHS, half), F32)], axis=0)
    last = jnp.where(row >= column, moved, moved.T)
    last = jnp.where((row < 3) & (column < 3), last, 0.0)
    gram = jnp.concatenate(
        [jnp.concatenate([first, right], axis=1), jnp.concatenate([right.T, last], axis=1)], axis=0
    )
    return gram, norms


def eliminate(gram):
    count = SSTEP * RHS // 8
    groups = [gram[8 * g : 8 * g + 8, :] for g in range(count)]
    shape = groups[0].shape
    row_ids = lax.broadcasted_iota(jnp.int32, shape, 0)
    lane_ids = lax.broadcasted_iota(jnp.int32, (1, shape[1]), 1)
    pivots = jnp.zeros((1, shape[1]), F32)
    for home in range(count):
        columns = [
            [jnp.broadcast_to(group[:, 8 * home + m : 8 * home + m + 1], shape) for m in range(8)]
            for group in groups
        ]
        own = list(columns[home])
        panel = groups[home]
        for m in range(8):
            pivot = own[m][m : m + 1, :]
            pivots = jnp.where(lane_ids == 8 * home + m, pivot, pivots)
            inverse = 1.0 / pivot
            scaled = panel[m : m + 1, :] * inverse
            panel = jnp.where(row_ids == m, scaled, panel - own[m] * scaled)
            for k in range(m + 1, 8):
                scaled = own[k][m : m + 1, :] * inverse
                own[k] = jnp.where(row_ids == m, scaled, own[k] - own[m] * scaled)
        for g in range(count):
            if g == home:
                groups[g] = panel
                continue
            for m in range(8):
                groups[g] = groups[g] - columns[g][m] * panel[m : m + 1, :]
    return jnp.concatenate(groups, axis=0)[:, SSTEP * RHS :], pivots


def exact(a, b, contract=(1, 0)):
    return lax.dot_general(
        a,
        b,
        (((contract[0],), (contract[1],)), ((), ())),
        precision=lax.Precision.HIGHEST,
        preferred_element_type=F32,
    )


def below(value, size, blocks):
    parts = [jnp.zeros((RHS * blocks, value.shape[1]), F32)] if blocks else []
    rest = size - RHS * blocks - value.shape[0]
    parts.append(value)
    if rest:
        parts.append(jnp.zeros((rest, value.shape[1]), F32))
    return jnp.concatenate(parts, axis=0)


def weighted(weights, rows):
    return jnp.dot(weights.astype(BF16), rows.astype(BF16), preferred_element_type=F32)


def mixing(left, right):
    gram, norms = unpack_gram(left, right)
    size = gram.shape[0]
    right = RHS * POWERS
    square = SSTEP * RHS
    eye = (
        lax.broadcasted_iota(jnp.int32, (RHS, RHS), 0) == lax.broadcasted_iota(jnp.int32, (RHS, RHS), 1)
    ).astype(F32)

    first, _ = eliminate(jnp.concatenate([gram[:square, :square], gram[:square, right : right + RHS]], axis=1))
    first_left = GROWTH * below(first, square + RHS, 1) - below(first, square + RHS, 0) + below(eye, square + RHS, 0)
    moved = jnp.concatenate([below(first_left, size, k) for k in range(SSTEP)], axis=1)
    images = jnp.concatenate([moved, below(eye, size, POWERS) - below(first, size, 0)], axis=1)
    projected = exact(images, exact(gram, images), (0, 0))
    second, pivots = eliminate(projected)
    change = exact(moved, second)
    sol = below(first, size, 0) + change
    res = below(first_left, size, 0) - change + GROWTH * below(change[: size - RHS], size, 1)
    half = size // 2
    is_diagonal = lax.broadcasted_iota(jnp.int32, (half, half), 0) == lax.broadcasted_iota(jnp.int32, (half, half), 1)
    diagonal = jnp.concatenate(
        [
            jnp.sum(jnp.where(is_diagonal, block, 0.0), axis=0, keepdims=True)
            for block in (gram[:half, :half], gram[half:, half:])
        ],
        axis=1,
    )
    reach = weighted(jnp.sqrt(diagonal), jnp.abs(images))
    reach = reach * reach
    corner = jnp.where(eye > 0, projected[square:, square:], 0.0)
    left_over = jnp.sum(corner, axis=0, keepdims=True) - jnp.sum(
        projected[:square, square:] * second, axis=0, keepdims=True
    )
    power = (lax.broadcasted_iota(jnp.int32, (1, size), 1) // RHS).astype(F32)
    rounding = weighted(norms * power, res * res)
    doubts = [
        jnp.where(reach[:, :square] <= TRUST_PIVOT * pivots[:, :square], 0.0, 1.0),
        jnp.where(reach[:, square:] <= TRUST_RESIDUAL * left_over, 0.0, 1.0),
        jnp.where(jnp.sum(rounding, axis=1, keepdims=True) <= TRUST_ROUNDING * jnp.sum(left_over, axis=1, keepdims=True), 0.0, 1.0),
    ]
    doubt = sum(jnp.sum(value, axis=1, keepdims=True) for value in doubts)
    return jnp.concatenate([sol, res], axis=1), doubt


def stack_kernel(*refs):
    fields, (high, low) = refs[:-2], refs[-2:]
    rows = fields[0].shape[0] * DOF
    columns = [field[...].reshape(rows, RHS) for field in fields]
    rest = high.shape[1] - RHS * len(fields)
    if rest:
        columns.append(jnp.zeros((rows, rest), F32))
    high[...], low[...] = split(jnp.concatenate(columns, axis=1))


def combined(mix, high, low, shape):
    mix_high, mix_low = split(mix)
    width = mix.shape[1]
    out = jnp.dot(high[...], jnp.concatenate([mix_high, mix_low], axis=1), preferred_element_type=F32)
    out = out[:, :width] + out[:, width:] + jnp.dot(low[...], mix_high, preferred_element_type=F32)
    return out[:, :RHS].reshape(shape), out[:, RHS:].reshape(shape)


def update_kernel(lists, left, right, high, low, x, new_x, r, blocks, own, to_chip, doubt, ext):
    count = x.shape[0]
    mix, found = mixing(left, right)
    doubt[...] = jnp.broadcast_to(found, doubt.shape)
    step, r[...] = combined(mix, high, low, x.shape)
    new_x[...] = x[...] + step
    pack(own, [r[e] for e in range(count)])
    blocks[...] = r[...].astype(BF16)
    ext[:count] = blocks[...]
    ext[count] = jnp.zeros(ext.shape[1:], BF16)
    pack(to_chip, listed(lists, 0, ext))


def finish_kernel(left, right, high, low, x, earlier, first_r, first_x, new_x, r, repeats):
    mix, found = mixing(left, right)
    found = found + earlier[:1, :1]
    repeats[0] = jnp.where(found[0, 0] == 0, 0, CYCLES)
    step, last = combined(mix, high, low, x.shape)
    trusted = (found == 0).reshape(1, 1, 1)
    new_x[...] = jnp.where(trusted, x[...] + step, first_x[...]).reshape(new_x.shape)
    r[...] = jnp.where(trusted, last, first_r[...]).reshape(r.shape)


def single_power_kernel(codes, couple, value, from_chip, from_link, power, ext):
    count = value.shape[0]
    ext[:count] = value[...].astype(BF16)
    unpack(ext, count, from_chip)
    unpack(ext, count + PACK * from_chip.shape[0], from_link)
    ext[ext.shape[0] - 1] = jnp.zeros(ext.shape[1:], BF16)
    for e in range(count):
        power[e] = coupled(codes, e, couple[e], ext)


def single_gram_kernel(*refs):
    fields, gram = refs[:-1], refs[-1]
    fields = [field[...].reshape(-1, RHS) for field in fields]
    columns = [fields[k] - fields[k + 1] for k in range(SSTEP)] + [fields[0]]
    gram[...] = inner_products(*split(jnp.concatenate(columns, axis=1)))


def single_update_kernel(gram, high, low, x, new_x, r):
    first, _ = eliminate(gram)
    size = gram.shape[0]
    eye = (
        lax.broadcasted_iota(jnp.int32, (RHS, RHS), 0) == lax.broadcasted_iota(jnp.int32, (RHS, RHS), 1)
    ).astype(F32)
    res = below(eye, size, 0) - below(first, size, 0) + below(first, size, 1)
    step, r[...] = combined(jnp.concatenate([below(first, size, 0), res], axis=1), high, low, x.shape)
    new_x[...] = x[...] + step


def shards(right_side, first_guess, couple, send_lists, neighbours):
    count = right_side.shape[0]
    slots = send_lists.shape[2]
    devices = lax.axis_size(AXES)
    assert lax.axis_size("sub") == 2 and slots % PACK == 0 and count % PACK == 0
    second = lax.axis_index("sub") == 1

    def shape(dtype, *sizes):
        return jax.ShapeDtypeStruct(sizes, dtype)

    field = shape(F32, count, DOF, RHS)
    blocks_shape = shape(BF16, count, DOF, RHS)
    slot_message = shape(BF16, slots // PACK, DOF, PACK * RHS)
    own_message = shape(BF16, count // PACK, DOF, PACK * RHS)
    message = shape(BF16, (count + slots) // PACK, DOF, PACK * RHS)
    rows_shape = shape(BF16, count, DOF, FACES * DOF)
    row_message = shape(BF16, slots, DOF + META, FACES * DOF)
    half_gram = shape(F32, (POWERS + 2) * RHS // 2, (POWERS + 2) * RHS // 2)
    doubt_shape = shape(F32, 8, LANES)
    table_shape = shape(jnp.int32, count + slots, LANES)

    def call(kernel, outs, specs, name, blocks=0, last=VMEM, scratch=()):
        return pl.pallas_call(
            kernel,
            out_shape=outs,
            in_specs=specs,
            out_specs=[VMEM] * (len(outs) - 1) + [last],
            scratch_shapes=list(scratch) + ([pltpu.VMEM((blocks, DOF, RHS), BF16)] if blocks else []),
            compiler_params=PARAMS,
            name=name,
        )

    nowhere = count + 2 * slots
    own_lists = jnp.where(send_lists[0] < 0, count, send_lists[0]).astype(jnp.int32)
    lists = jnp.where(second, own_lists[::-1], own_lists).reshape(1, 2 * slots)
    swapped = jnp.where(neighbours < count + slots, neighbours + slots, neighbours - slots)
    codes = jnp.where(second | (neighbours < count), neighbours, swapped)
    codes = jnp.where(neighbours < 0, nowhere, codes).astype(jnp.int32)
    codes = jnp.pad(codes, ((0, 0), (0, LANES - FACES)))

    chip_pairs = [(d, d ^ 1) for d in range(devices)]
    link_pairs = [(d, d + 1 if d % 2 else d - 1) for d in range(devices)]
    link_pairs = [(s, t) for s, t in link_pairs if 0 <= t < devices]

    def chip(value):
        return lax.ppermute(value, AXES, chip_pairs)

    def link(value):
        return lax.ppermute(value, AXES, link_pairs)

    def total(left, right):
        value = jnp.where(second, right, left) + chip(jnp.where(second, left, right))
        steps = [1 << k for k in range(1, devices.bit_length() - 1)]
        for first_step, second_step in zip(steps, steps[1:] + steps[:1]):
            pairs = [(d, d ^ (second_step if d % 2 else first_step)) for d in range(devices)]
            value = value + lax.ppermute(value, AXES, pairs)
        other = chip(value)
        return jnp.where(second, other, value), jnp.where(second, value, other)

    start = call(start_kernel, [slot_message] * 2, [VMEM, VMEM], "start", count + 1)
    prepare = call(
        first_kernel,
        [field, rows_shape, slot_message, slot_message],
        [ANY] * 3,
        "prepare",
        scratch=[
            pltpu.VMEM(send_lists.shape, jnp.int32),
            pltpu.VMEM(first_guess.shape, F32),
            pltpu.VMEM((count + 1, DOF, RHS), BF16),
            pltpu.SemaphoreType.DMA((3,)),
        ],
    )
    send_rows = call(rows_kernel, [row_message] * 2, [VMEM] * 3, "rows")
    tables = call(tables_kernel, [table_shape] * 2, [VMEM] * 4, "tables")
    first = call(
        residual_kernel,
        [field, blocks_shape, own_message, slot_message],
        [VMEM] * 7,
        "first_residual",
        nowhere + 1,
    )
    reach = 2 * (count + slots) + 1
    power = call(power_kernel, [field, blocks_shape, message], [VMEM] * 6, "power", reach)
    early_parts = [
        shape(BF16, count * DOF, 2 * LANES),
        shape(BF16, count * DOF, 2 * LANES),
        shape(F32, 2 * LANES, 2 * LANES),
        shape(F32, 8, RHS),
    ]
    early_gram = call(early_gram_kernel, early_parts, [VMEM] * 5, "early_gram")
    gram = call(gram_kernel, [field, half_gram, half_gram], [VMEM] * 11, "power_and_gram", reach)

    def stacked(fields):
        width = -(-len(fields) * RHS // LANES) * LANES
        parts = [shape(BF16, count * DOF, width)] * 2
        return call(stack_kernel, parts, [VMEM] * len(fields), "stack")(*fields)

    update = call(
        update_kernel,
        [field, field, blocks_shape, own_message, slot_message, doubt_shape],
        [VMEM] * 6,
        "solve_update",
        count + 1,
    )
    flat = shape(F32, *right_side.shape)
    finish = call(finish_kernel, [flat, flat, shape(jnp.int32, 1)], [VMEM] * 8, "solve_finish", last=SMEM)

    b = right_side.reshape(count, DOF, RHS)
    assert CYCLES == 2 * MERGED and POWERS == 6 and PACK * RHS == LANES
    first_x, kept, forward, backward = prepare(
        *(pltpu.with_memory_space_constraint(value, pltpu.HBM) for value in (send_lists, first_guess, couple))
    )
    to_chip = jnp.where(second, backward, forward)
    to_link = jnp.where(second, forward, backward)
    x = first_x
    from_link = link(to_link)
    from_chip = chip(to_chip)
    chip_rows, link_rows = send_rows(lists, codes, kept)
    link_rows = link(link_rows)
    chip_rows = chip(chip_rows)
    r, blocks, own, to_chip = first(lists, codes, kept, from_chip, from_link, b, x)
    chip_table, link_table = tables(lists, codes, chip_rows, link_rows)
    for group in range(CYCLES // MERGED):
        mine = jnp.concatenate([own, chip(to_chip)], axis=0)
        fields = [r]
        for k in range(POWERS - 1):
            if k % 2 == 0:
                value, blocks, mine = power(link_table, kept, link_rows, blocks, mine, link(mine))
            else:
                value, blocks, mine = power(chip_table, kept, chip_rows, blocks, mine, chip(mine))
            fields.append(value)
            if k == 3:
                early = early_gram(*fields)
        value, left, right = gram(chip_table, kept, blocks, mine, chip(mine), *fields[4:], *early)
        fields.append(value)
        sums = total(left, right)
        if group == 0:
            first_r = r
        if group + 1 < CYCLES // MERGED:
            x, r, blocks, own, to_chip, doubt = update(lists, *sums, *stacked(fields), x)
        else:
            x, r, repeats = finish(*sums, *stacked(fields), x, doubt, first_r, first_x)

    single_power = call(single_power_kernel, [field], [VMEM] * 5, "single_power", nowhere + 1)
    single_gram = call(single_gram_kernel, [shape(F32, LANES, LANES)], [VMEM] * (SSTEP + 1), "single_gram")
    single_update = call(single_update_kernel, [field, field], [VMEM] * 4, "single_update")

    def slots_of(value):
        to_chip, to_link = start(lists, value)
        return chip(to_chip), link(to_link)

    def one_cycle(_, state):
        x, r = (value.reshape(count, DOF, RHS) for value in state)
        fields = [r]
        for _ in range(SSTEP):
            fields += single_power(codes, couple, fields[-1], *slots_of(fields[-1]))
        (value,) = single_gram(*fields)
        step = 1
        while step < devices:
            value = value + lax.ppermute(value, AXES, [(d, d ^ step) for d in range(devices)])
            step *= 2
        x, r = single_update(value, *stacked(fields), x)
        return x.reshape(right_side.shape), r.reshape(right_side.shape)

    return lax.fori_loop(0, repeats[0], one_cycle, (x, r))


def solution(mesh):
    rows = ("grp", "leaf", "sub")
    placed = (P(rows, None), P(rows, None), P(rows, None, None), P(rows, None, None), P(rows, None))
    return jax.shard_map(
        shards,
        mesh=mesh,
        in_specs=placed,
        out_specs=(P(rows, None), P(rows, None)),
        check_vma=False,
    )
```

```python
import jax
import jax.numpy as jnp
from jax import lax
from jax.experimental import pallas as pl
from jax.experimental.pallas import tpu as pltpu
from jax.sharding import PartitionSpec as P

DOF = 64
FACES = 6
RHS = 32
SSTEP = 3
CYCLES = 4
MERGED = 2
POWERS = SSTEP * MERGED
GROWTH = 8.0
PACK = 4
TRUST_PIVOT = 1e3
TRUST_RESIDUAL = 5e4
TRUST_ROUNDING = 64.0
META = 16
LANES = 128
AXES = ("leaf", "sub")
F32 = jnp.float32
BF16 = jnp.bfloat16

VMEM = pl.BlockSpec(memory_space=pltpu.VMEM)
SMEM = pl.BlockSpec(memory_space=pltpu.SMEM)
ANY = pl.BlockSpec(memory_space=pl.ANY)
PARAMS = pltpu.CompilerParams(vmem_limit_bytes=16 * 1024 * 1024)


def pack(message, blocks):
    for g in range(len(blocks) // PACK):
        message[g] = jnp.concatenate(blocks[PACK * g : PACK * g + PACK], axis=1).astype(BF16)


def unpack(ext, start, message):
    for g in range(message.shape[0]):
        row = message[g]
        for j in range(PACK):
            ext[start + PACK * g + j] = row[:, RHS * j : RHS * j + RHS]


def coupled(table, e, rows, ext):
    gathered = jnp.concatenate([ext[table[e, f]] for f in range(FACES)], axis=0)
    return jnp.dot(rows, gathered, preferred_element_type=F32)


def split(value):
    high = value.astype(BF16)
    return high, (value - high.astype(F32)).astype(BF16)


def listed(lists, side, ext):
    slots = lists.shape[1] // 2
    return [ext[lists[0, side * slots + s]].astype(F32) for s in range(slots)]


def first_kernel(send_lists, guess, couple, x, kept, forward, backward, lists, flat, ext, sems):
    copies = [
        pltpu.make_async_copy(source, target, sems.at[k])
        for k, (source, target) in enumerate(((send_lists, lists), (guess, flat), (couple, kept)))
    ]
    for copy in copies:
        copy.start()
    count = x.shape[0]
    ext[count] = jnp.zeros(ext.shape[1:], BF16)
    copies[1].wait()
    x[...] = flat[...].reshape(x.shape)
    ext[:count] = x[...].astype(BF16)
    copies[0].wait()
    for side, message in ((0, forward), (1, backward)):
        places = [lists[0, side, s] for s in range(lists.shape[2])]
        pack(message, [ext[jnp.where(place < 0, count, place)].astype(F32) for place in places])
    copies[2].wait()


def start_kernel(lists, x, to_chip, to_link, ext):
    count = x.shape[0]
    ext[:count] = x[...].astype(BF16)
    ext[count] = jnp.zeros(ext.shape[1:], BF16)
    pack(to_chip, listed(lists, 0, ext))
    pack(to_link, listed(lists, 1, ext))


def rows_kernel(lists, codes, couple, to_chip, to_link):
    count, slots = couple.shape[0], to_chip.shape[0]
    lanes = lax.broadcasted_iota(jnp.int32, (1, LANES), 1)
    for side, message in ((0, to_chip), (1, to_link)):
        for s in range(slots):
            place = lists[0, side * slots + s]
            e = jnp.minimum(place, count - 1)
            message[s, :DOF] = couple[e]
            meta = jnp.where(place < count, codes[pl.ds(e, 1), :], count + 2 * slots)
            meta = jnp.where(lanes == FACES, place, meta).astype(F32)
            message[s, DOF:] = jnp.zeros((META, couple.shape[2]), BF16)
            message[s, DOF:, :LANES] = jnp.broadcast_to(meta, (META, LANES)).astype(BF16)


def tables_kernel(lists, codes, chip_rows, link_rows, chip_table, link_table):
    count, slots = codes.shape[0], chip_rows.shape[0]
    reach = count + slots
    chip_base, link_base, empty = count, count + slots, 2 * reach
    sides = ((0, chip_table, chip_rows, link_base, chip_base), (1, link_table, link_rows, chip_base, link_base))
    for side, table, rows, known_base, far_base in sides:
        meta = [rows[s, DOF:, :LANES].astype(F32)[:1].astype(jnp.int32) for s in range(slots)]
        far = [value[:, FACES : FACES + 1] for value in meta]
        near = [lists[:, side * slots + s : side * slots + s + 1] for s in range(slots)]

        def place(at, own, known, listed_at, listed_own):
            found = jnp.where((at >= known_base) & (at < known_base + slots), at - known_base + known, empty)
            for s in range(slots):
                target = jnp.where(listed_at[s] < count, listed_at[s] + listed_own, empty)
                found = jnp.where(at == far_base + s, target, found)
            return jnp.where(at < count, at + own, found)

        table[:count] = place(codes[...], 0, count, far, reach)
        for s in range(slots):
            table[count + s : count + s + 1] = place(meta[s], reach, reach + count, near, 0)


def residual_kernel(lists, positions, couple, from_chip, from_link, b, x, r, blocks, own, to_chip, ext):
    count = x.shape[0]
    ext[:count] = x[...].astype(BF16)
    unpack(ext, count, from_chip)
    unpack(ext, count + PACK * from_chip.shape[0], from_link)
    ext[ext.shape[0] - 1] = jnp.zeros(ext.shape[1:], BF16)
    for e in range(count):
        r[e] = b[e] - x[e] + coupled(positions, e, couple[e], ext)
    pack(own, [r[e] for e in range(count)])
    blocks[...] = r[...].astype(BF16)
    ext[:count] = blocks[...]
    ext[count] = jnp.zeros(ext.shape[1:], BF16)
    pack(to_chip, listed(lists, 0, ext))


def extend(ext, blocks, mine, theirs):
    count = blocks.shape[0]
    ext[:count] = blocks[...]
    unpack(ext, count, mine.at[count // PACK :])
    unpack(ext, PACK * mine.shape[0], theirs)
    ext[ext.shape[0] - 1] = jnp.zeros(ext.shape[1:], BF16)


def power_kernel(table, couple, extra, blocks, mine, theirs, power, new_blocks, message, ext):
    count, slots = couple.shape[0], extra.shape[0]
    extend(ext, blocks, mine, theirs)
    values = []
    for e in range(count + slots):
        rows = couple[e] if e < count else extra[e - count, :DOF]
        values.append(coupled(table, e, rows, ext) * (1.0 / GROWTH))
        if e < count:
            power[e] = values[e]
            new_blocks[e] = values[e].astype(BF16)
    pack(message, values)


def inner_products(high, low):
    width = high.shape[1]
    sums = by_rows(high, jnp.concatenate([high, low], axis=1))
    cross = sums[:, width:]
    return sums[:, :width] + cross + cross.T


def squared_norms(fields):
    rows = [jnp.sum(field * field, axis=0, keepdims=True) for field in fields]
    return jnp.concatenate(rows + [jnp.zeros((8 - len(rows), RHS), F32)], axis=0)


def early_gram_kernel(*refs):
    fields, (high, low, gram, norms) = refs[:5], refs[5:]
    fields = [field[...].reshape(-1, RHS) for field in fields]
    columns = [fields[k] - GROWTH * fields[k + 1] for k in range(4)] + [fields[0]]
    stacked = jnp.concatenate(columns + [jnp.zeros((columns[0].shape[0], 3 * RHS), F32)], axis=1)
    high[...], low[...] = split(stacked)
    gram[...] = inner_products(high[...], low[...])
    norms[...] = squared_norms(fields)


def by_rows(a, b):
    return lax.dot_general(a, b, (((0,), (0,)), ((), ())), preferred_element_type=F32)


def gram_kernel(table, couple, blocks, mine, theirs, b4, b5, high, low, early, norms, last, left, right, ext):
    count = couple.shape[0]
    rows = count * DOF
    extend(ext, blocks, mine, theirs)
    for e in range(count):
        last[e] = coupled(table, e, couple[e], ext) * (1.0 / GROWTH)
    b4, b5, b6 = (field[...].reshape(rows, RHS) for field in (b4, b5, last))
    late_high, late_low = split(jnp.concatenate([b4 - GROWTH * b5, b5 - GROWTH * b6], axis=1))
    both = jnp.concatenate([late_high, late_low], axis=1)
    width = late_high.shape[1]
    cross = by_rows(both, high[...])
    cross = cross[:width] + cross[width:] + by_rows(late_high, low[...])
    own = by_rows(both, both)
    own = own[:width, :width] + own[:width, width:] + own[width:, :width]
    half = left.shape[0]
    with_r = cross[:, half : half + RHS]
    r_r = early[half : half + RHS, half : half + RHS]
    corner = jnp.concatenate(
        [jnp.concatenate([own, with_r], axis=1), jnp.concatenate([with_r.T, r_r], axis=1)], axis=0
    )
    corner = jnp.concatenate([corner, jnp.zeros((half - RHS, RHS), F32)], axis=1)
    below_diagonal = jnp.concatenate([jnp.zeros((RHS, half), F32), corner], axis=0)
    left[...] = jnp.where(block_of(half, 0) > block_of(half, 1), below_diagonal, early[:half, :half])
    right[...] = jnp.concatenate(
        [cross[:, :half].T, early[:half, half : half + RHS], jnp.zeros((half, RHS), F32)], axis=1
    )
    right[:8, half - RHS :] = jnp.concatenate([norms[:5], squared_norms([b5, b6])[:3]], axis=0)


def block_of(size, dimension):
    return lax.broadcasted_iota(jnp.int32, (size, size), dimension) // RHS


def unpack_gram(left, right):
    half = left.shape[0]
    low_left, right = left[...], right[...]
    row, column = block_of(half, 0), block_of(half, 1)
    norms = jnp.concatenate([right[j : j + 1, half - RHS :] for j in range(POWERS + 2)], axis=1)
    right = jnp.where(column < 3, right, 0.0)
    first = jnp.where(row <= column, low_left, low_left.T)
    moved = jnp.concatenate([low_left[RHS:], jnp.zeros((RHS, half), F32)], axis=0)
    last = jnp.where(row >= column, moved, moved.T)
    last = jnp.where((row < 3) & (column < 3), last, 0.0)
    gram = jnp.concatenate(
        [jnp.concatenate([first, right], axis=1), jnp.concatenate([right.T, last], axis=1)], axis=0
    )
    return gram, norms


def eliminate(gram):
    count = SSTEP * RHS // 8
    groups = [gram[8 * g : 8 * g + 8, :] for g in range(count)]
    shape = groups[0].shape
    row_ids = lax.broadcasted_iota(jnp.int32, shape, 0)
    lane_ids = lax.broadcasted_iota(jnp.int32, (1, shape[1]), 1)
    pivots = jnp.zeros((1, shape[1]), F32)
    for home in range(count):
        columns = [
            [jnp.broadcast_to(group[:, 8 * home + m : 8 * home + m + 1], shape) for m in range(8)]
            for group in groups
        ]
        own = list(columns[home])
        panel = groups[home]
        for m in range(8):
            pivot = own[m][m : m + 1, :]
            pivots = jnp.where(lane_ids == 8 * home + m, pivot, pivots)
            inverse = 1.0 / pivot
            scaled = panel[m : m + 1, :] * inverse
            panel = jnp.where(row_ids == m, scaled, panel - own[m] * scaled)
            for k in range(m + 1, 8):
                scaled = own[k][m : m + 1, :] * inverse
                own[k] = jnp.where(row_ids == m, scaled, own[k] - own[m] * scaled)
        for g in range(count):
            if g == home:
                groups[g] = panel
                continue
            for m in range(8):
                groups[g] = groups[g] - columns[g][m] * panel[m : m + 1, :]
    return jnp.concatenate(groups, axis=0)[:, SSTEP * RHS :], pivots


def exact(a, b, contract=(1, 0)):
    return lax.dot_general(
        a,
        b,
        (((contract[0],), (contract[1],)), ((), ())),
        precision=lax.Precision.HIGHEST,
        preferred_element_type=F32,
    )


def below(value, size, blocks):
    parts = [jnp.zeros((RHS * blocks, value.shape[1]), F32)] if blocks else []
    rest = size - RHS * blocks - value.shape[0]
    parts.append(value)
    if rest:
        parts.append(jnp.zeros((rest, value.shape[1]), F32))
    return jnp.concatenate(parts, axis=0)


def weighted(weights, rows):
    return jnp.dot(weights.astype(BF16), rows.astype(BF16), preferred_element_type=F32)


def mixing(left, right):
    gram, norms = unpack_gram(left, right)
    size = gram.shape[0]
    right = RHS * POWERS
    square = SSTEP * RHS
    eye = (
        lax.broadcasted_iota(jnp.int32, (RHS, RHS), 0) == lax.broadcasted_iota(jnp.int32, (RHS, RHS), 1)
    ).astype(F32)

    first, _ = eliminate(jnp.concatenate([gram[:square, :square], gram[:square, right : right + RHS]], axis=1))
    first_left = GROWTH * below(first, square + RHS, 1) - below(first, square + RHS, 0) + below(eye, square + RHS, 0)
    moved = jnp.concatenate([below(first_left, size, k) for k in range(SSTEP)], axis=1)
    images = jnp.concatenate([moved, below(eye, size, POWERS) - below(first, size, 0)], axis=1)
    projected = exact(images, exact(gram, images), (0, 0))
    second, pivots = eliminate(projected)
    change = exact(moved, second)
    sol = below(first, size, 0) + change
    res = below(first_left, size, 0) - change + GROWTH * below(change[: size - RHS], size, 1)
    half = size // 2
    is_diagonal = lax.broadcasted_iota(jnp.int32, (half, half), 0) == lax.broadcasted_iota(jnp.int32, (half, half), 1)
    diagonal = jnp.concatenate(
        [
            jnp.sum(jnp.where(is_diagonal, block, 0.0), axis=0, keepdims=True)
            for block in (gram[:half, :half], gram[half:, half:])
        ],
        axis=1,
    )
    reach = weighted(jnp.sqrt(diagonal), jnp.abs(images))
    reach = reach * reach
    corner = jnp.where(eye > 0, projected[square:, square:], 0.0)
    left_over = jnp.sum(corner, axis=0, keepdims=True) - jnp.sum(
        projected[:square, square:] * second, axis=0, keepdims=True
    )
    power = (lax.broadcasted_iota(jnp.int32, (1, size), 1) // RHS).astype(F32)
    rounding = weighted(norms * power, res * res)
    doubts = [
        jnp.where(reach[:, :square] <= TRUST_PIVOT * pivots[:, :square], 0.0, 1.0),
        jnp.where(reach[:, square:] <= TRUST_RESIDUAL * left_over, 0.0, 1.0),
        jnp.where(jnp.sum(rounding, axis=1, keepdims=True) <= TRUST_ROUNDING * jnp.sum(left_over, axis=1, keepdims=True), 0.0, 1.0),
    ]
    doubt = sum(jnp.sum(value, axis=1, keepdims=True) for value in doubts)
    return jnp.concatenate([sol, res], axis=1), doubt


def stack_kernel(*refs):
    fields, (high, low) = refs[:-2], refs[-2:]
    rows = fields[0].shape[0] * DOF
    columns = [field[...].reshape(rows, RHS) for field in fields]
    rest = high.shape[1] - RHS * len(fields)
    if rest:
        columns.append(jnp.zeros((rows, rest), F32))
    high[...], low[...] = split(jnp.concatenate(columns, axis=1))


def times(mix_high, mix_low, high, low):
    width = mix_high.shape[1]
    out = jnp.dot(high, jnp.concatenate([mix_high, mix_low], axis=1), preferred_element_type=F32)
    return out[:, :width] + out[:, width:] + jnp.dot(low, mix_high, preferred_element_type=F32)


def combined(mix, high, low, shape):
    out = times(*split(mix), high[...], low[...])
    return out[:, :RHS].reshape(shape), out[:, RHS:].reshape(shape)


def mix_kernel(lists, left, right, high, low, mix_high, mix_low, to_chip, doubt):
    mix, found = mixing(left, right)
    doubt[...] = jnp.broadcast_to(found, doubt.shape)
    mix_high[...], mix_low[...] = split(mix)
    count, slots = high.shape[0] // DOF, lists.shape[1] // 2
    places = [lists[0, s] for s in range(slots)]
    starts = [pl.multiple_of(jnp.minimum(place, count - 1) * DOF, DOF) for place in places]
    rows = [jnp.concatenate([part[pl.ds(start, DOF), :] for start in starts], axis=0) for part in (high, low)]
    out = times(mix_high[...], mix_low[...], *rows)[:, RHS:]
    blocks = [out[DOF * s : DOF * s + DOF] for s in range(slots)]
    pack(to_chip, [jnp.where(place < count, block, 0.0) for place, block in zip(places, blocks)])


def update_kernel(mix_high, mix_low, high, low, x, new_x, r, blocks, own):
    out = times(mix_high[...], mix_low[...], high[...], low[...])
    new_x[...] = x[...] + out[:, :RHS].reshape(x.shape)
    r[...] = out[:, RHS:].reshape(x.shape)
    pack(own, [r[e] for e in range(x.shape[0])])
    blocks[...] = r[...].astype(BF16)


def finish_kernel(left, right, high, low, x, earlier, first_r, first_x, new_x, r, repeats):
    mix, found = mixing(left, right)
    found = found + earlier[:1, :1]
    repeats[0] = jnp.where(found[0, 0] == 0, 0, CYCLES)
    step, last = combined(mix, high, low, x.shape)
    trusted = (found == 0).reshape(1, 1, 1)
    new_x[...] = jnp.where(trusted, x[...] + step, first_x[...]).reshape(new_x.shape)
    r[...] = jnp.where(trusted, last, first_r[...]).reshape(r.shape)


def single_power_kernel(codes, couple, value, from_chip, from_link, power, ext):
    count = value.shape[0]
    ext[:count] = value[...].astype(BF16)
    unpack(ext, count, from_chip)
    unpack(ext, count + PACK * from_chip.shape[0], from_link)
    ext[ext.shape[0] - 1] = jnp.zeros(ext.shape[1:], BF16)
    for e in range(count):
        power[e] = coupled(codes, e, couple[e], ext)


def single_gram_kernel(*refs):
    fields, gram = refs[:-1], refs[-1]
    fields = [field[...].reshape(-1, RHS) for field in fields]
    columns = [fields[k] - fields[k + 1] for k in range(SSTEP)] + [fields[0]]
    gram[...] = inner_products(*split(jnp.concatenate(columns, axis=1)))


def single_update_kernel(gram, high, low, x, new_x, r):
    first, _ = eliminate(gram)
    size = gram.shape[0]
    eye = (
        lax.broadcasted_iota(jnp.int32, (RHS, RHS), 0) == lax.broadcasted_iota(jnp.int32, (RHS, RHS), 1)
    ).astype(F32)
    res = below(eye, size, 0) - below(first, size, 0) + below(first, size, 1)
    step, r[...] = combined(jnp.concatenate([below(first, size, 0), res], axis=1), high, low, x.shape)
    new_x[...] = x[...] + step


def shards(right_side, first_guess, couple, send_lists, neighbours):
    count = right_side.shape[0]
    slots = send_lists.shape[2]
    devices = lax.axis_size(AXES)
    assert lax.axis_size("sub") == 2 and slots % PACK == 0 and count % PACK == 0
    second = lax.axis_index("sub") == 1

    def shape(dtype, *sizes):
        return jax.ShapeDtypeStruct(sizes, dtype)

    field = shape(F32, count, DOF, RHS)
    blocks_shape = shape(BF16, count, DOF, RHS)
    slot_message = shape(BF16, slots // PACK, DOF, PACK * RHS)
    own_message = shape(BF16, count // PACK, DOF, PACK * RHS)
    message = shape(BF16, (count + slots) // PACK, DOF, PACK * RHS)
    rows_shape = shape(BF16, count, DOF, FACES * DOF)
    row_message = shape(BF16, slots, DOF + META, FACES * DOF)
    half_gram = shape(F32, (POWERS + 2) * RHS // 2, (POWERS + 2) * RHS // 2)
    doubt_shape = shape(F32, 8, LANES)
    table_shape = shape(jnp.int32, count + slots, LANES)

    def call(kernel, outs, specs, name, blocks=0, last=VMEM, scratch=()):
        return pl.pallas_call(
            kernel,
            out_shape=outs,
            in_specs=specs,
            out_specs=[VMEM] * (len(outs) - 1) + [last],
            scratch_shapes=list(scratch) + ([pltpu.VMEM((blocks, DOF, RHS), BF16)] if blocks else []),
            compiler_params=PARAMS,
            name=name,
        )

    nowhere = count + 2 * slots
    own_lists = jnp.where(send_lists[0] < 0, count, send_lists[0]).astype(jnp.int32)
    lists = jnp.where(second, own_lists[::-1], own_lists).reshape(1, 2 * slots)
    swapped = jnp.where(neighbours < count + slots, neighbours + slots, neighbours - slots)
    codes = jnp.where(second | (neighbours < count), neighbours, swapped)
    codes = jnp.where(neighbours < 0, nowhere, codes).astype(jnp.int32)
    codes = jnp.pad(codes, ((0, 0), (0, LANES - FACES)))

    chip_pairs = [(d, d ^ 1) for d in range(devices)]
    link_pairs = [(d, d + 1 if d % 2 else d - 1) for d in range(devices)]
    link_pairs = [(s, t) for s, t in link_pairs if 0 <= t < devices]

    def chip(value):
        return lax.ppermute(value, AXES, chip_pairs)

    def link(value):
        return lax.ppermute(value, AXES, link_pairs)

    def total(left, right):
        value = jnp.where(second, right, left) + chip(jnp.where(second, left, right))
        steps = [1 << k for k in range(1, devices.bit_length() - 1)]
        for first_step, second_step in zip(steps, steps[1:] + steps[:1]):
            pairs = [(d, d ^ (second_step if d % 2 else first_step)) for d in range(devices)]
            value = value + lax.ppermute(value, AXES, pairs)
        other = chip(value)
        return jnp.where(second, other, value), jnp.where(second, value, other)

    start = call(start_kernel, [slot_message] * 2, [VMEM, VMEM], "start", count + 1)
    prepare = call(
        first_kernel,
        [field, rows_shape, slot_message, slot_message],
        [ANY] * 3,
        "prepare",
        scratch=[
            pltpu.VMEM(send_lists.shape, jnp.int32),
            pltpu.VMEM(first_guess.shape, F32),
            pltpu.VMEM((count + 1, DOF, RHS), BF16),
            pltpu.SemaphoreType.DMA((3,)),
        ],
    )
    send_rows = call(rows_kernel, [row_message] * 2, [VMEM] * 3, "rows")
    tables = call(tables_kernel, [table_shape] * 2, [VMEM] * 4, "tables")
    first = call(
        residual_kernel,
        [field, blocks_shape, own_message, slot_message],
        [VMEM] * 7,
        "first_residual",
        nowhere + 1,
    )
    reach = 2 * (count + slots) + 1
    power = call(power_kernel, [field, blocks_shape, message], [VMEM] * 6, "power", reach)
    early_parts = [
        shape(BF16, count * DOF, 2 * LANES),
        shape(BF16, count * DOF, 2 * LANES),
        shape(F32, 2 * LANES, 2 * LANES),
        shape(F32, 8, RHS),
    ]
    early_gram = call(early_gram_kernel, early_parts, [VMEM] * 5, "early_gram")
    gram = call(gram_kernel, [field, half_gram, half_gram], [VMEM] * 11, "power_and_gram", reach)

    def stacked(fields):
        width = -(-len(fields) * RHS // LANES) * LANES
        parts = [shape(BF16, count * DOF, width)] * 2
        return call(stack_kernel, parts, [VMEM] * len(fields), "stack")(*fields)

    mix_shape = shape(BF16, (POWERS + 2) * RHS, 2 * RHS)
    mix = call(mix_kernel, [mix_shape, mix_shape, slot_message, doubt_shape], [VMEM] * 5, "solve")
    update = call(update_kernel, [field, field, blocks_shape, own_message], [VMEM] * 5, "update")
    flat = shape(F32, *right_side.shape)
    finish = call(finish_kernel, [flat, flat, shape(jnp.int32, 1)], [VMEM] * 8, "solve_finish", last=SMEM)

    b = right_side.reshape(count, DOF, RHS)
    assert CYCLES == 2 * MERGED and POWERS == 6 and PACK * RHS == LANES
    first_x, kept, forward, backward = prepare(
        *(pltpu.with_memory_space_constraint(value, pltpu.HBM) for value in (send_lists, first_guess, couple))
    )
    to_chip = jnp.where(second, backward, forward)
    to_link = jnp.where(second, forward, backward)
    x = first_x
    from_link = link(to_link)
    from_chip = chip(to_chip)
    chip_rows, link_rows = send_rows(lists, codes, kept)
    link_rows = link(link_rows)
    chip_rows = chip(chip_rows)
    r, blocks, own, to_chip = first(lists, codes, kept, from_chip, from_link, b, x)
    chip_table, link_table = tables(lists, codes, chip_rows, link_rows)
    for group in range(CYCLES // MERGED):
        mine = jnp.concatenate([own, chip(to_chip)], axis=0)
        fields = [r]
        for k in range(POWERS - 1):
            if k % 2 == 0:
                value, blocks, mine = power(link_table, kept, link_rows, blocks, mine, link(mine))
            else:
                value, blocks, mine = power(chip_table, kept, chip_rows, blocks, mine, chip(mine))
            fields.append(value)
            if k == 3:
                early = early_gram(*fields)
        value, left, right = gram(chip_table, kept, blocks, mine, chip(mine), *fields[4:], *early)
        fields.append(value)
        sums = total(left, right)
        if group == 0:
            first_r = r
        if group + 1 < CYCLES // MERGED:
            parts = stacked(fields)
            mix_high, mix_low, to_chip, doubt = mix(lists, *sums, *parts)
            x, r, blocks, own = update(mix_high, mix_low, *parts, x)
        else:
            x, r, repeats = finish(*sums, *stacked(fields), x, doubt, first_r, first_x)

    single_power = call(single_power_kernel, [field], [VMEM] * 5, "single_power", nowhere + 1)
    single_gram = call(single_gram_kernel, [shape(F32, LANES, LANES)], [VMEM] * (SSTEP + 1), "single_gram")
    single_update = call(single_update_kernel, [field, field], [VMEM] * 4, "single_update")

    def slots_of(value):
        to_chip, to_link = start(lists, value)
        return chip(to_chip), link(to_link)

    def one_cycle(_, state):
        x, r = (value.reshape(count, DOF, RHS) for value in state)
        fields = [r]
        for _ in range(SSTEP):
            fields += single_power(codes, couple, fields[-1], *slots_of(fields[-1]))
        (value,) = single_gram(*fields)
        step = 1
        while step < devices:
            value = value + lax.ppermute(value, AXES, [(d, d ^ step) for d in range(devices)])
            step *= 2
        x, r = single_update(value, *stacked(fields), x)
        return x.reshape(right_side.shape), r.reshape(right_side.shape)

    return lax.fori_loop(0, repeats[0], one_cycle, (x, r))


def solution(mesh):
    rows = ("grp", "leaf", "sub")
    placed = (P(rows, None), P(rows, None), P(rows, None, None), P(rows, None, None), P(rows, None))
    return jax.shard_map(
        shards,
        mesh=mesh,
        in_specs=placed,
        out_specs=(P(rows, None), P(rows, None)),
        check_vma=False,
    )
```

```python
import functools

import jax
import jax.numpy as jnp
from jax import lax
from jax.experimental import pallas as pl
from jax.experimental.pallas import tpu as pltpu
from jax.sharding import PartitionSpec as P

DOF = 64
FACES = 6
RHS = 32
SSTEP = 3
CYCLES = 4
MERGED = 2
POWERS = SSTEP * MERGED
GROWTH = 8.0
PACK = 4
TRUST_PIVOT = 1e3
TRUST_RESIDUAL = 5e4
TRUST_ROUNDING = 64.0
META = 16
LANES = 128
AXES = ("leaf", "sub")
F32 = jnp.float32
BF16 = jnp.bfloat16

VMEM = pl.BlockSpec(memory_space=pltpu.VMEM)
SMEM = pl.BlockSpec(memory_space=pltpu.SMEM)
ANY = pl.BlockSpec(memory_space=pl.ANY)
PARAMS = pltpu.CompilerParams(vmem_limit_bytes=16 * 1024 * 1024)


def pack(message, blocks):
    for g in range(len(blocks) // PACK):
        message[g] = jnp.concatenate(blocks[PACK * g : PACK * g + PACK], axis=1).astype(BF16)


def unpack(ext, start, message):
    for g in range(message.shape[0]):
        row = message[g]
        for j in range(PACK):
            ext[start + PACK * g + j] = row[:, RHS * j : RHS * j + RHS]


def coupled(table, e, rows, ext):
    gathered = jnp.concatenate([ext[table[e, f]] for f in range(FACES)], axis=0)
    return jnp.dot(rows, gathered, preferred_element_type=F32)


def split(value):
    high = value.astype(BF16)
    return high, (value - high.astype(F32)).astype(BF16)


def listed(lists, side, ext):
    slots = lists.shape[1] // 2
    return [ext[lists[0, side * slots + s]].astype(F32) for s in range(slots)]


def first_kernel(send_lists, guess, couple, x, kept, forward, backward, lists, flat, ext, sems):
    copies = [
        pltpu.make_async_copy(source, target, sems.at[k])
        for k, (source, target) in enumerate(((send_lists, lists), (guess, flat), (couple, kept)))
    ]
    for copy in copies:
        copy.start()
    count = x.shape[0]
    ext[count] = jnp.zeros(ext.shape[1:], BF16)
    copies[1].wait()
    x[...] = flat[...].reshape(x.shape)
    ext[:count] = x[...].astype(BF16)
    copies[0].wait()
    for side, message in ((0, forward), (1, backward)):
        places = [lists[0, side, s] for s in range(lists.shape[2])]
        pack(message, [ext[jnp.where(place < 0, count, place)].astype(F32) for place in places])
    copies[2].wait()


def start_kernel(lists, x, to_chip, to_link, ext):
    count = x.shape[0]
    ext[:count] = x[...].astype(BF16)
    ext[count] = jnp.zeros(ext.shape[1:], BF16)
    pack(to_chip, listed(lists, 0, ext))
    pack(to_link, listed(lists, 1, ext))


def rows_kernel(side, lists, codes, couple, after, message):
    count, slots = couple.shape[0], message.shape[0]
    lanes = lax.broadcasted_iota(jnp.int32, (1, LANES), 1)
    for s in range(slots):
        place = lists[0, side * slots + s]
        e = jnp.minimum(place, count - 1)
        message[s, :DOF] = couple[e]
        meta = jnp.where(place < count, codes[pl.ds(e, 1), :], count + 2 * slots)
        meta = jnp.where(lanes == FACES, place, meta).astype(F32)
        message[s, DOF:] = jnp.zeros((META, couple.shape[2]), BF16)
        message[s, DOF:, :LANES] = jnp.broadcast_to(meta, (META, LANES)).astype(BF16)


def table_kernel(side, lists, codes, rows, table):
    count, slots = codes.shape[0], rows.shape[0]
    reach = count + slots
    chip_base, link_base, empty = count, count + slots, 2 * reach
    known_base, far_base = (chip_base, link_base) if side else (link_base, chip_base)
    meta = [rows[s, DOF:, :LANES].astype(F32)[:1].astype(jnp.int32) for s in range(slots)]
    far = [value[:, FACES : FACES + 1] for value in meta]
    near = [lists[:, side * slots + s : side * slots + s + 1] for s in range(slots)]

    def place(at, own, known, listed_at, listed_own):
        found = jnp.where((at >= known_base) & (at < known_base + slots), at - known_base + known, empty)
        for s in range(slots):
            target = jnp.where(listed_at[s] < count, listed_at[s] + listed_own, empty)
            found = jnp.where(at == far_base + s, target, found)
        return jnp.where(at < count, at + own, found)

    table[:count] = place(codes[...], 0, count, far, reach)
    for s in range(slots):
        table[count + s : count + s + 1] = place(meta[s], reach, reach + count, near, 0)


def residual_kernel(lists, positions, couple, from_chip, from_link, b, x, r, blocks, own, to_chip, ext):
    count = x.shape[0]
    ext[:count] = x[...].astype(BF16)
    unpack(ext, count, from_chip)
    unpack(ext, count + PACK * from_chip.shape[0], from_link)
    ext[ext.shape[0] - 1] = jnp.zeros(ext.shape[1:], BF16)
    for e in range(count):
        r[e] = b[e] - x[e] + coupled(positions, e, couple[e], ext)
    pack(own, [r[e] for e in range(count)])
    blocks[...] = r[...].astype(BF16)
    ext[:count] = blocks[...]
    ext[count] = jnp.zeros(ext.shape[1:], BF16)
    pack(to_chip, listed(lists, 0, ext))


def extend(ext, blocks, mine, theirs):
    count = blocks.shape[0]
    ext[:count] = blocks[...]
    unpack(ext, count, mine.at[count // PACK :])
    unpack(ext, PACK * mine.shape[0], theirs)
    ext[ext.shape[0] - 1] = jnp.zeros(ext.shape[1:], BF16)


def power_kernel(table, couple, extra, blocks, mine, theirs, power, new_blocks, message, ext):
    count, slots = couple.shape[0], extra.shape[0]
    extend(ext, blocks, mine, theirs)
    values = []
    for e in range(count + slots):
        rows = couple[e] if e < count else extra[e - count, :DOF]
        values.append(coupled(table, e, rows, ext) * (1.0 / GROWTH))
        if e < count:
            power[e] = values[e]
            new_blocks[e] = values[e].astype(BF16)
    pack(message, values)


def inner_products(high, low):
    width = high.shape[1]
    sums = by_rows(high, jnp.concatenate([high, low], axis=1))
    cross = sums[:, width:]
    return sums[:, :width] + cross + cross.T


def squared_norms(fields):
    rows = [jnp.sum(field * field, axis=0, keepdims=True) for field in fields]
    return jnp.concatenate(rows + [jnp.zeros((8 - len(rows), RHS), F32)], axis=0)


def early_gram_kernel(*refs):
    fields, (high, low, gram, norms) = refs[:5], refs[5:]
    fields = [field[...].reshape(-1, RHS) for field in fields]
    columns = [fields[k] - GROWTH * fields[k + 1] for k in range(4)] + [fields[0]]
    stacked = jnp.concatenate(columns + [jnp.zeros((columns[0].shape[0], 3 * RHS), F32)], axis=1)
    high[...], low[...] = split(stacked)
    gram[...] = inner_products(high[...], low[...])
    norms[...] = squared_norms(fields)


def by_rows(a, b):
    return lax.dot_general(a, b, (((0,), (0,)), ((), ())), preferred_element_type=F32)


def gram_kernel(table, couple, blocks, mine, theirs, b4, b5, high, low, early, norms, last, left, right, ext):
    count = couple.shape[0]
    rows = count * DOF
    extend(ext, blocks, mine, theirs)
    for e in range(count):
        last[e] = coupled(table, e, couple[e], ext) * (1.0 / GROWTH)
    b4, b5, b6 = (field[...].reshape(rows, RHS) for field in (b4, b5, last))
    late_high, late_low = split(jnp.concatenate([b4 - GROWTH * b5, b5 - GROWTH * b6], axis=1))
    both = jnp.concatenate([late_high, late_low], axis=1)
    width = late_high.shape[1]
    cross = by_rows(both, high[...])
    cross = cross[:width] + cross[width:] + by_rows(late_high, low[...])
    own = by_rows(both, both)
    own = own[:width, :width] + own[:width, width:] + own[width:, :width]
    half = left.shape[0]
    with_r = cross[:, half : half + RHS]
    r_r = early[half : half + RHS, half : half + RHS]
    corner = jnp.concatenate(
        [jnp.concatenate([own, with_r], axis=1), jnp.concatenate([with_r.T, r_r], axis=1)], axis=0
    )
    corner = jnp.concatenate([corner, jnp.zeros((half - RHS, RHS), F32)], axis=1)
    below_diagonal = jnp.concatenate([jnp.zeros((RHS, half), F32), corner], axis=0)
    left[...] = jnp.where(block_of(half, 0) > block_of(half, 1), below_diagonal, early[:half, :half])
    right[...] = jnp.concatenate(
        [cross[:, :half].T, early[:half, half : half + RHS], jnp.zeros((half, RHS), F32)], axis=1
    )
    right[:8, half - RHS :] = jnp.concatenate([norms[:5], squared_norms([b5, b6])[:3]], axis=0)


def block_of(size, dimension):
    return lax.broadcasted_iota(jnp.int32, (size, size), dimension) // RHS


def unpack_gram(left, right):
    half = left.shape[0]
    low_left, right = left[...], right[...]
    row, column = block_of(half, 0), block_of(half, 1)
    norms = jnp.concatenate([right[j : j + 1, half - RHS :] for j in range(POWERS + 2)], axis=1)
    right = jnp.where(column < 3, right, 0.0)
    first = jnp.where(row <= column, low_left, low_left.T)
    moved = jnp.concatenate([low_left[RHS:], jnp.zeros((RHS, half), F32)], axis=0)
    last = jnp.where(row >= column, moved, moved.T)
    last = jnp.where((row < 3) & (column < 3), last, 0.0)
    gram = jnp.concatenate(
        [jnp.concatenate([first, right], axis=1), jnp.concatenate([right.T, last], axis=1)], axis=0
    )
    return gram, norms


def eliminate(gram):
    count = SSTEP * RHS // 8
    groups = [gram[8 * g : 8 * g + 8, :] for g in range(count)]
    shape = groups[0].shape
    row_ids = lax.broadcasted_iota(jnp.int32, shape, 0)
    lane_ids = lax.broadcasted_iota(jnp.int32, (1, shape[1]), 1)
    pivots = jnp.zeros((1, shape[1]), F32)
    for home in range(count):
        columns = [
            [jnp.broadcast_to(group[:, 8 * home + m : 8 * home + m + 1], shape) for m in range(8)]
            for group in groups
        ]
        own = list(columns[home])
        panel = groups[home]
        for m in range(8):
            pivot = own[m][m : m + 1, :]
            pivots = jnp.where(lane_ids == 8 * home + m, pivot, pivots)
            inverse = 1.0 / pivot
            scaled = panel[m : m + 1, :] * inverse
            panel = jnp.where(row_ids == m, scaled, panel - own[m] * scaled)
            for k in range(m + 1, 8):
                scaled = own[k][m : m + 1, :] * inverse
                own[k] = jnp.where(row_ids == m, scaled, own[k] - own[m] * scaled)
        for g in range(count):
            if g == home:
                groups[g] = panel
                continue
            for m in range(8):
                groups[g] = groups[g] - columns[g][m] * panel[m : m + 1, :]
    return jnp.concatenate(groups, axis=0)[:, SSTEP * RHS :], pivots


def exact(a, b, contract=(1, 0)):
    return lax.dot_general(
        a,
        b,
        (((contract[0],), (contract[1],)), ((), ())),
        precision=lax.Precision.HIGHEST,
        preferred_element_type=F32,
    )


def below(value, size, blocks):
    parts = [jnp.zeros((RHS * blocks, value.shape[1]), F32)] if blocks else []
    rest = size - RHS * blocks - value.shape[0]
    parts.append(value)
    if rest:
        parts.append(jnp.zeros((rest, value.shape[1]), F32))
    return jnp.concatenate(parts, axis=0)


def weighted(weights, rows):
    return jnp.dot(weights.astype(BF16), rows.astype(BF16), preferred_element_type=F32)


def mixing(left, right):
    gram, norms = unpack_gram(left, right)
    size = gram.shape[0]
    right = RHS * POWERS
    square = SSTEP * RHS
    eye = (
        lax.broadcasted_iota(jnp.int32, (RHS, RHS), 0) == lax.broadcasted_iota(jnp.int32, (RHS, RHS), 1)
    ).astype(F32)

    first, _ = eliminate(jnp.concatenate([gram[:square, :square], gram[:square, right : right + RHS]], axis=1))
    first_left = GROWTH * below(first, square + RHS, 1) - below(first, square + RHS, 0) + below(eye, square + RHS, 0)
    moved = jnp.concatenate([below(first_left, size, k) for k in range(SSTEP)], axis=1)
    images = jnp.concatenate([moved, below(eye, size, POWERS) - below(first, size, 0)], axis=1)
    projected = exact(images, exact(gram, images), (0, 0))
    second, pivots = eliminate(projected)
    change = exact(moved, second)
    sol = below(first, size, 0) + change
    res = below(first_left, size, 0) - change + GROWTH * below(change[: size - RHS], size, 1)
    half = size // 2
    is_diagonal = lax.broadcasted_iota(jnp.int32, (half, half), 0) == lax.broadcasted_iota(jnp.int32, (half, half), 1)
    diagonal = jnp.concatenate(
        [
            jnp.sum(jnp.where(is_diagonal, block, 0.0), axis=0, keepdims=True)
            for block in (gram[:half, :half], gram[half:, half:])
        ],
        axis=1,
    )
    reach = weighted(jnp.sqrt(diagonal), jnp.abs(images))
    reach = reach * reach
    corner = jnp.where(eye > 0, projected[square:, square:], 0.0)
    left_over = jnp.sum(corner, axis=0, keepdims=True) - jnp.sum(
        projected[:square, square:] * second, axis=0, keepdims=True
    )
    power = (lax.broadcasted_iota(jnp.int32, (1, size), 1) // RHS).astype(F32)
    rounding = weighted(norms * power, res * res)
    doubts = [
        jnp.where(reach[:, :square] <= TRUST_PIVOT * pivots[:, :square], 0.0, 1.0),
        jnp.where(reach[:, square:] <= TRUST_RESIDUAL * left_over, 0.0, 1.0),
        jnp.where(jnp.sum(rounding, axis=1, keepdims=True) <= TRUST_ROUNDING * jnp.sum(left_over, axis=1, keepdims=True), 0.0, 1.0),
    ]
    doubt = sum(jnp.sum(value, axis=1, keepdims=True) for value in doubts)
    return jnp.concatenate([sol, res], axis=1), doubt


def stack_kernel(*refs):
    fields, (high, low) = refs[:-2], refs[-2:]
    rows = fields[0].shape[0] * DOF
    columns = [field[...].reshape(rows, RHS) for field in fields]
    rest = high.shape[1] - RHS * len(fields)
    if rest:
        columns.append(jnp.zeros((rows, rest), F32))
    high[...], low[...] = split(jnp.concatenate(columns, axis=1))


def times(mix_high, mix_low, high, low):
    width = mix_high.shape[1]
    out = jnp.dot(high, jnp.concatenate([mix_high, mix_low], axis=1), preferred_element_type=F32)
    return out[:, :width] + out[:, width:] + jnp.dot(low, mix_high, preferred_element_type=F32)


def combined(mix, high, low, shape):
    out = times(*split(mix), high[...], low[...])
    return out[:, :RHS].reshape(shape), out[:, RHS:].reshape(shape)


def mix_kernel(lists, left, right, high, low, mix_high, mix_low, to_chip, doubt):
    mix, found = mixing(left, right)
    doubt[...] = jnp.broadcast_to(found, doubt.shape)
    mix_high[...], mix_low[...] = split(mix)
    count, slots = high.shape[0] // DOF, lists.shape[1] // 2
    places = [lists[0, s] for s in range(slots)]
    starts = [pl.multiple_of(jnp.minimum(place, count - 1) * DOF, DOF) for place in places]
    rows = [jnp.concatenate([part[pl.ds(start, DOF), :] for start in starts], axis=0) for part in (high, low)]
    out = times(mix_high[...], mix_low[...], *rows)[:, RHS:]
    blocks = [out[DOF * s : DOF * s + DOF] for s in range(slots)]
    pack(to_chip, [jnp.where(place < count, block, 0.0) for place, block in zip(places, blocks)])


def update_kernel(mix_high, mix_low, high, low, x, new_x, r, blocks, own):
    out = times(mix_high[...], mix_low[...], high[...], low[...])
    new_x[...] = x[...] + out[:, :RHS].reshape(x.shape)
    r[...] = out[:, RHS:].reshape(x.shape)
    pack(own, [r[e] for e in range(x.shape[0])])
    blocks[...] = r[...].astype(BF16)


def finish_kernel(left, right, high, low, x, earlier, first_r, first_x, new_x, r, repeats):
    mix, found = mixing(left, right)
    found = found + earlier[:1, :1]
    repeats[0] = jnp.where(found[0, 0] == 0, 0, CYCLES)
    step, last = combined(mix, high, low, x.shape)
    trusted = (found == 0).reshape(1, 1, 1)
    new_x[...] = jnp.where(trusted, x[...] + step, first_x[...]).reshape(new_x.shape)
    r[...] = jnp.where(trusted, last, first_r[...]).reshape(r.shape)


def single_power_kernel(codes, couple, value, from_chip, from_link, power, ext):
    count = value.shape[0]
    ext[:count] = value[...].astype(BF16)
    unpack(ext, count, from_chip)
    unpack(ext, count + PACK * from_chip.shape[0], from_link)
    ext[ext.shape[0] - 1] = jnp.zeros(ext.shape[1:], BF16)
    for e in range(count):
        power[e] = coupled(codes, e, couple[e], ext)


def single_gram_kernel(*refs):
    fields, gram = refs[:-1], refs[-1]
    fields = [field[...].reshape(-1, RHS) for field in fields]
    columns = [fields[k] - fields[k + 1] for k in range(SSTEP)] + [fields[0]]
    gram[...] = inner_products(*split(jnp.concatenate(columns, axis=1)))


def single_update_kernel(gram, high, low, x, new_x, r):
    first, _ = eliminate(gram)
    size = gram.shape[0]
    eye = (
        lax.broadcasted_iota(jnp.int32, (RHS, RHS), 0) == lax.broadcasted_iota(jnp.int32, (RHS, RHS), 1)
    ).astype(F32)
    res = below(eye, size, 0) - below(first, size, 0) + below(first, size, 1)
    step, r[...] = combined(jnp.concatenate([below(first, size, 0), res], axis=1), high, low, x.shape)
    new_x[...] = x[...] + step


def shards(right_side, first_guess, couple, send_lists, neighbours):
    count = right_side.shape[0]
    slots = send_lists.shape[2]
    devices = lax.axis_size(AXES)
    assert lax.axis_size("sub") == 2 and slots % PACK == 0 and count % PACK == 0
    second = lax.axis_index("sub") == 1

    def shape(dtype, *sizes):
        return jax.ShapeDtypeStruct(sizes, dtype)

    field = shape(F32, count, DOF, RHS)
    blocks_shape = shape(BF16, count, DOF, RHS)
    slot_message = shape(BF16, slots // PACK, DOF, PACK * RHS)
    own_message = shape(BF16, count // PACK, DOF, PACK * RHS)
    message = shape(BF16, (count + slots) // PACK, DOF, PACK * RHS)
    rows_shape = shape(BF16, count, DOF, FACES * DOF)
    row_message = shape(BF16, slots, DOF + META, FACES * DOF)
    half_gram = shape(F32, (POWERS + 2) * RHS // 2, (POWERS + 2) * RHS // 2)
    doubt_shape = shape(F32, 8, LANES)
    table_shape = shape(jnp.int32, count + slots, LANES)

    def call(kernel, outs, specs, name, blocks=0, last=VMEM, scratch=()):
        return pl.pallas_call(
            kernel,
            out_shape=outs,
            in_specs=specs,
            out_specs=[VMEM] * (len(outs) - 1) + [last],
            scratch_shapes=list(scratch) + ([pltpu.VMEM((blocks, DOF, RHS), BF16)] if blocks else []),
            compiler_params=PARAMS,
            name=name,
        )

    nowhere = count + 2 * slots
    own_lists = jnp.where(send_lists[0] < 0, count, send_lists[0]).astype(jnp.int32)
    lists = jnp.where(second, own_lists[::-1], own_lists).reshape(1, 2 * slots)
    swapped = jnp.where(neighbours < count + slots, neighbours + slots, neighbours - slots)
    codes = jnp.where(second | (neighbours < count), neighbours, swapped)
    codes = jnp.where(neighbours < 0, nowhere, codes).astype(jnp.int32)
    codes = jnp.pad(codes, ((0, 0), (0, LANES - FACES)))

    chip_pairs = [(d, d ^ 1) for d in range(devices)]
    link_pairs = [(d, d + 1 if d % 2 else d - 1) for d in range(devices)]
    link_pairs = [(s, t) for s, t in link_pairs if 0 <= t < devices]

    def chip(value):
        return lax.ppermute(value, AXES, chip_pairs)

    def link(value):
        return lax.ppermute(value, AXES, link_pairs)

    def total(left, right):
        value = jnp.where(second, right, left) + chip(jnp.where(second, left, right))
        steps = [1 << k for k in range(1, devices.bit_length() - 1)]
        for first_step, second_step in zip(steps, steps[1:] + steps[:1]):
            pairs = [(d, d ^ (second_step if d % 2 else first_step)) for d in range(devices)]
            value = value + lax.ppermute(value, AXES, pairs)
        other = chip(value)
        return jnp.where(second, other, value), jnp.where(second, value, other)

    start = call(start_kernel, [slot_message] * 2, [VMEM, VMEM], "start", count + 1)
    prepare = call(
        first_kernel,
        [field, rows_shape, slot_message, slot_message],
        [ANY] * 3,
        "prepare",
        scratch=[
            pltpu.VMEM(send_lists.shape, jnp.int32),
            pltpu.VMEM(first_guess.shape, F32),
            pltpu.VMEM((count + 1, DOF, RHS), BF16),
            pltpu.SemaphoreType.DMA((3,)),
        ],
    )
    send_rows = [
        call(functools.partial(rows_kernel, side), [row_message], [VMEM, VMEM, VMEM, ANY], "rows") for side in (0, 1)
    ]
    tables = [call(functools.partial(table_kernel, side), [table_shape], [VMEM] * 3, "table") for side in (0, 1)]
    first = call(
        residual_kernel,
        [field, blocks_shape, own_message, slot_message],
        [VMEM] * 7,
        "first_residual",
        nowhere + 1,
    )
    reach = 2 * (count + slots) + 1
    power = call(power_kernel, [field, blocks_shape, message], [VMEM] * 6, "power", reach)
    early_parts = [
        shape(BF16, count * DOF, 2 * LANES),
        shape(BF16, count * DOF, 2 * LANES),
        shape(F32, 2 * LANES, 2 * LANES),
        shape(F32, 8, RHS),
    ]
    early_gram = call(early_gram_kernel, early_parts, [VMEM] * 5, "early_gram")
    gram = call(gram_kernel, [field, half_gram, half_gram], [VMEM] * 11, "power_and_gram", reach)

    def stacked(fields):
        width = -(-len(fields) * RHS // LANES) * LANES
        parts = [shape(BF16, count * DOF, width)] * 2
        return call(stack_kernel, parts, [VMEM] * len(fields), "stack")(*fields)

    mix_shape = shape(BF16, (POWERS + 2) * RHS, 2 * RHS)
    mix = call(mix_kernel, [mix_shape, mix_shape, slot_message, doubt_shape], [VMEM] * 5, "solve")
    update = call(update_kernel, [field, field, blocks_shape, own_message], [VMEM] * 5, "update")
    flat = shape(F32, *right_side.shape)
    finish = call(finish_kernel, [flat, flat, shape(jnp.int32, 1)], [VMEM] * 8, "solve_finish", last=SMEM)

    b = right_side.reshape(count, DOF, RHS)
    assert CYCLES == 2 * MERGED and POWERS == 6 and PACK * RHS == LANES
    first_x, kept, forward, backward = prepare(
        *(pltpu.with_memory_space_constraint(value, pltpu.HBM) for value in (send_lists, first_guess, couple))
    )
    to_chip = jnp.where(second, backward, forward)
    to_link = jnp.where(second, forward, backward)
    x = first_x
    from_link = link(to_link)
    from_chip = chip(to_chip)
    link_rows = link(send_rows[1](lists, codes, kept, to_link)[0])
    r, blocks, own, to_chip = first(lists, codes, kept, from_chip, from_link, b, x)
    chip_rows = chip(send_rows[0](lists, codes, kept, own)[0])
    (link_table,) = tables[1](lists, codes, link_rows)
    (chip_table,) = tables[0](lists, codes, chip_rows)
    for group in range(CYCLES // MERGED):
        mine = jnp.concatenate([own, chip(to_chip)], axis=0)
        fields = [r]
        for k in range(POWERS - 1):
            if k % 2 == 0:
                value, blocks, mine = power(link_table, kept, link_rows, blocks, mine, link(mine))
            else:
                value, blocks, mine = power(chip_table, kept, chip_rows, blocks, mine, chip(mine))
            fields.append(value)
            if k == 3:
                early = early_gram(*fields)
        value, left, right = gram(chip_table, kept, blocks, mine, chip(mine), *fields[4:], *early)
        fields.append(value)
        sums = total(left, right)
        if group == 0:
            first_r = r
        if group + 1 < CYCLES // MERGED:
            parts = stacked(fields)
            mix_high, mix_low, to_chip, doubt = mix(lists, *sums, *parts)
            x, r, blocks, own = update(mix_high, mix_low, *parts, x)
        else:
            x, r, repeats = finish(*sums, *stacked(fields), x, doubt, first_r, first_x)

    single_power = call(single_power_kernel, [field], [VMEM] * 5, "single_power", nowhere + 1)
    single_gram = call(single_gram_kernel, [shape(F32, LANES, LANES)], [VMEM] * (SSTEP + 1), "single_gram")
    single_update = call(single_update_kernel, [field, field], [VMEM] * 4, "single_update")

    def slots_of(value):
        to_chip, to_link = start(lists, value)
        return chip(to_chip), link(to_link)

    def one_cycle(_, state):
        x, r = (value.reshape(count, DOF, RHS) for value in state)
        fields = [r]
        for _ in range(SSTEP):
            fields += single_power(codes, couple, fields[-1], *slots_of(fields[-1]))
        (value,) = single_gram(*fields)
        step = 1
        while step < devices:
            value = value + lax.ppermute(value, AXES, [(d, d ^ step) for d in range(devices)])
            step *= 2
        x, r = single_update(value, *stacked(fields), x)
        return x.reshape(right_side.shape), r.reshape(right_side.shape)

    return lax.fori_loop(0, repeats[0], one_cycle, (x, r))


def solution(mesh):
    rows = ("grp", "leaf", "sub")
    placed = (P(rows, None), P(rows, None), P(rows, None, None), P(rows, None, None), P(rows, None))
    return jax.shard_map(
        shards,
        mesh=mesh,
        in_specs=placed,
        out_specs=(P(rows, None), P(rows, None)),
        check_vma=False,
    )
```

```python
import functools

import jax
import jax.numpy as jnp
from jax import lax
from jax.experimental import pallas as pl
from jax.experimental.pallas import tpu as pltpu
from jax.sharding import PartitionSpec as P

DOF = 64
FACES = 6
RHS = 32
SSTEP = 3
CYCLES = 4
MERGED = 2
POWERS = SSTEP * MERGED
GROWTH = 8.0
PACK = 4
TRUST_PIVOT = 1e3
TRUST_RESIDUAL = 5e4
TRUST_ROUNDING = 64.0
META = 16
LANES = 128
AXES = ("leaf", "sub")
F32 = jnp.float32
BF16 = jnp.bfloat16

VMEM = pl.BlockSpec(memory_space=pltpu.VMEM)
SMEM = pl.BlockSpec(memory_space=pltpu.SMEM)
ANY = pl.BlockSpec(memory_space=pl.ANY)
PARAMS = pltpu.CompilerParams(vmem_limit_bytes=16 * 1024 * 1024)


def pack(message, blocks):
    for g in range(len(blocks) // PACK):
        message[g] = jnp.concatenate(blocks[PACK * g : PACK * g + PACK], axis=1).astype(BF16)


def unpack(ext, start, message):
    for g in range(message.shape[0]):
        row = message[g]
        for j in range(PACK):
            ext[start + PACK * g + j] = row[:, RHS * j : RHS * j + RHS]


def coupled(table, e, rows, ext):
    gathered = jnp.concatenate([ext[table[e, f]] for f in range(FACES)], axis=0)
    return jnp.dot(rows, gathered, preferred_element_type=F32)


def split(value):
    high = value.astype(BF16)
    return high, (value - high.astype(F32)).astype(BF16)


def listed(lists, side, ext):
    slots = lists.shape[1] // 2
    return [ext[lists[0, side * slots + s]].astype(F32) for s in range(slots)]


def first_kernel(send_lists, guess, couple, x, kept, forward, backward, lists, flat, ext, sems):
    copies = [
        pltpu.make_async_copy(source, target, sems.at[k])
        for k, (source, target) in enumerate(((send_lists, lists), (guess, flat), (couple, kept)))
    ]
    for copy in copies:
        copy.start()
    count = x.shape[0]
    ext[count] = jnp.zeros(ext.shape[1:], BF16)
    copies[1].wait()
    x[...] = flat[...].reshape(x.shape)
    ext[:count] = x[...].astype(BF16)
    copies[0].wait()
    for side, message in ((0, forward), (1, backward)):
        places = [lists[0, side, s] for s in range(lists.shape[2])]
        pack(message, [ext[jnp.where(place < 0, count, place)].astype(F32) for place in places])
    copies[2].wait()


def start_kernel(lists, x, to_chip, to_link, ext):
    count = x.shape[0]
    ext[:count] = x[...].astype(BF16)
    ext[count] = jnp.zeros(ext.shape[1:], BF16)
    pack(to_chip, listed(lists, 0, ext))
    pack(to_link, listed(lists, 1, ext))


def rows_kernel(side, lists, codes, couple, after, message):
    count, slots = couple.shape[0], message.shape[0]
    lanes = lax.broadcasted_iota(jnp.int32, (1, LANES), 1)
    for s in range(slots):
        place = lists[0, side * slots + s]
        e = jnp.minimum(place, count - 1)
        message[s, :DOF] = couple[e]
        meta = jnp.where(place < count, codes[pl.ds(e, 1), :], count + 2 * slots)
        meta = jnp.where(lanes == FACES, place, meta).astype(F32)
        message[s, DOF:] = jnp.zeros((META, couple.shape[2]), BF16)
        message[s, DOF:, :LANES] = jnp.broadcast_to(meta, (META, LANES)).astype(BF16)


def table_kernel(side, lists, codes, rows, table):
    count, slots = codes.shape[0], rows.shape[0]
    reach = count + slots
    chip_base, link_base, empty = count, count + slots, 2 * reach
    known_base, far_base = (chip_base, link_base) if side else (link_base, chip_base)
    meta = [rows[s, DOF:, :LANES].astype(F32)[:1].astype(jnp.int32) for s in range(slots)]
    far = [value[:, FACES : FACES + 1] for value in meta]
    near = [lists[:, side * slots + s : side * slots + s + 1] for s in range(slots)]

    def place(at, own, known, listed_at, listed_own):
        found = jnp.where((at >= known_base) & (at < known_base + slots), at - known_base + known, empty)
        for s in range(slots):
            target = jnp.where(listed_at[s] < count, listed_at[s] + listed_own, empty)
            found = jnp.where(at == far_base + s, target, found)
        return jnp.where(at < count, at + own, found)

    table[:count] = place(codes[...], 0, count, far, reach)
    for s in range(slots):
        table[count + s : count + s + 1] = place(meta[s], reach, reach + count, near, 0)


def residual_kernel(lists, positions, couple, from_chip, from_link, b, x, r, blocks, own, to_chip, ext):
    count = x.shape[0]
    ext[:count] = x[...].astype(BF16)
    unpack(ext, count, from_chip)
    unpack(ext, count + PACK * from_chip.shape[0], from_link)
    ext[ext.shape[0] - 1] = jnp.zeros(ext.shape[1:], BF16)
    for e in range(count):
        r[e] = b[e] - x[e] + coupled(positions, e, couple[e], ext)
    pack(own, [r[e] for e in range(count)])
    blocks[...] = r[...].astype(BF16)
    ext[:count] = blocks[...]
    ext[count] = jnp.zeros(ext.shape[1:], BF16)
    pack(to_chip, listed(lists, 0, ext))


def extend(ext, blocks, mine, theirs):
    count = blocks.shape[0]
    ext[:count] = blocks[...]
    unpack(ext, count, mine.at[count // PACK :])
    unpack(ext, PACK * mine.shape[0], theirs)
    ext[ext.shape[0] - 1] = jnp.zeros(ext.shape[1:], BF16)


def power_kernel(table, couple, extra, blocks, mine, theirs, power, new_blocks, message, ext):
    count, slots = couple.shape[0], extra.shape[0]
    extend(ext, blocks, mine, theirs)
    values = []
    for e in range(count + slots):
        rows = couple[e] if e < count else extra[e - count, :DOF]
        values.append(coupled(table, e, rows, ext) * (1.0 / GROWTH))
        if e < count:
            power[e] = values[e]
            new_blocks[e] = values[e].astype(BF16)
    pack(message, values)


def inner_products(high, low):
    width = high.shape[1]
    sums = by_rows(high, jnp.concatenate([high, low], axis=1))
    cross = sums[:, width:]
    return sums[:, :width] + cross + cross.T


def squared_norms(fields):
    rows = [jnp.sum(field * field, axis=0, keepdims=True) for field in fields]
    return jnp.concatenate(rows + [jnp.zeros((8 - len(rows), RHS), F32)], axis=0)


def early_gram_kernel(*refs):
    fields, (high, low, gram, norms) = refs[:5], refs[5:]
    fields = [field[...].reshape(-1, RHS) for field in fields]
    columns = [fields[k] - GROWTH * fields[k + 1] for k in range(4)] + [fields[0]]
    stacked = jnp.concatenate(columns + [jnp.zeros((columns[0].shape[0], 3 * RHS), F32)], axis=1)
    high[...], low[...] = split(stacked)
    gram[...] = inner_products(high[...], low[...])
    norms[...] = squared_norms(fields)


def by_rows(a, b):
    return lax.dot_general(a, b, (((0,), (0,)), ((), ())), preferred_element_type=F32)


def gram_kernel(table, couple, blocks, mine, theirs, b4, b5, high, low, early, norms, last, left, right, ext):
    count = couple.shape[0]
    rows = count * DOF
    extend(ext, blocks, mine, theirs)
    for e in range(count):
        last[e] = coupled(table, e, couple[e], ext) * (1.0 / GROWTH)
    b4, b5, b6 = (field[...].reshape(rows, RHS) for field in (b4, b5, last))
    late_high, late_low = split(jnp.concatenate([b4 - GROWTH * b5, b5 - GROWTH * b6], axis=1))
    both = jnp.concatenate([late_high, late_low], axis=1)
    width = late_high.shape[1]
    cross = by_rows(both, high[...])
    cross = cross[:width] + cross[width:] + by_rows(late_high, low[...])
    own = by_rows(both, both)
    own = own[:width, :width] + own[:width, width:] + own[width:, :width]
    half = left.shape[0]
    with_r = cross[:, half : half + RHS]
    r_r = early[half : half + RHS, half : half + RHS]
    corner = jnp.concatenate(
        [jnp.concatenate([own, with_r], axis=1), jnp.concatenate([with_r.T, r_r], axis=1)], axis=0
    )
    corner = jnp.concatenate([corner, jnp.zeros((half - RHS, RHS), F32)], axis=1)
    below_diagonal = jnp.concatenate([jnp.zeros((RHS, half), F32), corner], axis=0)
    left[...] = jnp.where(block_of(half, 0) > block_of(half, 1), below_diagonal, early[:half, :half])
    right[...] = jnp.concatenate(
        [cross[:, :half].T, early[:half, half : half + RHS], jnp.zeros((half, RHS), F32)], axis=1
    )
    right[:8, half - RHS :] = jnp.concatenate([norms[:5], squared_norms([b5, b6])[:3]], axis=0)


def block_of(size, dimension):
    return lax.broadcasted_iota(jnp.int32, (size, size), dimension) // RHS


def unpack_gram(left, right):
    half = left.shape[0]
    low_left, right = left[...], right[...]
    row, column = block_of(half, 0), block_of(half, 1)
    norms = jnp.concatenate([right[j : j + 1, half - RHS :] for j in range(POWERS + 2)], axis=1)
    right = jnp.where(column < 3, right, 0.0)
    first = jnp.where(row <= column, low_left, low_left.T)
    moved = jnp.concatenate([low_left[RHS:], jnp.zeros((RHS, half), F32)], axis=0)
    last = jnp.where(row >= column, moved, moved.T)
    last = jnp.where((row < 3) & (column < 3), last, 0.0)
    gram = jnp.concatenate(
        [jnp.concatenate([first, right], axis=1), jnp.concatenate([right.T, last], axis=1)], axis=0
    )
    return gram, norms


def eliminate(gram):
    count = SSTEP * RHS // 8
    groups = [gram[8 * g : 8 * g + 8, :] for g in range(count)]
    shape = groups[0].shape
    row_ids = lax.broadcasted_iota(jnp.int32, shape, 0)
    lane_ids = lax.broadcasted_iota(jnp.int32, (1, shape[1]), 1)
    pivots = jnp.zeros((1, shape[1]), F32)
    for home in range(count):
        columns = [
            [jnp.broadcast_to(group[:, 8 * home + m : 8 * home + m + 1], shape) for m in range(8)]
            for group in groups
        ]
        own = list(columns[home])
        panel = groups[home]
        for m in range(8):
            pivot = own[m][m : m + 1, :]
            pivots = jnp.where(lane_ids == 8 * home + m, pivot, pivots)
            inverse = 1.0 / pivot
            scaled = panel[m : m + 1, :] * inverse
            panel = jnp.where(row_ids == m, scaled, panel - own[m] * scaled)
            for k in range(m + 1, 8):
                scaled = own[k][m : m + 1, :] * inverse
                own[k] = jnp.where(row_ids == m, scaled, own[k] - own[m] * scaled)
        for g in range(count):
            if g == home:
                groups[g] = panel
                continue
            terms = [columns[g][m] * panel[m : m + 1, :] for m in range(8)]
            while len(terms) > 1:
                terms = [x + y for x, y in zip(terms[::2], terms[1::2])]
            groups[g] = groups[g] - terms[0]
    return jnp.concatenate(groups, axis=0)[:, SSTEP * RHS :], pivots


def exact(a, b, contract=(1, 0)):
    return lax.dot_general(
        a,
        b,
        (((contract[0],), (contract[1],)), ((), ())),
        precision=lax.Precision.HIGHEST,
        preferred_element_type=F32,
    )


def below(value, size, blocks):
    parts = [jnp.zeros((RHS * blocks, value.shape[1]), F32)] if blocks else []
    rest = size - RHS * blocks - value.shape[0]
    parts.append(value)
    if rest:
        parts.append(jnp.zeros((rest, value.shape[1]), F32))
    return jnp.concatenate(parts, axis=0)


def weighted(weights, rows):
    return jnp.dot(weights.astype(BF16), rows.astype(BF16), preferred_element_type=F32)


def mixing(left, right):
    gram, norms = unpack_gram(left, right)
    size = gram.shape[0]
    right = RHS * POWERS
    square = SSTEP * RHS
    eye = (
        lax.broadcasted_iota(jnp.int32, (RHS, RHS), 0) == lax.broadcasted_iota(jnp.int32, (RHS, RHS), 1)
    ).astype(F32)

    first, _ = eliminate(jnp.concatenate([gram[:square, :square], gram[:square, right : right + RHS]], axis=1))
    first_left = GROWTH * below(first, square + RHS, 1) - below(first, square + RHS, 0) + below(eye, square + RHS, 0)
    moved = jnp.concatenate([below(first_left, size, k) for k in range(SSTEP)], axis=1)
    images = jnp.concatenate([moved, below(eye, size, POWERS) - below(first, size, 0)], axis=1)
    projected = exact(images, exact(gram, images), (0, 0))
    second, pivots = eliminate(projected)
    change = exact(moved, second)
    sol = below(first, size, 0) + change
    res = below(first_left, size, 0) - change + GROWTH * below(change[: size - RHS], size, 1)
    half = size // 2
    is_diagonal = lax.broadcasted_iota(jnp.int32, (half, half), 0) == lax.broadcasted_iota(jnp.int32, (half, half), 1)
    diagonal = jnp.concatenate(
        [
            jnp.sum(jnp.where(is_diagonal, block, 0.0), axis=0, keepdims=True)
            for block in (gram[:half, :half], gram[half:, half:])
        ],
        axis=1,
    )
    reach = weighted(jnp.sqrt(diagonal), jnp.abs(images))
    reach = reach * reach
    corner = jnp.where(eye > 0, projected[square:, square:], 0.0)
    left_over = jnp.sum(corner, axis=0, keepdims=True) - jnp.sum(
        projected[:square, square:] * second, axis=0, keepdims=True
    )
    power = (lax.broadcasted_iota(jnp.int32, (1, size), 1) // RHS).astype(F32)
    rounding = weighted(norms * power, res * res)
    doubts = [
        jnp.where(reach[:, :square] <= TRUST_PIVOT * pivots[:, :square], 0.0, 1.0),
        jnp.where(reach[:, square:] <= TRUST_RESIDUAL * left_over, 0.0, 1.0),
        jnp.where(jnp.sum(rounding, axis=1, keepdims=True) <= TRUST_ROUNDING * jnp.sum(left_over, axis=1, keepdims=True), 0.0, 1.0),
    ]
    doubt = sum(jnp.sum(value, axis=1, keepdims=True) for value in doubts)
    return jnp.concatenate([sol, res], axis=1), doubt


def stack_kernel(*refs):
    fields, (high, low) = refs[:-2], refs[-2:]
    rows = fields[0].shape[0] * DOF
    columns = [field[...].reshape(rows, RHS) for field in fields]
    rest = high.shape[1] - RHS * len(fields)
    if rest:
        columns.append(jnp.zeros((rows, rest), F32))
    high[...], low[...] = split(jnp.concatenate(columns, axis=1))


def times(mix_high, mix_low, high, low):
    width = mix_high.shape[1]
    out = jnp.dot(high, jnp.concatenate([mix_high, mix_low], axis=1), preferred_element_type=F32)
    return out[:, :width] + out[:, width:] + jnp.dot(low, mix_high, preferred_element_type=F32)


def combined(mix, high, low, shape):
    out = times(*split(mix), high[...], low[...])
    return out[:, :RHS].reshape(shape), out[:, RHS:].reshape(shape)


def mix_kernel(lists, left, right, high, low, mix_high, mix_low, to_chip, doubt):
    mix, found = mixing(left, right)
    doubt[...] = jnp.broadcast_to(found, doubt.shape)
    mix_high[...], mix_low[...] = split(mix)
    count, slots = high.shape[0] // DOF, lists.shape[1] // 2
    places = [lists[0, s] for s in range(slots)]
    starts = [pl.multiple_of(jnp.minimum(place, count - 1) * DOF, DOF) for place in places]
    rows = [jnp.concatenate([part[pl.ds(start, DOF), :] for start in starts], axis=0) for part in (high, low)]
    out = times(mix_high[...], mix_low[...], *rows)[:, RHS:]
    blocks = [out[DOF * s : DOF * s + DOF] for s in range(slots)]
    pack(to_chip, [jnp.where(place < count, block, 0.0) for place, block in zip(places, blocks)])


def update_kernel(mix_high, mix_low, high, low, x, new_x, r, blocks, own):
    out = times(mix_high[...], mix_low[...], high[...], low[...])
    new_x[...] = x[...] + out[:, :RHS].reshape(x.shape)
    r[...] = out[:, RHS:].reshape(x.shape)
    pack(own, [r[e] for e in range(x.shape[0])])
    blocks[...] = r[...].astype(BF16)


def finish_kernel(left, right, high, low, x, earlier, first_r, first_x, new_x, r, repeats):
    mix, found = mixing(left, right)
    found = found + earlier[:1, :1]
    repeats[0] = jnp.where(found[0, 0] == 0, 0, CYCLES)
    step, last = combined(mix, high, low, x.shape)
    trusted = (found == 0).reshape(1, 1, 1)
    new_x[...] = jnp.where(trusted, x[...] + step, first_x[...]).reshape(new_x.shape)
    r[...] = jnp.where(trusted, last, first_r[...]).reshape(r.shape)


def single_power_kernel(codes, couple, value, from_chip, from_link, power, ext):
    count = value.shape[0]
    ext[:count] = value[...].astype(BF16)
    unpack(ext, count, from_chip)
    unpack(ext, count + PACK * from_chip.shape[0], from_link)
    ext[ext.shape[0] - 1] = jnp.zeros(ext.shape[1:], BF16)
    for e in range(count):
        power[e] = coupled(codes, e, couple[e], ext)


def single_gram_kernel(*refs):
    fields, gram = refs[:-1], refs[-1]
    fields = [field[...].reshape(-1, RHS) for field in fields]
    columns = [fields[k] - fields[k + 1] for k in range(SSTEP)] + [fields[0]]
    gram[...] = inner_products(*split(jnp.concatenate(columns, axis=1)))


def single_update_kernel(gram, high, low, x, new_x, r):
    first, _ = eliminate(gram)
    size = gram.shape[0]
    eye = (
        lax.broadcasted_iota(jnp.int32, (RHS, RHS), 0) == lax.broadcasted_iota(jnp.int32, (RHS, RHS), 1)
    ).astype(F32)
    res = below(eye, size, 0) - below(first, size, 0) + below(first, size, 1)
    step, r[...] = combined(jnp.concatenate([below(first, size, 0), res], axis=1), high, low, x.shape)
    new_x[...] = x[...] + step


def shards(right_side, first_guess, couple, send_lists, neighbours):
    count = right_side.shape[0]
    slots = send_lists.shape[2]
    devices = lax.axis_size(AXES)
    assert lax.axis_size("sub") == 2 and slots % PACK == 0 and count % PACK == 0
    second = lax.axis_index("sub") == 1

    def shape(dtype, *sizes):
        return jax.ShapeDtypeStruct(sizes, dtype)

    field = shape(F32, count, DOF, RHS)
    blocks_shape = shape(BF16, count, DOF, RHS)
    slot_message = shape(BF16, slots // PACK, DOF, PACK * RHS)
    own_message = shape(BF16, count // PACK, DOF, PACK * RHS)
    message = shape(BF16, (count + slots) // PACK, DOF, PACK * RHS)
    rows_shape = shape(BF16, count, DOF, FACES * DOF)
    row_message = shape(BF16, slots, DOF + META, FACES * DOF)
    half_gram = shape(F32, (POWERS + 2) * RHS // 2, (POWERS + 2) * RHS // 2)
    doubt_shape = shape(F32, 8, LANES)
    table_shape = shape(jnp.int32, count + slots, LANES)

    def call(kernel, outs, specs, name, blocks=0, last=VMEM, scratch=()):
        return pl.pallas_call(
            kernel,
            out_shape=outs,
            in_specs=specs,
            out_specs=[VMEM] * (len(outs) - 1) + [last],
            scratch_shapes=list(scratch) + ([pltpu.VMEM((blocks, DOF, RHS), BF16)] if blocks else []),
            compiler_params=PARAMS,
            name=name,
        )

    nowhere = count + 2 * slots
    own_lists = jnp.where(send_lists[0] < 0, count, send_lists[0]).astype(jnp.int32)
    lists = jnp.where(second, own_lists[::-1], own_lists).reshape(1, 2 * slots)
    swapped = jnp.where(neighbours < count + slots, neighbours + slots, neighbours - slots)
    codes = jnp.where(second | (neighbours < count), neighbours, swapped)
    codes = jnp.where(neighbours < 0, nowhere, codes).astype(jnp.int32)
    codes = jnp.pad(codes, ((0, 0), (0, LANES - FACES)))

    chip_pairs = [(d, d ^ 1) for d in range(devices)]
    link_pairs = [(d, d + 1 if d % 2 else d - 1) for d in range(devices)]
    link_pairs = [(s, t) for s, t in link_pairs if 0 <= t < devices]

    def chip(value):
        return lax.ppermute(value, AXES, chip_pairs)

    def link(value):
        return lax.ppermute(value, AXES, link_pairs)

    def total(left, right):
        value = jnp.where(second, right, left) + chip(jnp.where(second, left, right))
        steps = [1 << k for k in range(1, devices.bit_length() - 1)]
        for first_step, second_step in zip(steps, steps[1:] + steps[:1]):
            pairs = [(d, d ^ (second_step if d % 2 else first_step)) for d in range(devices)]
            value = value + lax.ppermute(value, AXES, pairs)
        other = chip(value)
        return jnp.where(second, other, value), jnp.where(second, value, other)

    start = call(start_kernel, [slot_message] * 2, [VMEM, VMEM], "start", count + 1)
    prepare = call(
        first_kernel,
        [field, rows_shape, slot_message, slot_message],
        [ANY] * 3,
        "prepare",
        scratch=[
            pltpu.VMEM(send_lists.shape, jnp.int32),
            pltpu.VMEM(first_guess.shape, F32),
            pltpu.VMEM((count + 1, DOF, RHS), BF16),
            pltpu.SemaphoreType.DMA((3,)),
        ],
    )
    send_rows = [
        call(functools.partial(rows_kernel, side), [row_message], [VMEM, VMEM, VMEM, ANY], "rows") for side in (0, 1)
    ]
    tables = [call(functools.partial(table_kernel, side), [table_shape], [VMEM] * 3, "table") for side in (0, 1)]
    first = call(
        residual_kernel,
        [field, blocks_shape, own_message, slot_message],
        [VMEM] * 7,
        "first_residual",
        nowhere + 1,
    )
    reach = 2 * (count + slots) + 1
    power = call(power_kernel, [field, blocks_shape, message], [VMEM] * 6, "power", reach)
    early_parts = [
        shape(BF16, count * DOF, 2 * LANES),
        shape(BF16, count * DOF, 2 * LANES),
        shape(F32, 2 * LANES, 2 * LANES),
        shape(F32, 8, RHS),
    ]
    early_gram = call(early_gram_kernel, early_parts, [VMEM] * 5, "early_gram")
    gram = call(gram_kernel, [field, half_gram, half_gram], [VMEM] * 11, "power_and_gram", reach)

    def stacked(fields):
        width = -(-len(fields) * RHS // LANES) * LANES
        parts = [shape(BF16, count * DOF, width)] * 2
        return call(stack_kernel, parts, [VMEM] * len(fields), "stack")(*fields)

    mix_shape = shape(BF16, (POWERS + 2) * RHS, 2 * RHS)
    mix = call(mix_kernel, [mix_shape, mix_shape, slot_message, doubt_shape], [VMEM] * 5, "solve")
    update = call(update_kernel, [field, field, blocks_shape, own_message], [VMEM] * 5, "update")
    flat = shape(F32, *right_side.shape)
    finish = call(finish_kernel, [flat, flat, shape(jnp.int32, 1)], [VMEM] * 8, "solve_finish", last=SMEM)

    b = right_side.reshape(count, DOF, RHS)
    assert CYCLES == 2 * MERGED and POWERS == 6 and PACK * RHS == LANES
    first_x, kept, forward, backward = prepare(
        *(pltpu.with_memory_space_constraint(value, pltpu.HBM) for value in (send_lists, first_guess, couple))
    )
    to_chip = jnp.where(second, backward, forward)
    to_link = jnp.where(second, forward, backward)
    x = first_x
    from_link = link(to_link)
    from_chip = chip(to_chip)
    link_rows = link(send_rows[1](lists, codes, kept, to_link)[0])
    r, blocks, own, to_chip = first(lists, codes, kept, from_chip, from_link, b, x)
    chip_rows = chip(send_rows[0](lists, codes, kept, own)[0])
    (link_table,) = tables[1](lists, codes, link_rows)
    (chip_table,) = tables[0](lists, codes, chip_rows)
    for group in range(CYCLES // MERGED):
        mine = jnp.concatenate([own, chip(to_chip)], axis=0)
        fields = [r]
        for k in range(POWERS - 1):
            if k % 2 == 0:
                value, blocks, mine = power(link_table, kept, link_rows, blocks, mine, link(mine))
            else:
                value, blocks, mine = power(chip_table, kept, chip_rows, blocks, mine, chip(mine))
            fields.append(value)
            if k == 3:
                early = early_gram(*fields)
        value, left, right = gram(chip_table, kept, blocks, mine, chip(mine), *fields[4:], *early)
        fields.append(value)
        sums = total(left, right)
        if group == 0:
            first_r = r
        if group + 1 < CYCLES // MERGED:
            parts = stacked(fields)
            mix_high, mix_low, to_chip, doubt = mix(lists, *sums, *parts)
            x, r, blocks, own = update(mix_high, mix_low, *parts, x)
        else:
            x, r, repeats = finish(*sums, *stacked(fields), x, doubt, first_r, first_x)

    single_power = call(single_power_kernel, [field], [VMEM] * 5, "single_power", nowhere + 1)
    single_gram = call(single_gram_kernel, [shape(F32, LANES, LANES)], [VMEM] * (SSTEP + 1), "single_gram")
    single_update = call(single_update_kernel, [field, field], [VMEM] * 4, "single_update")

    def slots_of(value):
        to_chip, to_link = start(lists, value)
        return chip(to_chip), link(to_link)

    def one_cycle(_, state):
        x, r = (value.reshape(count, DOF, RHS) for value in state)
        fields = [r]
        for _ in range(SSTEP):
            fields += single_power(codes, couple, fields[-1], *slots_of(fields[-1]))
        (value,) = single_gram(*fields)
        step = 1
        while step < devices:
            value = value + lax.ppermute(value, AXES, [(d, d ^ step) for d in range(devices)])
            step *= 2
        x, r = single_update(value, *stacked(fields), x)
        return x.reshape(right_side.shape), r.reshape(right_side.shape)

    return lax.fori_loop(0, repeats[0], one_cycle, (x, r))


def solution(mesh):
    rows = ("grp", "leaf", "sub")
    placed = (P(rows, None), P(rows, None), P(rows, None, None), P(rows, None, None), P(rows, None))
    return jax.shard_map(
        shards,
        mesh=mesh,
        in_specs=placed,
        out_specs=(P(rows, None), P(rows, None)),
        check_vma=False,
    )
```
